256 devices in a mesh: dom: 64 (over x_lo, y, z), grp: 4 (over x_hi, core).
Axes of the slice: x: 4 (x_hi: 2, x_lo: 2; x = x_hi * 2 + x_lo), y: 4, z: 8, core: 2. Of those that a mesh axis runs over, the one named last changes fastest.
Arguments:
- particles: bfloat16 [114688, 4096], P(('dom', 'grp')), may hold values from -40 to 40
- rot_center: int32 [114688], P(('dom', 'grp')), may hold values from 0 to 29
- shifts: int32 [2, 114688], P(None, ('dom', 'grp')), may hold values from -3 to 3
- references: bfloat16 [32, 30, 4096], P('grp'), may hold values from -3 to 3
- class_prior: float32 [32], replicated, may hold values from 0.0001 to 1
- sigma2: float32 [2048], replicated, may hold values from 10 to 40
Outputs:
- class_means: float32 [32, 122880], P('grp', 'dom')
The draws below stay inside these ranges and needn't reach their ends.
All inputs are finite; a program needn't handle non-finite values.
Results may differ from the reference program's by a relative error of at most 0.0023.
Values may be sent and summed in bfloat16 or wider, within the bound.
No kernel may reach another device: no remote copies, remote signals or barrier semaphores. Data moves between devices by JAX's collectives and lax.ppermute only.
A program may use at most 128 MiB of HBM per device.

```python
import math
import jax
import jax.numpy as jnp
from jax import lax

PART_DEV = 448
CLASSES = 32
ROTS = 30
HALFWIN = 6
BOX = 128
KXW = 32
KYW = 64
F = 2048
PARTICLES = 114688
N_DOM = 64
N_GRP = 4


def common_draw(key):
    offsets = jax.random.randint(jax.random.fold_in(key, 101), (2, PARTICLES), -3, 4).astype(jnp.int32)
    return offsets


def draw_shifts(key, part):
    offsets = common_draw(key)
    return offsets


def draw_particles(key, part):
    key = jax.random.fold_in(key, 1)
    values = 4.5 * jax.random.normal(key, (PARTICLES, 2 * F), jnp.float32)
    return jnp.clip(values, -40.0, 40.0).astype(jnp.bfloat16)


def draw_references(key, part):
    key = jax.random.fold_in(key, 2)
    spread = 0.05 * jnp.sqrt(2048.0 / F)
    values = spread * jax.random.normal(key, (CLASSES, ROTS, 2 * F), jnp.float32)
    return jnp.clip(values, -3.0, 3.0).astype(jnp.bfloat16)


def plant(result, key, smallest, largest):
    dims = result.shape
    spot = [jax.random.randint(jax.random.fold_in(key, axis), (), 0, dims[axis]) for axis in range(len(dims))]
    result = result.at[tuple(spot)].set(smallest)
    longest = dims.index(max(dims))
    spot[longest] = (spot[longest] + 1) % dims[longest]
    return result.at[tuple(spot)].set(largest)


def setup_inputs(seed: int = 0) -> dict:
    streams_of = jax.random.split(jax.random.key(seed), 7)
    return {
        "particles": draw_particles(jax.random.fold_in(streams_of[6], 71), 0),
        "rot_center": plant(jax.random.randint(streams_of[1], (PARTICLES,), 0, ROTS), jax.random.fold_in(streams_of[1], 1), 0, ROTS - 1).astype(jnp.int32),
        "shifts": draw_shifts(jax.random.fold_in(streams_of[6], 71), 0),
        "references": draw_references(jax.random.fold_in(streams_of[6], 71), 0),
        "class_prior": jnp.clip(jnp.exp(jax.random.uniform(streams_of[4], (CLASSES,), jnp.float32, math.log(0.0001), math.log(1.0))), 0.0001, 1.0),
        "sigma2": jnp.clip(jnp.exp(jax.random.uniform(streams_of[5], (F,), jnp.float32, math.log(10.0), math.log(40.0))), 10.0, 40.0),
    }


TWO_PI = 6.283185307179586
REG_WEIGHT = 0.05


def phases(shifts, coeffs):
    indices = jnp.arange(coeffs, dtype=jnp.int32)
    wave_y = (indices // KXW - KYW // 2).astype(jnp.float32)
    wave_x = (indices % KXW).astype(jnp.float32)
    shift_x = shifts[0].astype(jnp.float32)
    shift_y = shifts[1].astype(jnp.float32)
    return (TWO_PI / BOX) * (shift_x[:, None] * wave_x[None, :] + shift_y[:, None] * wave_y[None, :])


def shift_particles(particles, shifts):
    coeffs = particles.shape[1] // 2
    angle_table = phases(shifts, coeffs)
    cosine = jnp.cos(angle_table)
    sinus = jnp.sin(angle_table)
    real_part = particles[:, :coeffs].astype(jnp.float32)
    imag_part = particles[:, coeffs:].astype(jnp.float32)
    moved = jnp.concatenate([real_part * cosine + imag_part * sinus, imag_part * cosine - real_part * sinus], axis=1)
    return moved.astype(jnp.bfloat16)


def block_scores(weighted, refs_block, inverse):
    flat_refs = refs_block.reshape(-1, refs_block.shape[-1])
    correlation = lax.dot_general(weighted, flat_refs, (((1,), (1,)), ((), ())), preferred_element_type=jnp.float32)
    widened = flat_refs.astype(jnp.float32)
    energy = jnp.sum(widened * widened * inverse[None, :], axis=1)
    return correlation - 0.5 * energy[None, :]


def posterior_of(fitted, rot_center, class_prior, rotations):
    columns = jnp.arange(fitted.shape[1], dtype=jnp.int32)
    rotation_of = columns % rotations
    log_prior = jnp.repeat(jnp.log(class_prior), rotations)
    scores = log_prior[None, :] + fitted
    distance = (rotation_of[None, :] - rot_center[:, None]) % rotations
    inside = (distance <= HALFWIN) | (distance >= rotations - HALFWIN)
    masked = jnp.where(inside, scores, -jnp.inf)
    highest = jnp.max(masked, axis=1, keepdims=True)
    raised = jnp.exp(masked - highest)
    return raised / jnp.sum(raised, axis=1, keepdims=True)


def reference(particles, rot_center, shifts, references, class_prior, sigma2):
    noise_power = jnp.concatenate([sigma2, sigma2])
    inverse = 1.0 / noise_power
    blocks = N_DOM * N_GRP
    part_blocks = particles.reshape(blocks, PART_DEV, 2 * F)
    centers = rot_center.reshape(blocks, PART_DEV)
    shift_blocks = jnp.transpose(shifts.reshape(2, blocks, PART_DEV), (1, 0, 2))

    def accumulate(running, inputs):
        class_sums, totals = running
        block, center, offset = inputs
        shifted = shift_particles(block, offset)
        weighted = (shifted.astype(jnp.float32) * inverse[None, :]).astype(jnp.bfloat16)
        fitted = block_scores(weighted, references, inverse)
        weights_f = posterior_of(fitted, center, class_prior, ROTS)
        weights_b = weights_f.astype(jnp.bfloat16)
        class_sums = class_sums + lax.dot_general(weights_b, shifted, (((0,), (0,)), ((), ())), preferred_element_type=jnp.float32)
        totals = totals + jnp.sum(weights_f, axis=0)
        return (class_sums, totals), None

    start_sums = jnp.zeros((CLASSES * ROTS, 2 * F), jnp.float32)
    start_totals = jnp.zeros((CLASSES * ROTS,), jnp.float32)
    (class_sums, totals), _ = lax.scan(accumulate, (start_sums, start_totals), (part_blocks, centers, shift_blocks))
    divisor = totals.reshape(CLASSES, ROTS)[:, :, None] + REG_WEIGHT * noise_power[None, None, :]
    return (class_sums.reshape(CLASSES, ROTS, 2 * F) / divisor).reshape(CLASSES, ROTS * 2 * F)
```

```python
import functools

import jax
import jax.numpy as jnp
from jax import lax
from jax.experimental import pallas as pl
from jax.experimental.pallas import tpu as pltpu
from jax.sharding import Mesh, PartitionSpec as P

HALFWIN = 6
BOX = 128
KXW = 32
KYW = 64
TWO_PI = 6.283185307179586
REG_WEIGHT = 0.05

F = 2048
WIDE = 2 * F
ROTS = 30
ROWS = 32 * 8
NP = 448
NP2 = 2 * NP
LANES = NP2 // 128
DIRECT = 1536
QUART = 640
UNITS = 60
BROWS = UNITS * 8 + 16

BF = jnp.bfloat16
F32 = jnp.float32
MB = 1024 * 1024


def turn_cos_sin(turns):
    quarter = jnp.floor(4.0 * turns + 0.5)
    x = TWO_PI * (turns - 0.25 * quarter)
    q = quarter - 4.0 * jnp.floor(0.25 * quarter)
    x2 = x * x
    s = x * (1.0 + x2 * (-1.0 / 6 + x2 * (1.0 / 120 + x2 * (-1.0 / 5040 + x2 * (1.0 / 362880)))))
    c = 1.0 + x2 * (-0.5 + x2 * (1.0 / 24 + x2 * (-1.0 / 720 + x2 * (1.0 / 40320))))
    odd = (q == 1.0) | (q == 3.0)
    cos = jnp.where(odd, s, c)
    sin = jnp.where(odd, c, s)
    cos = jnp.where((q == 1.0) | (q == 2.0), -cos, cos)
    sin = jnp.where(q >= 2.0, -sin, sin)
    return cos, sin


def shift_kernel(sh_ref, p_ref, o_ref):
    rows = p_ref.shape[0]
    lane = lax.broadcasted_iota(jnp.int32, (rows, 128), 1)
    kx = (lane & (KXW - 1)).astype(F32)
    ky = ((lane >> 5) - KYW // 2).astype(F32)
    sx = sh_ref[:, 0:1]
    sy = sh_ref[:, 1:2]
    c, s = turn_cos_sin((sx * kx + sy * ky) * (1.0 / BOX))
    step = jnp.broadcast_to(sy * (128 // KXW), (rows, 128)) * (1.0 / BOX)
    dc, ds = turn_cos_sin(step)
    for b in range(F // 128):
        re = p_ref[:, b * 128 : (b + 1) * 128].astype(F32)
        im = p_ref[:, F + b * 128 : F + (b + 1) * 128].astype(F32)
        o_ref[:, b * 128 : (b + 1) * 128] = (re * c + im * s).astype(BF)
        o_ref[:, F + b * 128 : F + (b + 1) * 128] = (im * c - re * s).astype(BF)
        c, s = c * dc - s * ds, s * dc + c * ds


def shift_particles(particles, shifts):
    block = 64
    return pl.pallas_call(
        shift_kernel,
        grid=(NP // block,),
        out_shape=jax.ShapeDtypeStruct((NP, WIDE), BF),
        in_specs=[
            pl.BlockSpec((block, 2), lambda i: (i, 0)),
            pl.BlockSpec((block, WIDE), lambda i: (i, 0)),
        ],
        out_specs=pl.BlockSpec((block, WIDE), lambda i: (i, 0)),
        compiler_params=pltpu.CompilerParams(vmem_limit_bytes=16 * MB),
    )(shifts.T.astype(F32), particles)


def correlate(where_ref, own_ref, oth_ref, inv_ref, bias_ref, pieces, w_ref, acc_ref):
    energy = jnp.zeros((ROWS, 128), F32)
    first = True
    for number, (piece, width) in enumerate(pieces):
        total = piece.shape[1]
        for start in range(0, total, width):
            off = pl.multiple_of(where_ref[number] + start, 128)
            cols = pl.ds(off, width)
            inv = inv_ref[:, cols]
            w_ref[0:NP, 0:width] = (own_ref[:, cols].astype(F32) * inv).astype(BF)
            w_ref[NP:NP2, 0:width] = (oth_ref[:, cols].astype(F32) * inv).astype(BF)
            part = lax.dot_general(
                piece[:, start : start + width],
                w_ref[:, 0:width],
                (((1,), (1,)), ((), ())),
                preferred_element_type=F32,
            )
            for j in range(LANES):
                block = part[:, j * 128 : (j + 1) * 128]
                acc_ref[j] = block if first else acc_ref[j] + block
            first = False
            for lanes in range(0, width, 128):
                v = piece[:, start + lanes : start + lanes + 128].astype(F32)
                energy = energy + v * v * inv[:, lanes : lanes + 128]
    bias = bias_ref[...] - 0.5 * jnp.sum(energy, axis=1, keepdims=True)
    for j in range(LANES):
        acc_ref[j] = acc_ref[j] + bias


def own_kernel(where_ref, own_ref, oth_ref, inv_ref, bias_ref, refs_ref, out_ref, w_ref):
    correlate(where_ref, own_ref, oth_ref, inv_ref, bias_ref, [(refs_ref, 512)], w_ref, out_ref)


def inside_window(rotation, rot):
    distance = rotation - rot
    distance = jnp.where(distance < 0, distance + ROTS, distance)
    return (distance <= HALFWIN) | (distance >= ROTS - HALFWIN)


def other_kernel(
    where_ref, own_ref, oth_ref, inv_ref, bias_ref, d_ref, q0, q1, q2, q3, first_ref, rot_ref,
    out_ref, stats_ref, w_ref,
):
    pieces = [(d_ref, 512), (q0, QUART), (q1, QUART), (q2, QUART), (q3, QUART)]
    correlate(where_ref, own_ref, oth_ref, inv_ref, bias_ref, pieces, w_ref, out_ref)
    row = lax.broadcasted_iota(jnp.int32, (8, 128), 0)
    low = jnp.full((8, 128), -jnp.inf, F32)
    for j in range(LANES):
        lanes = slice(j * 128, (j + 1) * 128)
        rot = rot_ref[:, lanes]
        top = low
        for r in range(ROTS):
            rows = pl.ds(r, 8, stride=32)
            best = jnp.maximum(first_ref[j, rows, :], out_ref[j, rows, :])
            top = jnp.maximum(top, jnp.where(inside_window(r, rot), best, low))
        top = jnp.max(top, axis=0, keepdims=True)
        mass = jnp.zeros((8, 128), F32)
        for r in range(ROTS):
            rows = pl.ds(r, 8, stride=32)
            both = jnp.exp(first_ref[j, rows, :] - top) + jnp.exp(out_ref[j, rows, :] - top)
            mass = mass + jnp.where(inside_window(r, rot), both, 0.0)
        mass = jnp.sum(mass, axis=0, keepdims=True)
        stats_ref[:, lanes] = jnp.where(row == 0, top, mass)


def sums_kernel(
    where_ref, first_ref, second_ref, mine_ref, theirs_ref, rot_ref, own_ref, oth_ref,
    a_ref, b_ref, p_ref, x_ref, acc_ref, mass_ref,
):
    x_hi = where_ref[0]
    y = where_ref[1]
    theirs = pltpu.roll(theirs_ref[...], NP, 1)
    top_a, mass_a = mine_ref[0:1, :], mine_ref[1:2, :]
    top_b, mass_b = theirs[0:1, :], theirs[1:2, :]
    top = jnp.maximum(top_a, top_b)
    scale = 1.0 / (mass_a * jnp.exp(top_a - top) + mass_b * jnp.exp(top_b - top))
    mass_ref[...] = jnp.zeros_like(mass_ref)
    for j in range(LANES):
        lanes = slice(j * 128, (j + 1) * 128)
        rot = rot_ref[:, lanes]
        top_j, scale_j = top[:, lanes], scale[:, lanes]
        for r in range(ROTS):
            rows = pl.ds(r, 8, stride=32)
            inside = inside_window(r, rot)
            p = jnp.where(inside, jnp.exp(first_ref[j, rows, :] - top_j) * scale_j, 0.0)
            q = jnp.where(inside, jnp.exp(second_ref[j, rows, :] - top_j) * scale_j, 0.0)
            low = jnp.where(x_hi == 0, p, q)
            high = jnp.where(x_hi == 0, q, p)
            both = jnp.concatenate([low, high], axis=0)
            p_ref[r * 16 : (r + 1) * 16, lanes] = both.astype(BF)
            mass_ref[r * 16 : (r + 1) * 16, :] += both
    lane = lax.broadcasted_iota(jnp.int32, (16, 128), 1)
    totals = jnp.zeros((16, 128), F32)
    for r in range(ROTS):
        row_sum = jnp.sum(mass_ref[r * 16 : (r + 1) * 16, :], axis=1, keepdims=True)
        totals = jnp.where(lane == r, row_sum, totals)
    slots = [((dest - y) & 3) for dest in range(4)]
    coarse = totals.astype(BF)
    fine = (totals - coarse.astype(F32)).astype(BF)
    for kx in range(2):
        extra = jnp.concatenate(
            [coarse[kx * 8 : kx * 8 + 8].astype(F32), fine[kx * 8 : kx * 8 + 8].astype(F32)], axis=0
        ).astype(BF)
        for x_lo in range(2):
            for dest in range(4):
                a_ref[2 * x_lo + kx, slots[dest], UNITS * 8 : BROWS, :] = extra
                b_ref[slots[dest], 2 * x_lo + kx, UNITS * 8 : BROWS, :] = extra
    width = 512
    for cb in range(WIDE // width):
        cols = slice(cb * width, (cb + 1) * width)
        x_ref[0:NP, :] = own_ref[:, cols]
        x_ref[NP:NP2, :] = oth_ref[:, cols]
        acc_ref[...] = jnp.dot(p_ref[...], x_ref[...], preferred_element_type=F32)
        for r in range(ROTS):
            for pair in range(width // 256):
                unit = 32 * r + 4 * cb + 2 * pair
                block = unit // UNITS
                x_lo, dest, z_half = block // 8, (block // 2) % 4, block % 2
                row = (unit % UNITS) * 8
                for kx in range(2):
                    sub = slice(r * 16 + kx * 8, r * 16 + kx * 8 + 8)
                    tile = jnp.concatenate(
                        [
                            acc_ref[sub, pair * 256 : pair * 256 + 128],
                            acc_ref[sub, pair * 256 + 128 : pair * 256 + 256],
                        ],
                        axis=0,
                    ).astype(BF)
                    if z_half == 0:
                        a_ref[2 * x_lo + kx, slots[dest], row : row + 16, :] = tile
                    else:
                        b_ref[slots[dest], 2 * x_lo + kx, row : row + 16, :] = tile


def final_kernel(where_ref, z_ref, sigma_ref, out_ref):
    d = where_ref[0]
    total = z_ref[0]
    for source in range(1, 8):
        total = total + z_ref[source]
    mass = total[120:128, :]
    lane = lax.broadcasted_iota(jnp.int32, (8, 128), 1)
    for i in range(15):
        unit = d * 15 + i
        rotation = unit >> 5
        here = jnp.sum(jnp.where(lane == rotation, mass, 0.0), axis=1, keepdims=True)
        noise = sigma_ref[pl.ds(unit & 15, 1), :]
        out_ref[:, i * 128 : (i + 1) * 128] = total[i * 8 : i * 8 + 8, :] / (here + REG_WEIGHT * noise)


SMEM = pl.BlockSpec(memory_space=pltpu.SMEM)
VMEM = pl.BlockSpec(memory_space=pltpu.VMEM)


def ring(size, step):
    return [((i + step) % size, i) for i in range(size)]


X = ("x_lo", "x_hi")
X_SWAP = [(0, 3), (1, 2), (2, 1), (3, 0)]
CORE_SWAP = [(0, 1), (1, 0)]


def from_y(value, step):
    return lax.ppermute(value, "y", ring(4, step))


def local(particles, rot_center, shifts, references, class_prior, sigma2):
    x_lo, y, z = lax.axis_index("x_lo"), lax.axis_index("y"), lax.axis_index("z")
    x_hi, core = lax.axis_index("x_hi"), lax.axis_index("core")
    padded = jnp.pad(references, ((0, 0), (0, 2), (0, 0))).reshape(ROWS, WIDE)

    with jax.named_scope("references"):
        quarter = lax.dynamic_slice_in_dim(padded, DIRECT + y * QUART, QUART, 1)
        crossed = lax.ppermute(quarter, X, X_SWAP)
        direct = lax.ppermute(padded[:, :DIRECT], X, X_SWAP)
        quarters = [crossed] + [from_y(crossed, s) for s in (1, 2, 3)]

    with jax.named_scope("shift"):
        own = shift_particles(particles, shifts)
    with jax.named_scope("swap"):
        oth = lax.ppermute(own, "core", CORE_SWAP)
        rot_oth = lax.ppermute(rot_center, "core", CORE_SWAP)
    rot = jnp.concatenate([rot_center, rot_oth]).reshape(1, NP2)

    inv = (1.0 / jnp.concatenate([sigma2, sigma2])).reshape(1, WIDE)
    log_prior = jnp.log(class_prior).reshape(2, 2, 8)
    own_bias = jnp.repeat(log_prior[x_hi, core], 32).reshape(ROWS, 1)
    oth_bias = jnp.repeat(log_prior[1 - x_hi, core], 32).reshape(ROWS, 1)

    with jax.named_scope("scores"):
        first = pl.pallas_call(
            own_kernel,
            out_shape=jax.ShapeDtypeStruct((LANES, ROWS, 128), F32),
            in_specs=[SMEM] + [VMEM] * 5,
            out_specs=VMEM,
            scratch_shapes=[pltpu.VMEM((NP2, 512), BF)],
            compiler_params=pltpu.CompilerParams(vmem_limit_bytes=32 * MB),
        )(jnp.zeros((1,), jnp.int32), own, oth, inv, own_bias, padded)
        offsets = jnp.stack([jnp.int32(0)] + [DIRECT + ((y + s) & 3) * QUART for s in range(4)])
        second, mine = pl.pallas_call(
            other_kernel,
            out_shape=[
                jax.ShapeDtypeStruct((LANES, ROWS, 128), F32),
                jax.ShapeDtypeStruct((8, NP2), F32),
            ],
            in_specs=[SMEM] + [VMEM] * 11,
            out_specs=[VMEM, VMEM],
            scratch_shapes=[pltpu.VMEM((NP2, QUART), BF)],
            compiler_params=pltpu.CompilerParams(vmem_limit_bytes=32 * MB),
        )(offsets, own, oth, inv, oth_bias, direct, *quarters, first, rot)
        theirs = lax.ppermute(mine, "core", CORE_SWAP)

    with jax.named_scope("sums"):
        a, b = pl.pallas_call(
            sums_kernel,
            out_shape=[
                jax.ShapeDtypeStruct((4, 4, BROWS, 128), BF),
                jax.ShapeDtypeStruct((4, 4, BROWS, 128), BF),
            ],
            in_specs=[SMEM] + [VMEM] * 7,
            out_specs=[VMEM, VMEM],
            scratch_shapes=[
                pltpu.VMEM((ROTS * 16, NP2), BF),
                pltpu.VMEM((NP2, 512), BF),
                pltpu.VMEM((ROTS * 16, 512), F32),
                pltpu.VMEM((ROTS * 16, 128), F32),
            ],
            compiler_params=pltpu.CompilerParams(vmem_limit_bytes=40 * MB),
        )(jnp.stack([x_hi, y]), first, second, mine, theirs, rot, own, oth)

    with jax.named_scope("reduce1"):
        b_parts = [b[0]] + [from_y(b[s], -s) for s in (1, 2, 3)]
        a_parts = lax.all_to_all(a, X, 0, 0)
        a_sum = jnp.sum(a_parts.astype(F32), axis=0)
        b_sum = sum(part.astype(F32) for part in b_parts)
    with jax.named_scope("reduce2"):
        a_parts = [a_sum[0]] + [from_y(a_sum[s], -s) for s in (1, 2, 3)]
        b_parts = lax.all_to_all(b_sum, X, 0, 0)
        a_sum = sum(a_parts)
        b_sum = jnp.sum(b_parts, axis=0)

    def for_z(block):
        body = block[: UNITS * 8].reshape(4, 120, 128)
        mass = block[UNITS * 8 : UNITS * 8 + 8] + block[UNITS * 8 + 8 :]
        return jnp.concatenate([body, jnp.broadcast_to(mass[None], (4, 8, 128))], axis=1)

    with jax.named_scope("reduce3"):
        parts = jnp.concatenate([for_z(a_sum), for_z(b_sum)], axis=0)
        parts = lax.all_to_all(parts, "z", 0, 0)

    with jax.named_scope("means"):
        d = (x_lo * 4 + y) * 8 + z
        return pl.pallas_call(
            final_kernel,
            out_shape=jax.ShapeDtypeStruct((8, 1920), F32),
            in_specs=[SMEM, VMEM, VMEM],
            out_specs=VMEM,
            compiler_params=pltpu.CompilerParams(vmem_limit_bytes=16 * MB),
        )(d.reshape(1), parts, sigma2.reshape(16, 128))


def solution(mesh):
    fine = Mesh(mesh.devices.reshape(2, 4, 8, 2, 2), ("x_lo", "y", "z", "x_hi", "core"))
    dom, grp = ("x_lo", "y", "z"), ("x_hi", "core")
    return jax.shard_map(
        local,
        mesh=fine,
        in_specs=(P(dom + grp, None), P(dom + grp), P(None, dom + grp), P(grp, None, None), P(), P()),
        out_specs=P(grp, dom),
        check_vma=False,
    )
```

```python
import functools

import jax
import jax.numpy as jnp
from jax import lax
from jax.experimental import pallas as pl
from jax.experimental.pallas import tpu as pltpu
from jax.sharding import Mesh, PartitionSpec as P

HALFWIN = 6
BOX = 128
KXW = 32
KYW = 64
TWO_PI = 6.283185307179586
REG_WEIGHT = 0.05

F = 2048
WIDE = 2 * F
ROTS = 30
ROWS = ROTS * 8
NP = 448
PAD = 512
NP2 = 2 * PAD
LANES = NP2 // 128
DIRECT = 1536
QUART = 640
UNITS = 60
BROWS = UNITS * 8 + 16

BF = jnp.bfloat16
F32 = jnp.float32
MB = 1024 * 1024


def turn_cos_sin(turns):
    quarter = jnp.floor(4.0 * turns + 0.5)
    x = TWO_PI * (turns - 0.25 * quarter)
    q = quarter - 4.0 * jnp.floor(0.25 * quarter)
    x2 = x * x
    s = x * (1.0 + x2 * (-1.0 / 6 + x2 * (1.0 / 120 + x2 * (-1.0 / 5040 + x2 * (1.0 / 362880)))))
    c = 1.0 + x2 * (-0.5 + x2 * (1.0 / 24 + x2 * (-1.0 / 720 + x2 * (1.0 / 40320))))
    odd = (q == 1.0) | (q == 3.0)
    cos = jnp.where(odd, s, c)
    sin = jnp.where(odd, c, s)
    cos = jnp.where((q == 1.0) | (q == 2.0), -cos, cos)
    sin = jnp.where(q >= 2.0, -sin, sin)
    return cos, sin


def shift_kernel(sh_ref, p_ref, o_ref):
    rows = p_ref.shape[0]
    lane = lax.broadcasted_iota(jnp.int32, (rows, 128), 1)
    kx = (lane & (KXW - 1)).astype(F32)
    ky = ((lane >> 5) - KYW // 2).astype(F32)
    sx = sh_ref[:, 0:1]
    sy = sh_ref[:, 1:2]
    c, s = turn_cos_sin((sx * kx + sy * ky) * (1.0 / BOX))
    step = jnp.broadcast_to(sy * (128 // KXW), (rows, 128)) * (1.0 / BOX)
    dc, ds = turn_cos_sin(step)
    for b in range(F // 128):
        re = p_ref[:, b * 128 : (b + 1) * 128].astype(F32)
        im = p_ref[:, F + b * 128 : F + (b + 1) * 128].astype(F32)
        o_ref[:, b * 128 : (b + 1) * 128] = (re * c + im * s).astype(BF)
        o_ref[:, F + b * 128 : F + (b + 1) * 128] = (im * c - re * s).astype(BF)
        c, s = c * dc - s * ds, s * dc + c * ds


def shift_particles(particles, shifts):
    block = 64
    return pl.pallas_call(
        shift_kernel,
        grid=(NP // block,),
        out_shape=jax.ShapeDtypeStruct((NP, WIDE), BF),
        in_specs=[
            pl.BlockSpec((block, 2), lambda i: (i, 0)),
            pl.BlockSpec((block, WIDE), lambda i: (i, 0)),
        ],
        out_specs=pl.BlockSpec((block, WIDE), lambda i: (i, 0)),
        compiler_params=pltpu.CompilerParams(vmem_limit_bytes=16 * MB),
    )(shifts.T.astype(F32), particles)


def weigh(own_ref, oth_ref, inv_ref, w_ref):
    width = 512
    for start in range(0, WIDE, width):
        cols = slice(start, start + width)
        inv = inv_ref[:, cols]
        w_ref[0:NP, cols] = (own_ref[:, cols].astype(F32) * inv).astype(BF)
        w_ref[PAD : PAD + NP, cols] = (oth_ref[:, cols].astype(F32) * inv).astype(BF)
        w_ref[NP:PAD, cols] = jnp.zeros((PAD - NP, width), BF)
        w_ref[PAD + NP :, cols] = jnp.zeros((PAD - NP, width), BF)


def correlate(w_ref, inv_ref, bias_ref, pieces, acc_ref):
    energy = jnp.zeros((ROWS, 128), F32)
    first = True
    for piece, base, width in pieces:
        for start in range(0, piece.shape[1], width):
            cols = pl.ds(base + start, width)
            inv = inv_ref[:, cols]
            part = lax.dot_general(
                piece[:, start : start + width],
                w_ref[:, cols],
                (((1,), (1,)), ((), ())),
                preferred_element_type=F32,
            )
            for j in range(LANES):
                block = part[:, j * 128 : (j + 1) * 128]
                acc_ref[j] = block if first else acc_ref[j] + block
            first = False
            for lanes in range(0, width, 128):
                v = piece[:, start + lanes : start + lanes + 128].astype(F32)
                energy = energy + v * v * inv[:, lanes : lanes + 128]
    return bias_ref[...] - 0.5 * jnp.sum(energy, axis=1, keepdims=True)


def exponentiate(acc_ref, bias, rot_ref, out_ref, j):
    rot = rot_ref[:, j * 128 : (j + 1) * 128]
    low = jnp.full((8, 128), -jnp.inf, F32)
    top = low
    for r in range(ROTS):
        rows = slice(r * 8, r * 8 + 8)
        score = jnp.where(inside_window(r, rot), acc_ref[j, rows, :] + bias[rows, :], low)
        out_ref[j, rows, :] = score
        top = jnp.maximum(top, score)
    top = jnp.max(top, axis=0, keepdims=True)
    mass = jnp.zeros((8, 128), F32)
    for r in range(ROTS):
        rows = slice(r * 8, r * 8 + 8)
        raised = jnp.exp(out_ref[j, rows, :] - top)
        out_ref[j, rows, :] = raised
        mass = mass + raised
    return top, jnp.sum(mass, axis=0, keepdims=True)


def inside_window(rotation, rot):
    return jnp.abs(jnp.abs(rotation - rot) - ROTS // 2) >= ROTS // 2 - HALFWIN


def own_kernel(own_ref, oth_ref, inv_ref, bias_ref, refs_ref, rot_ref, w_ref, e_ref, stats_ref, acc_ref):
    weigh(own_ref, oth_ref, inv_ref, w_ref)
    bias = correlate(w_ref, inv_ref, bias_ref, [(refs_ref, 0, 512)], acc_ref)
    row = lax.broadcasted_iota(jnp.int32, (8, 128), 0)
    for j in range(LANES):
        top, mass = exponentiate(acc_ref, bias, rot_ref, e_ref, j)
        stats_ref[:, j * 128 : (j + 1) * 128] = jnp.where(row == 0, top, mass)


def other_kernel(
    where_ref, w_ref, inv_ref, bias_ref, rot_ref, first_ref, d_ref, q0, q1, q2, q3,
    e_ref, stats_ref, acc_ref,
):
    pieces = [(d_ref, 0, 512)]
    for s, q in enumerate((q0, q1, q2, q3)):
        pieces.append((q, pl.multiple_of(where_ref[s], 128), QUART))
    bias = correlate(w_ref, inv_ref, bias_ref, pieces, acc_ref)
    row = lax.broadcasted_iota(jnp.int32, (8, 128), 0)
    for j in range(LANES):
        lanes = slice(j * 128, (j + 1) * 128)
        top_b, mass_b = exponentiate(acc_ref, bias, rot_ref, e_ref, j)
        top_a, mass_a = first_ref[0:1, lanes], first_ref[1:2, lanes]
        top = jnp.maximum(top_a, top_b)
        mass = mass_a * jnp.exp(top_a - top) + mass_b * jnp.exp(top_b - top)
        tops = jnp.where(row == 2, top_a, top_b)
        stats_ref[:, lanes] = jnp.where(row == 0, top, jnp.where(row == 1, mass, tops))


def sums_kernel(
    where_ref, first_ref, second_ref, mine_ref, theirs_ref, own_ref, oth_ref,
    a_ref, b_ref, p_ref, acc_ref, mass_ref,
):
    x_hi = where_ref[0]
    y = where_ref[1]
    mass_ref[...] = jnp.zeros_like(mass_ref)
    for j in range(LANES):
        lanes = slice(j * 128, (j + 1) * 128)
        facing = (j + LANES // 2) % LANES
        crossed = slice(facing * 128, (facing + 1) * 128)
        top_a, mass_a = mine_ref[0:1, lanes], mine_ref[1:2, lanes]
        top_b, mass_b = theirs_ref[0:1, crossed], theirs_ref[1:2, crossed]
        top = jnp.maximum(top_a, top_b)
        scale = 1.0 / (mass_a * jnp.exp(top_a - top) + mass_b * jnp.exp(top_b - top))
        scale_a = jnp.exp(mine_ref[2:3, lanes] - top) * scale
        scale_b = jnp.exp(mine_ref[3:4, lanes] - top) * scale
        if j % (LANES // 2) == LANES // 2 - 1:
            used = lax.broadcasted_iota(jnp.int32, (1, 128), 1) < 128 - (PAD - NP)
            scale_a = jnp.where(used, scale_a, 0.0)
            scale_b = jnp.where(used, scale_b, 0.0)
        for r in range(ROTS):
            rows = slice(r * 8, r * 8 + 8)
            p = first_ref[j, rows, :] * scale_a
            q = second_ref[j, rows, :] * scale_b
            low = jnp.where(x_hi == 0, p, q)
            high = jnp.where(x_hi == 0, q, p)
            both = jnp.concatenate([low, high], axis=0)
            p_ref[r * 16 : (r + 1) * 16, lanes] = both.astype(BF)
            mass_ref[r * 16 : (r + 1) * 16, :] += both
    lane = lax.broadcasted_iota(jnp.int32, (16, 128), 1)
    totals = jnp.zeros((16, 128), F32)
    for r in range(ROTS):
        row_sum = jnp.sum(mass_ref[r * 16 : (r + 1) * 16, :], axis=1, keepdims=True)
        totals = jnp.where(lane == r, row_sum, totals)
    slots = [((dest - y) & 3) for dest in range(4)]
    coarse = totals.astype(BF)
    fine = (totals - coarse.astype(F32)).astype(BF)
    for kx in range(2):
        extra = jnp.concatenate(
            [coarse[kx * 8 : kx * 8 + 8].astype(F32), fine[kx * 8 : kx * 8 + 8].astype(F32)], axis=0
        ).astype(BF)
        for x_lo in range(2):
            for dest in range(4):
                a_ref[2 * x_lo + kx, slots[dest], UNITS * 8 : BROWS, :] = extra
                b_ref[slots[dest], 2 * x_lo + kx, UNITS * 8 : BROWS, :] = extra
    width = 512
    for cb in range(WIDE // width):
        cols = slice(cb * width, (cb + 1) * width)
        acc_ref[...] = jnp.dot(p_ref[:, 0:NP], own_ref[:, cols], preferred_element_type=F32) + jnp.dot(
            p_ref[:, PAD : PAD + NP], oth_ref[:, cols], preferred_element_type=F32
        )
        for r in range(ROTS):
            for pair in range(width // 256):
                unit = 32 * r + 4 * cb + 2 * pair
                block = unit // UNITS
                x_lo, dest, z_half = block // 8, (block // 2) % 4, block % 2
                row = (unit % UNITS) * 8
                for kx in range(2):
                    sub = slice(r * 16 + kx * 8, r * 16 + kx * 8 + 8)
                    tile = jnp.concatenate(
                        [
                            acc_ref[sub, pair * 256 : pair * 256 + 128],
                            acc_ref[sub, pair * 256 + 128 : pair * 256 + 256],
                        ],
                        axis=0,
                    ).astype(BF)
                    if z_half == 0:
                        a_ref[2 * x_lo + kx, slots[dest], row : row + 16, :] = tile
                    else:
                        b_ref[slots[dest], 2 * x_lo + kx, row : row + 16, :] = tile


def final_kernel(where_ref, z_ref, sigma_ref, out_ref):
    d = where_ref[0]
    total = z_ref[0]
    for source in range(1, 8):
        total = total + z_ref[source]
    mass = total[120:128, :]
    lane = lax.broadcasted_iota(jnp.int32, (8, 128), 1)
    for i in range(15):
        unit = d * 15 + i
        rotation = unit >> 5
        here = jnp.sum(jnp.where(lane == rotation, mass, 0.0), axis=1, keepdims=True)
        noise = sigma_ref[pl.ds(unit & 15, 1), :]
        out_ref[:, i * 128 : (i + 1) * 128] = total[i * 8 : i * 8 + 8, :] / (here + REG_WEIGHT * noise)


SMEM = pl.BlockSpec(memory_space=pltpu.SMEM)
VMEM = pl.BlockSpec(memory_space=pltpu.VMEM)


def ring(size, step):
    return [((i + step) % size, i) for i in range(size)]


X = ("x_lo", "x_hi")
X_SWAP = [(0, 3), (1, 2), (2, 1), (3, 0)]
CORE_SWAP = [(0, 1), (1, 0)]


def from_y(value, step):
    return lax.ppermute(value, "y", ring(4, step))


def local(particles, rot_center, shifts, references, class_prior, sigma2):
    x_lo, y, z = lax.axis_index("x_lo"), lax.axis_index("y"), lax.axis_index("z")
    x_hi, core = lax.axis_index("x_hi"), lax.axis_index("core")
    refs = jnp.transpose(references, (1, 0, 2)).reshape(ROWS, WIDE)

    with jax.named_scope("references"):
        quarter = lax.dynamic_slice_in_dim(refs, DIRECT + y * QUART, QUART, 1)
        crossed = lax.ppermute(quarter, X, X_SWAP)
        direct = lax.ppermute(refs[:, :DIRECT], X, X_SWAP)
        quarters = [crossed] + [from_y(crossed, s) for s in (1, 2, 3)]

    with jax.named_scope("shift"):
        own = shift_particles(particles, shifts)
    with jax.named_scope("swap"):
        oth = lax.ppermute(own, "core", CORE_SWAP)
        rot_oth = lax.ppermute(rot_center, "core", CORE_SWAP)
    rot = jnp.concatenate([jnp.pad(r, (0, PAD - NP)) for r in (rot_center, rot_oth)]).reshape(1, NP2)

    inv = (1.0 / jnp.concatenate([sigma2, sigma2])).reshape(1, WIDE)
    log_prior = jnp.log(class_prior).reshape(2, 2, 8)
    own_bias = jnp.tile(log_prior[x_hi, core], ROTS).reshape(ROWS, 1)
    oth_bias = jnp.tile(log_prior[1 - x_hi, core], ROTS).reshape(ROWS, 1)

    raised = jax.ShapeDtypeStruct((LANES, ROWS, 128), F32)
    stats = jax.ShapeDtypeStruct((8, NP2), F32)
    with jax.named_scope("scores"):
        weighted, first, first_stats = pl.pallas_call(
            own_kernel,
            out_shape=[jax.ShapeDtypeStruct((NP2, WIDE), BF), raised, stats],
            in_specs=[VMEM] * 6,
            out_specs=[VMEM] * 3,
            scratch_shapes=[pltpu.VMEM((LANES, ROWS, 128), F32)],
            compiler_params=pltpu.CompilerParams(vmem_limit_bytes=32 * MB),
        )(own, oth, inv, own_bias, refs, rot)
        offsets = jnp.stack([DIRECT + ((y + s) & 3) * QUART for s in range(4)])
        second, mine = pl.pallas_call(
            other_kernel,
            out_shape=[raised, stats],
            in_specs=[SMEM] + [VMEM] * 10,
            out_specs=[VMEM] * 2,
            scratch_shapes=[pltpu.VMEM((LANES, ROWS, 128), F32)],
            compiler_params=pltpu.CompilerParams(vmem_limit_bytes=32 * MB),
        )(offsets, weighted, inv, oth_bias, rot, first_stats, direct, *quarters)
        theirs = lax.ppermute(mine, "core", CORE_SWAP)

    with jax.named_scope("sums"):
        a, b = pl.pallas_call(
            sums_kernel,
            out_shape=[
                jax.ShapeDtypeStruct((4, 4, BROWS, 128), BF),
                jax.ShapeDtypeStruct((4, 4, BROWS, 128), BF),
            ],
            in_specs=[SMEM] + [VMEM] * 6,
            out_specs=[VMEM, VMEM],
            scratch_shapes=[
                pltpu.VMEM((ROTS * 16, NP2), BF),
                pltpu.VMEM((ROTS * 16, 512), F32),
                pltpu.VMEM((ROTS * 16, 128), F32),
            ],
            compiler_params=pltpu.CompilerParams(vmem_limit_bytes=40 * MB),
        )(jnp.stack([x_hi, y]), first, second, mine, theirs, own, oth)

    with jax.named_scope("reduce1"):
        b_parts = [b[0]] + [from_y(b[s], -s) for s in (1, 2, 3)]
        a_parts = lax.all_to_all(a, X, 0, 0)
        a_sum = jnp.sum(a_parts.astype(F32), axis=0)
        b_sum = sum(part.astype(F32) for part in b_parts)
    with jax.named_scope("reduce2"):
        a_parts = [a_sum[0]] + [from_y(a_sum[s], -s) for s in (1, 2, 3)]
        b_parts = lax.all_to_all(b_sum, X, 0, 0)
        a_sum = sum(a_parts)
        b_sum = jnp.sum(b_parts, axis=0)

    def for_z(block):
        body = block[: UNITS * 8].reshape(4, 120, 128)
        mass = block[UNITS * 8 : UNITS * 8 + 8] + block[UNITS * 8 + 8 :]
        return jnp.concatenate([body, jnp.broadcast_to(mass[None], (4, 8, 128))], axis=1)

    with jax.named_scope("reduce3"):
        parts = jnp.concatenate([for_z(a_sum), for_z(b_sum)], axis=0)
        parts = lax.all_to_all(parts, "z", 0, 0)

    with jax.named_scope("means"):
        d = (x_lo * 4 + y) * 8 + z
        return pl.pallas_call(
            final_kernel,
            out_shape=jax.ShapeDtypeStruct((8, 1920), F32),
            in_specs=[SMEM, VMEM, VMEM],
            out_specs=VMEM,
            compiler_params=pltpu.CompilerParams(vmem_limit_bytes=16 * MB),
        )(d.reshape(1), parts, sigma2.reshape(16, 128))


def solution(mesh):
    fine = Mesh(mesh.devices.reshape(2, 4, 8, 2, 2), ("x_lo", "y", "z", "x_hi", "core"))
    dom, grp = ("x_lo", "y", "z"), ("x_hi", "core")
    return jax.shard_map(
        local,
        mesh=fine,
        in_specs=(P(dom + grp, None), P(dom + grp), P(None, dom + grp), P(grp, None, None), P(), P()),
        out_specs=P(grp, dom),
        check_vma=False,
    )
```

```python
import functools

import jax
import jax.numpy as jnp
from jax import lax
from jax.experimental import pallas as pl
from jax.experimental.pallas import tpu as pltpu
from jax.sharding import Mesh, PartitionSpec as P

HALFWIN = 6
BOX = 128
KXW = 32
KYW = 64
TWO_PI = 6.283185307179586
REG_WEIGHT = 0.05

F = 2048
WIDE = 2 * F
ROTS = 30
ROWS = ROTS * 8
NP = 448
PAD = 512
NP2 = 2 * PAD
LANES = NP2 // 128
DIRECT = 1536
QUART = 640
UNITS = 15
FIRST = 11
GROWS = FIRST * 8 + 8
HROWS = (UNITS - FIRST) * 8

BF = jnp.bfloat16
F32 = jnp.float32
MB = 1024 * 1024


def turn_cos_sin(turns):
    quarter = jnp.floor(4.0 * turns + 0.5)
    x = TWO_PI * (turns - 0.25 * quarter)
    q = quarter - 4.0 * jnp.floor(0.25 * quarter)
    x2 = x * x
    s = x * (1.0 + x2 * (-1.0 / 6 + x2 * (1.0 / 120 + x2 * (-1.0 / 5040 + x2 * (1.0 / 362880)))))
    c = 1.0 + x2 * (-0.5 + x2 * (1.0 / 24 + x2 * (-1.0 / 720 + x2 * (1.0 / 40320))))
    odd = (q == 1.0) | (q == 3.0)
    cos = jnp.where(odd, s, c)
    sin = jnp.where(odd, c, s)
    cos = jnp.where((q == 1.0) | (q == 2.0), -cos, cos)
    sin = jnp.where(q >= 2.0, -sin, sin)
    return cos, sin


def shift_kernel(sh_ref, p_ref, o_ref):
    rows = p_ref.shape[0]
    lane = lax.broadcasted_iota(jnp.int32, (rows, 128), 1)
    kx = (lane & (KXW - 1)).astype(F32)
    ky = ((lane >> 5) - KYW // 2).astype(F32)
    sx = sh_ref[:, 0:1]
    sy = sh_ref[:, 1:2]
    c, s = turn_cos_sin((sx * kx + sy * ky) * (1.0 / BOX))
    step = jnp.broadcast_to(sy * (128 // KXW), (rows, 128)) * (1.0 / BOX)
    dc, ds = turn_cos_sin(step)
    for b in range(F // 128):
        re = p_ref[:, b * 128 : (b + 1) * 128].astype(F32)
        im = p_ref[:, F + b * 128 : F + (b + 1) * 128].astype(F32)
        o_ref[:, b * 128 : (b + 1) * 128] = (re * c + im * s).astype(BF)
        o_ref[:, F + b * 128 : F + (b + 1) * 128] = (im * c - re * s).astype(BF)
        c, s = c * dc - s * ds, s * dc + c * ds


def shift_particles(particles, shifts):
    block = 64
    return pl.pallas_call(
        shift_kernel,
        grid=(NP // block,),
        out_shape=jax.ShapeDtypeStruct((NP, WIDE), BF),
        in_specs=[
            pl.BlockSpec((block, 2), lambda i: (i, 0)),
            pl.BlockSpec((block, WIDE), lambda i: (i, 0)),
        ],
        out_specs=pl.BlockSpec((block, WIDE), lambda i: (i, 0)),
        cost_estimate=cost(5),
            compiler_params=pltpu.CompilerParams(vmem_limit_bytes=8 * MB),
    )(shifts.T.astype(F32), particles)


def weigh(own_ref, oth_ref, inv_ref, w_ref):
    width = 512
    for start in range(0, WIDE, width):
        cols = slice(start, start + width)
        inv = inv_ref[:, cols]
        w_ref[0:NP, cols] = (own_ref[:, cols].astype(F32) * inv).astype(BF)
        w_ref[PAD : PAD + NP, cols] = (oth_ref[:, cols].astype(F32) * inv).astype(BF)
        w_ref[NP:PAD, cols] = jnp.zeros((PAD - NP, width), BF)
        w_ref[PAD + NP :, cols] = jnp.zeros((PAD - NP, width), BF)


def correlate(w_ref, inv_ref, bias_ref, pieces, acc_ref):
    energy = jnp.zeros((ROWS, 128), F32)
    first = True
    for piece, base, width in pieces:
        for start in range(0, piece.shape[1], width):
            cols = pl.ds(base + start, width)
            inv = inv_ref[:, cols]
            part = lax.dot_general(
                piece[:, start : start + width],
                w_ref[:, cols],
                (((1,), (1,)), ((), ())),
                preferred_element_type=F32,
            )
            for j in range(LANES):
                block = part[:, j * 128 : (j + 1) * 128]
                acc_ref[j] = block if first else acc_ref[j] + block
            first = False
            for lanes in range(0, width, 128):
                v = piece[:, start + lanes : start + lanes + 128].astype(F32)
                energy = energy + v * v * inv[:, lanes : lanes + 128]
    return bias_ref[...] - 0.5 * jnp.sum(energy, axis=1, keepdims=True)


def exponentiate(acc_ref, bias, rot_ref, out_ref, j):
    rot = rot_ref[:, j * 128 : (j + 1) * 128]
    low = jnp.full((8, 128), -jnp.inf, F32)
    top = low
    for r in range(ROTS):
        rows = slice(r * 8, r * 8 + 8)
        score = jnp.where(inside_window(r, rot), acc_ref[j, rows, :] + bias[rows, :], low)
        out_ref[j, rows, :] = score
        top = jnp.maximum(top, score)
    top = jnp.max(top, axis=0, keepdims=True)
    mass = jnp.zeros((8, 128), F32)
    for r in range(ROTS):
        rows = slice(r * 8, r * 8 + 8)
        raised = jnp.exp(out_ref[j, rows, :] - top)
        out_ref[j, rows, :] = raised
        mass = mass + raised
    return top, jnp.sum(mass, axis=0, keepdims=True)


def inside_window(rotation, rot):
    return jnp.abs(jnp.abs(rotation - rot) - ROTS // 2) >= ROTS // 2 - HALFWIN


def own_kernel(own_ref, oth_ref, inv_ref, bias_ref, refs_ref, rot_ref, w_ref, e_ref, stats_ref, acc_ref):
    weigh(own_ref, oth_ref, inv_ref, w_ref)
    bias = correlate(w_ref, inv_ref, bias_ref, [(refs_ref, 0, 512)], acc_ref)
    row = lax.broadcasted_iota(jnp.int32, (8, 128), 0)
    for j in range(LANES):
        top, mass = exponentiate(acc_ref, bias, rot_ref, e_ref, j)
        stats_ref[:, j * 128 : (j + 1) * 128] = jnp.where(row == 0, top, mass)


def other_kernel(
    where_ref, w_ref, inv_ref, bias_ref, rot_ref, first_ref, d_ref, q0, q1, q2, q3,
    e_ref, stats_ref, acc_ref,
):
    pieces = [(d_ref, 0, 512)]
    for s, q in enumerate((q0, q1, q2, q3)):
        pieces.append((q, pl.multiple_of(where_ref[s], 128), QUART))
    bias = correlate(w_ref, inv_ref, bias_ref, pieces, acc_ref)
    row = lax.broadcasted_iota(jnp.int32, (8, 128), 0)
    for j in range(LANES):
        lanes = slice(j * 128, (j + 1) * 128)
        top_b, mass_b = exponentiate(acc_ref, bias, rot_ref, e_ref, j)
        top_a, mass_a = first_ref[0:1, lanes], first_ref[1:2, lanes]
        top = jnp.maximum(top_a, top_b)
        mass = mass_a * jnp.exp(top_a - top) + mass_b * jnp.exp(top_b - top)
        tops = jnp.where(row == 2, top_a, top_b)
        stats_ref[:, lanes] = jnp.where(row == 0, top, jnp.where(row == 1, mass, tops))


def sums_kernel(
    where_ref, first_ref, second_ref, mine_ref, theirs_ref, own_ref, oth_ref,
    g_ref, h_ref, p_ref, acc_ref, mass_ref,
):
    x_hi = where_ref[0]
    z = where_ref[1]
    mass_ref[...] = jnp.zeros_like(mass_ref)
    for j in range(LANES):
        lanes = slice(j * 128, (j + 1) * 128)
        facing = (j + LANES // 2) % LANES
        crossed = slice(facing * 128, (facing + 1) * 128)
        top_a, mass_a = mine_ref[0:1, lanes], mine_ref[1:2, lanes]
        top_b, mass_b = theirs_ref[0:1, crossed], theirs_ref[1:2, crossed]
        top = jnp.maximum(top_a, top_b)
        scale = 1.0 / (mass_a * jnp.exp(top_a - top) + mass_b * jnp.exp(top_b - top))
        scale_a = jnp.exp(mine_ref[2:3, lanes] - top) * scale
        scale_b = jnp.exp(mine_ref[3:4, lanes] - top) * scale
        if j % (LANES // 2) == LANES // 2 - 1:
            used = lax.broadcasted_iota(jnp.int32, (1, 128), 1) < 128 - (PAD - NP)
            scale_a = jnp.where(used, scale_a, 0.0)
            scale_b = jnp.where(used, scale_b, 0.0)
        for r in range(ROTS):
            rows = slice(r * 8, r * 8 + 8)
            p = first_ref[j, rows, :] * scale_a
            q = second_ref[j, rows, :] * scale_b
            low = jnp.where(x_hi == 0, p, q)
            high = jnp.where(x_hi == 0, q, p)
            both = jnp.concatenate([low, high], axis=0)
            p_ref[r * 16 : (r + 1) * 16, lanes] = both.astype(BF)
            mass_ref[r * 16 : (r + 1) * 16, :] += both
    lane = lax.broadcasted_iota(jnp.int32, (16, 128), 1)
    totals = jnp.zeros((16, 128), F32)
    for r in range(ROTS):
        row_sum = jnp.sum(mass_ref[r * 16 : (r + 1) * 16, :], axis=1, keepdims=True)
        totals = jnp.where(lane == r, row_sum, totals)
    coarse = totals.astype(BF).astype(F32)
    extra = jnp.where(lane < 32, coarse, pltpu.roll(totals - coarse, 32, 1))
    slots = [(dest - z) & 7 for dest in range(8)]
    width = 512

    def unit_tile(unit, kx):
        sub = (unit // 32) * 16 + kx * 8
        return acc_ref[sub : sub + 8, (unit % 32) * 128 : (unit % 32 + 1) * 128]

    def ready(unit):
        return (unit % 32) * 128 // width

    for cb in range(WIDE // width):
        cols = slice(cb * width, (cb + 1) * width)
        acc_ref[:, cols] = jnp.dot(p_ref[:, 0:NP], own_ref[:, cols], preferred_element_type=F32) + jnp.dot(
            p_ref[:, PAD : PAD + NP], oth_ref[:, cols], preferred_element_type=F32
        )
        for chunk in range(64):
            xy, dest = chunk // 8, chunk % 8
            for i in range(0, UNITS + 1, 2):
                unit = chunk * UNITS + (i if i < FIRST else i - 1)
                paired = i != FIRST - 1
                if max(ready(unit), ready(unit + 1) if paired else 0) != cb:
                    continue
                for kx in range(2):
                    upper = unit_tile(unit + 1, kx) if paired else extra[kx * 8 : kx * 8 + 8]
                    tile = jnp.concatenate([unit_tile(unit, kx), upper], axis=0).astype(BF)
                    if i < FIRST:
                        g_ref[2 * xy + kx, slots[dest], i * 8 : i * 8 + 16, :] = tile
                    else:
                        row = (i - FIRST - 1) * 8
                        h_ref[slots[dest], 2 * xy + kx, row : row + 16, :] = tile


def sum_g_kernel(g_ref, *out_refs):
    for slot, out_ref in enumerate(out_refs):
        total = g_ref[0, slot].astype(F32)
        for source in range(1, 16):
            total = total + g_ref[source, slot].astype(F32)
        out_ref[...] = total


def sum_h_kernel(*refs):
    out_ref = refs[-1]
    for xy in range(16):
        total = refs[0][xy].astype(F32)
        for ref in refs[1:-1]:
            total = total + ref[xy].astype(F32)
        out_ref[xy] = total


def final_kernel(where_ref, sigma_ref, h_ref, *refs):
    d = where_ref[0]
    g_refs, out_ref = refs[:-1], refs[-1]

    def g_rows(rows):
        total = g_refs[0][rows, :]
        for ref in g_refs[1:]:
            total = total + ref[rows, :]
        return total

    def h_rows(rows):
        total = h_ref[0, rows, :]
        for source in range(1, 16):
            total = total + h_ref[source, rows, :]
        return total

    mass = g_rows(slice(FIRST * 8, GROWS))
    mass = mass + pltpu.roll(mass, 128 - 32, 1)
    lane = lax.broadcasted_iota(jnp.int32, (8, 128), 1)
    for i in range(UNITS):
        unit = d * UNITS + i
        rotation = unit >> 5
        here = jnp.sum(jnp.where(lane == rotation, mass, 0.0), axis=1, keepdims=True)
        noise = sigma_ref[pl.ds(unit & 15, 1), :]
        total = g_rows(slice(i * 8, i * 8 + 8)) if i < FIRST else h_rows(slice((i - FIRST) * 8, (i - FIRST) * 8 + 8))
        out_ref[:, i * 128 : (i + 1) * 128] = total / (here + REG_WEIGHT * noise)


def cost(micros):
    return pl.CostEstimate(flops=int(micros * 1e9), bytes_accessed=0, transcendentals=0)


SMEM = pl.BlockSpec(memory_space=pltpu.SMEM)
VMEM = pl.BlockSpec(memory_space=pltpu.VMEM)


def ring(size, step):
    return [((i + step) % size, i) for i in range(size)]


X = ("x_lo", "x_hi")
X_SWAP = [(0, 3), (1, 2), (2, 1), (3, 0)]
CORE_SWAP = [(0, 1), (1, 0)]


XY = ("x_lo", "y", "x_hi")


def to_z(value, step):
    return lax.ppermute(value, "z", ring(8, -step))


def from_y(value, step):
    return lax.ppermute(value, "y", ring(4, step))


def local(particles, rot_center, shifts, references, class_prior, sigma2):
    x_lo, y, z = lax.axis_index("x_lo"), lax.axis_index("y"), lax.axis_index("z")
    x_hi, core = lax.axis_index("x_hi"), lax.axis_index("core")
    refs = jnp.transpose(references, (1, 0, 2)).reshape(ROWS, WIDE)

    with jax.named_scope("references"):
        quarter = lax.dynamic_slice_in_dim(refs, DIRECT + y * QUART, QUART, 1)
        crossed = lax.ppermute(quarter, X, X_SWAP)
        direct, crossed = lax.optimization_barrier((refs[:, :DIRECT], crossed))
        direct = lax.ppermute(direct, X, X_SWAP)
        quarters = [crossed] + [from_y(crossed, s) for s in (1, 2, 3)]

    with jax.named_scope("swap"):
        raw = lax.ppermute(particles, "core", CORE_SWAP)
        rot_oth = lax.ppermute(rot_center, "core", CORE_SWAP)
        shifts_oth = lax.ppermute(shifts, "core", CORE_SWAP)
    with jax.named_scope("shift"):
        own = shift_particles(particles, shifts)
        raw, crossed = lax.optimization_barrier((raw, crossed))
        oth = shift_particles(raw, shifts_oth)
    rot = jnp.concatenate([jnp.pad(r, (0, PAD - NP)) for r in (rot_center, rot_oth)]).reshape(1, NP2)

    inv = (1.0 / jnp.concatenate([sigma2, sigma2])).reshape(1, WIDE)
    log_prior = jnp.log(class_prior).reshape(2, 2, 8)
    own_bias = jnp.tile(log_prior[x_hi, core], ROTS).reshape(ROWS, 1)
    oth_bias = jnp.tile(log_prior[1 - x_hi, core], ROTS).reshape(ROWS, 1)

    raised = jax.ShapeDtypeStruct((LANES, ROWS, 128), F32)
    stats = jax.ShapeDtypeStruct((8, NP2), F32)
    with jax.named_scope("scores"):
        weighted, first, first_stats = pl.pallas_call(
            own_kernel,
            out_shape=[jax.ShapeDtypeStruct((NP2, WIDE), BF), raised, stats],
            in_specs=[VMEM] * 6,
            out_specs=[VMEM] * 3,
            scratch_shapes=[pltpu.VMEM((LANES, ROWS, 128), F32)],
            cost_estimate=cost(7),
            compiler_params=pltpu.CompilerParams(vmem_limit_bytes=24 * MB),
        )(own, oth, inv, own_bias, refs, rot)
        offsets = jnp.stack([DIRECT + ((y + s) & 3) * QUART for s in range(4)])
        second, mine = pl.pallas_call(
            other_kernel,
            out_shape=[raised, stats],
            in_specs=[SMEM] + [VMEM] * 10,
            out_specs=[VMEM] * 2,
            scratch_shapes=[pltpu.VMEM((LANES, ROWS, 128), F32)],
            cost_estimate=cost(5),
            compiler_params=pltpu.CompilerParams(vmem_limit_bytes=16 * MB),
        )(offsets, weighted, inv, oth_bias, rot, first_stats, direct, *quarters)
        theirs = lax.ppermute(mine, "core", CORE_SWAP)

    with jax.named_scope("sums"):
        g, h = pl.pallas_call(
            sums_kernel,
            out_shape=[
                jax.ShapeDtypeStruct((16, 8, GROWS, 128), BF),
                jax.ShapeDtypeStruct((8, 16, HROWS, 128), BF),
            ],
            in_specs=[SMEM] + [VMEM] * 6,
            out_specs=[VMEM, VMEM],
            scratch_shapes=[
                pltpu.VMEM((ROTS * 16, NP2), BF),
                pltpu.VMEM((ROTS * 16, WIDE), F32),
                pltpu.VMEM((ROTS * 16, 128), F32),
            ],
            cost_estimate=cost(8),
            compiler_params=pltpu.CompilerParams(vmem_limit_bytes=28 * MB),
        )(jnp.stack([x_hi, z]), first, second, mine, theirs, own, oth)

    with jax.named_scope("reduce1"):
        h_parts = [h[0]] + [to_z(h[s], s) for s in range(1, 8)]
        g_parts = lax.all_to_all(g, XY, 0, 0)
        h_sum = pl.pallas_call(
            sum_h_kernel,
            out_shape=jax.ShapeDtypeStruct((16, HROWS, 128), F32),
            in_specs=[VMEM] * 8,
            out_specs=VMEM,
        )(*h_parts)
        g_sums = pl.pallas_call(
            sum_g_kernel,
            out_shape=[jax.ShapeDtypeStruct((GROWS, 128), F32)] * 8,
            in_specs=[VMEM],
            out_specs=[VMEM] * 8,
            compiler_params=pltpu.CompilerParams(vmem_limit_bytes=16 * MB),
        )(g_parts)
    with jax.named_scope("reduce2"):
        h_sums = lax.all_to_all(h_sum, XY, 0, 0)
        g_sums = [g_sums[0]] + [to_z(g_sums[s], s) for s in range(1, 8)]

    with jax.named_scope("means"):
        d = (x_lo * 4 + y) * 8 + z
        return pl.pallas_call(
            final_kernel,
            out_shape=jax.ShapeDtypeStruct((8, 1920), F32),
            in_specs=[SMEM] + [VMEM] * 10,
            out_specs=VMEM,
            compiler_params=pltpu.CompilerParams(vmem_limit_bytes=16 * MB),
        )(d.reshape(1), sigma2.reshape(16, 128), h_sums, *g_sums)


def solution(mesh):
    fine = Mesh(mesh.devices.reshape(2, 4, 8, 2, 2), ("x_lo", "y", "z", "x_hi", "core"))
    dom, grp = ("x_lo", "y", "z"), ("x_hi", "core")
    return jax.shard_map(
        local,
        mesh=fine,
        in_specs=(P(dom + grp, None), P(dom + grp), P(None, dom + grp), P(grp, None, None), P(), P()),
        out_specs=P(grp, dom),
        check_vma=False,
    )
```

```python
import functools

import jax
import jax.numpy as jnp
from jax import lax
from jax.experimental import pallas as pl
from jax.experimental.pallas import tpu as pltpu
from jax.sharding import Mesh, PartitionSpec as P

HALFWIN = 6
BOX = 128
KXW = 32
KYW = 64
TWO_PI = 6.283185307179586
REG_WEIGHT = 0.05

F = 2048
WIDE = 2 * F
ROTS = 30
ROWS = ROTS * 8
NP = 448
PAD = 512
NP2 = 2 * PAD
LANES = NP2 // 128
DIRECT = 1536
QUART = 640
UNITS = 15
PART = 4
PROWS = PART * 8

BF = jnp.bfloat16
F32 = jnp.float32
MB = 1024 * 1024


def turn_cos_sin(turns):
    quarter = jnp.floor(4.0 * turns + 0.5)
    x = TWO_PI * (turns - 0.25 * quarter)
    q = quarter - 4.0 * jnp.floor(0.25 * quarter)
    x2 = x * x
    s = x * (1.0 + x2 * (-1.0 / 6 + x2 * (1.0 / 120 + x2 * (-1.0 / 5040 + x2 * (1.0 / 362880)))))
    c = 1.0 + x2 * (-0.5 + x2 * (1.0 / 24 + x2 * (-1.0 / 720 + x2 * (1.0 / 40320))))
    odd = (q == 1.0) | (q == 3.0)
    cos = jnp.where(odd, s, c)
    sin = jnp.where(odd, c, s)
    cos = jnp.where((q == 1.0) | (q == 2.0), -cos, cos)
    sin = jnp.where(q >= 2.0, -sin, sin)
    return cos, sin


def shift_kernel(sh_ref, p_ref, o_ref):
    rows = p_ref.shape[0]
    lane = lax.broadcasted_iota(jnp.int32, (rows, 128), 1)
    kx = (lane & (KXW - 1)).astype(F32)
    ky = ((lane >> 5) - KYW // 2).astype(F32)
    sx = sh_ref[:, 0:1]
    sy = sh_ref[:, 1:2]
    c, s = turn_cos_sin((sx * kx + sy * ky) * (1.0 / BOX))
    step = jnp.broadcast_to(sy * (128 // KXW), (rows, 128)) * (1.0 / BOX)
    dc, ds = turn_cos_sin(step)
    for b in range(F // 128):
        re = p_ref[:, b * 128 : (b + 1) * 128].astype(F32)
        im = p_ref[:, F + b * 128 : F + (b + 1) * 128].astype(F32)
        o_ref[:, b * 128 : (b + 1) * 128] = (re * c + im * s).astype(BF)
        o_ref[:, F + b * 128 : F + (b + 1) * 128] = (im * c - re * s).astype(BF)
        c, s = c * dc - s * ds, s * dc + c * ds


def shift_particles(particles, shifts):
    block = 64
    return pl.pallas_call(
        shift_kernel,
        grid=(NP // block,),
        out_shape=jax.ShapeDtypeStruct((NP, WIDE), BF),
        in_specs=[
            pl.BlockSpec((block, 2), lambda i: (i, 0)),
            pl.BlockSpec((block, WIDE), lambda i: (i, 0)),
        ],
        out_specs=pl.BlockSpec((block, WIDE), lambda i: (i, 0)),
        cost_estimate=cost(5),
            compiler_params=pltpu.CompilerParams(vmem_limit_bytes=8 * MB),
    )(shifts.T.astype(F32), particles)


def weigh(own_ref, oth_ref, inv_ref, w_ref):
    width = 512
    for start in range(0, WIDE, width):
        cols = slice(start, start + width)
        inv = inv_ref[:, cols]
        w_ref[0:NP, cols] = (own_ref[:, cols].astype(F32) * inv).astype(BF)
        w_ref[PAD : PAD + NP, cols] = (oth_ref[:, cols].astype(F32) * inv).astype(BF)
        w_ref[NP:PAD, cols] = jnp.zeros((PAD - NP, width), BF)
        w_ref[PAD + NP :, cols] = jnp.zeros((PAD - NP, width), BF)


def correlate(w_ref, inv_ref, bias_ref, pieces, acc_ref):
    energy = jnp.zeros((ROWS, 128), F32)
    first = True
    for piece, base, width in pieces:
        for start in range(0, piece.shape[1], width):
            cols = pl.ds(base + start, width)
            inv = inv_ref[:, cols]
            part = lax.dot_general(
                piece[:, start : start + width],
                w_ref[:, cols],
                (((1,), (1,)), ((), ())),
                preferred_element_type=F32,
            )
            for j in range(LANES):
                block = part[:, j * 128 : (j + 1) * 128]
                acc_ref[j] = block if first else acc_ref[j] + block
            first = False
            for lanes in range(0, width, 128):
                v = piece[:, start + lanes : start + lanes + 128].astype(F32)
                energy = energy + v * v * inv[:, lanes : lanes + 128]
    return bias_ref[...] - 0.5 * jnp.sum(energy, axis=1, keepdims=True)


def exponentiate(acc_ref, bias, rot_ref, out_ref, j):
    rot = rot_ref[:, j * 128 : (j + 1) * 128]
    low = jnp.full((8, 128), -jnp.inf, F32)
    top = low
    for r in range(ROTS):
        rows = slice(r * 8, r * 8 + 8)
        score = jnp.where(inside_window(r, rot), acc_ref[j, rows, :] + bias[rows, :], low)
        out_ref[j, rows, :] = score
        top = jnp.maximum(top, score)
    top = jnp.max(top, axis=0, keepdims=True)
    mass = jnp.zeros((8, 128), F32)
    for r in range(ROTS):
        rows = slice(r * 8, r * 8 + 8)
        raised = jnp.exp(out_ref[j, rows, :] - top)
        out_ref[j, rows, :] = raised
        mass = mass + raised
    return top, jnp.sum(mass, axis=0, keepdims=True)


def inside_window(rotation, rot):
    return jnp.abs(jnp.abs(rotation - rot) - ROTS // 2) >= ROTS // 2 - HALFWIN


def own_kernel(own_ref, oth_ref, inv_ref, bias_ref, refs_ref, rot_ref, w_ref, e_ref, stats_ref, acc_ref):
    weigh(own_ref, oth_ref, inv_ref, w_ref)
    bias = correlate(w_ref, inv_ref, bias_ref, [(refs_ref, 0, 512)], acc_ref)
    row = lax.broadcasted_iota(jnp.int32, (8, 128), 0)
    for j in range(LANES):
        top, mass = exponentiate(acc_ref, bias, rot_ref, e_ref, j)
        stats_ref[:, j * 128 : (j + 1) * 128] = jnp.where(row == 0, top, mass)


def other_kernel(
    where_ref, w_ref, inv_ref, bias_ref, rot_ref, first_ref, d_ref, q0, q1, q2, q3,
    e_ref, stats_ref, acc_ref,
):
    pieces = [(d_ref, 0, 512)]
    for s, q in enumerate((q0, q1, q2, q3)):
        pieces.append((q, pl.multiple_of(where_ref[s], 128), QUART))
    bias = correlate(w_ref, inv_ref, bias_ref, pieces, acc_ref)
    row = lax.broadcasted_iota(jnp.int32, (8, 128), 0)
    for j in range(LANES):
        lanes = slice(j * 128, (j + 1) * 128)
        top_b, mass_b = exponentiate(acc_ref, bias, rot_ref, e_ref, j)
        top_a, mass_a = first_ref[0:1, lanes], first_ref[1:2, lanes]
        top = jnp.maximum(top_a, top_b)
        mass = mass_a * jnp.exp(top_a - top) + mass_b * jnp.exp(top_b - top)
        tops = jnp.where(row == 2, top_a, top_b)
        stats_ref[:, lanes] = jnp.where(row == 0, top, jnp.where(row == 1, mass, tops))


def sums_kernel(where_ref, first_ref, second_ref, mine_ref, theirs_ref, own_ref, oth_ref, *refs):
    parts, (p_ref, acc_ref, mass_ref, extra_ref) = refs[:16], refs[16:]
    x_hi, x_lo, y = where_ref[0], where_ref[1], where_ref[2]
    mass_ref[...] = jnp.zeros_like(mass_ref)
    for j in range(LANES):
        lanes = slice(j * 128, (j + 1) * 128)
        facing = (j + LANES // 2) % LANES
        crossed = slice(facing * 128, (facing + 1) * 128)
        top_a, mass_a = mine_ref[0:1, lanes], mine_ref[1:2, lanes]
        top_b, mass_b = theirs_ref[0:1, crossed], theirs_ref[1:2, crossed]
        top = jnp.maximum(top_a, top_b)
        scale = 1.0 / (mass_a * jnp.exp(top_a - top) + mass_b * jnp.exp(top_b - top))
        scale_a = jnp.exp(mine_ref[2:3, lanes] - top) * scale
        scale_b = jnp.exp(mine_ref[3:4, lanes] - top) * scale
        if j % (LANES // 2) == LANES // 2 - 1:
            used = lax.broadcasted_iota(jnp.int32, (1, 128), 1) < 128 - (PAD - NP)
            scale_a = jnp.where(used, scale_a, 0.0)
            scale_b = jnp.where(used, scale_b, 0.0)
        for r in range(ROTS):
            rows = slice(r * 8, r * 8 + 8)
            p = first_ref[j, rows, :] * scale_a
            q = second_ref[j, rows, :] * scale_b
            low = jnp.where(x_hi == 0, p, q)
            high = jnp.where(x_hi == 0, q, p)
            both = jnp.concatenate([low, high], axis=0)
            p_ref[r * 16 : (r + 1) * 16, lanes] = both.astype(BF)
            mass_ref[r * 16 : (r + 1) * 16, :] += both
    lane = lax.broadcasted_iota(jnp.int32, (16, 128), 1)
    totals = jnp.zeros((16, 128), F32)
    for r in range(ROTS):
        row_sum = jnp.sum(mass_ref[r * 16 : (r + 1) * 16, :], axis=1, keepdims=True)
        totals = jnp.where(lane == r, row_sum, totals)
    coarse = totals.astype(BF).astype(F32)
    extra_ref[...] = jnp.where(lane < 32, coarse, pltpu.roll(totals - coarse, 32, 1))
    width = 512
    for cb in range(WIDE // width):
        cols = slice(cb * width, (cb + 1) * width)
        part = jnp.dot(p_ref[:, 0:NP], own_ref[:, cols], preferred_element_type=F32) + jnp.dot(
            p_ref[:, PAD : PAD + NP], oth_ref[:, cols], preferred_element_type=F32
        )
        for j in range(width // 128):
            acc_ref[cb * (width // 128) + j] = part[:, j * 128 : (j + 1) * 128]

    def place(dest_z, carry):
        for sx in range(4):
            kx, dest_x = x_hi ^ (sx >> 1), x_lo ^ (sx & 1)
            for sy in range(4):
                base = ((dest_x * 4 + ((y + sy) & 3)) * 8 + dest_z) * UNITS

                def tile(i):
                    if i == UNITS:
                        return extra_ref[pl.ds(pl.multiple_of(kx * 8, 8), 8), :]
                    unit = base + i
                    return acc_ref[unit & 31, pl.ds(pl.multiple_of((unit >> 5) * 16 + kx * 8, 8), 8), :]

                for i in range(0, UNITS + 1, 2):
                    both = jnp.concatenate([tile(i), tile(i + 1)], axis=0).astype(BF)
                    number = i // PART
                    hop, rest = (sx, sy) if number % 2 == 0 else (sy, sx)
                    row = (i % PART) * 8
                    parts[number * 4 + hop][rest, dest_z, row : row + 16, :] = both
        return carry

    lax.fori_loop(0, 8, place, 0)


def first_sum_kernel(*refs):
    for rest, out_ref in enumerate(refs[4:]):
        for z in range(8):
            total = refs[0][rest, z].astype(F32)
            for ref in refs[1:4]:
                total = total + ref[rest, z].astype(F32)
            out_ref[z] = total


def second_sum_kernel(*refs):
    out_ref = refs[8]
    for half in range(2):
        for z in range(8):
            total = refs[4 * half][z]
            for ref in refs[4 * half + 1 : 4 * half + 4]:
                total = total + ref[z]
            out_ref[z, half * PROWS : (half + 1) * PROWS, :] = total


def final_kernel(where_ref, sigma_ref, *refs):
    d = where_ref[0]
    out_ref = refs[2]

    def rows_of(i):
        ref, row = refs[i // (2 * PART)], (i % (2 * PART)) * 8
        total = ref[0, row : row + 8, :]
        for source in range(1, 8):
            total = total + ref[source, row : row + 8, :]
        return total

    mass = rows_of(UNITS)
    mass = mass + pltpu.roll(mass, 128 - 32, 1)
    lane = lax.broadcasted_iota(jnp.int32, (8, 128), 1)
    for i in range(UNITS):
        unit = d * UNITS + i
        rotation = unit >> 5
        here = jnp.sum(jnp.where(lane == rotation, mass, 0.0), axis=1, keepdims=True)
        noise = sigma_ref[pl.ds(unit & 15, 1), :]
        out_ref[:, i * 128 : (i + 1) * 128] = rows_of(i) / (here + REG_WEIGHT * noise)


def cost(micros):
    return pl.CostEstimate(flops=int(micros * 1e9), bytes_accessed=0, transcendentals=0)


SMEM = pl.BlockSpec(memory_space=pltpu.SMEM)
VMEM = pl.BlockSpec(memory_space=pltpu.VMEM)


def ring(size, step):
    return [((i + step) % size, i) for i in range(size)]


X = ("x_lo", "x_hi")
X_SWAP = [(0, 3), (1, 2), (2, 1), (3, 0)]
CORE_SWAP = [(0, 1), (1, 0)]


def from_y(value, step):
    return lax.ppermute(value, "y", ring(4, step))


def to_x(value, flips):
    return lax.ppermute(value, X, [(i, i ^ (flips >> 1) ^ ((flips & 1) << 1)) for i in range(4)])


def to_y(value, step):
    return lax.ppermute(value, "y", ring(4, -step))


def local(particles, rot_center, shifts, references, class_prior, sigma2):
    x_lo, y, z = lax.axis_index("x_lo"), lax.axis_index("y"), lax.axis_index("z")
    x_hi, core = lax.axis_index("x_hi"), lax.axis_index("core")
    refs = jnp.transpose(references, (1, 0, 2)).reshape(ROWS, WIDE)

    with jax.named_scope("references"):
        quarter = lax.dynamic_slice_in_dim(refs, DIRECT + y * QUART, QUART, 1)
        crossed = lax.ppermute(quarter, X, X_SWAP)
        direct, crossed = lax.optimization_barrier((refs[:, :DIRECT], crossed))
        direct = lax.ppermute(direct, X, X_SWAP)
        quarters = [crossed] + [from_y(crossed, s) for s in (1, 2, 3)]

    with jax.named_scope("swap"):
        raw = lax.ppermute(particles, "core", CORE_SWAP)
        rot_oth = lax.ppermute(rot_center, "core", CORE_SWAP)
        shifts_oth = lax.ppermute(shifts, "core", CORE_SWAP)
    with jax.named_scope("shift"):
        own = shift_particles(particles, shifts)
        raw, crossed = lax.optimization_barrier((raw, crossed))
        oth = shift_particles(raw, shifts_oth)
    rot = jnp.concatenate([jnp.pad(r, (0, PAD - NP)) for r in (rot_center, rot_oth)]).reshape(1, NP2)

    inv = (1.0 / jnp.concatenate([sigma2, sigma2])).reshape(1, WIDE)
    log_prior = jnp.log(class_prior).reshape(2, 2, 8)
    own_bias = jnp.tile(log_prior[x_hi, core], ROTS).reshape(ROWS, 1)
    oth_bias = jnp.tile(log_prior[1 - x_hi, core], ROTS).reshape(ROWS, 1)

    raised = jax.ShapeDtypeStruct((LANES, ROWS, 128), F32)
    stats = jax.ShapeDtypeStruct((8, NP2), F32)
    with jax.named_scope("scores"):
        weighted, first, first_stats = pl.pallas_call(
            own_kernel,
            out_shape=[jax.ShapeDtypeStruct((NP2, WIDE), BF), raised, stats],
            in_specs=[VMEM] * 6,
            out_specs=[VMEM] * 3,
            scratch_shapes=[pltpu.VMEM((LANES, ROWS, 128), F32)],
            cost_estimate=cost(7),
            compiler_params=pltpu.CompilerParams(vmem_limit_bytes=24 * MB),
        )(own, oth, inv, own_bias, refs, rot)
        offsets = jnp.stack([DIRECT + ((y + s) & 3) * QUART for s in range(4)])
        second, mine = pl.pallas_call(
            other_kernel,
            out_shape=[raised, stats],
            in_specs=[SMEM] + [VMEM] * 10,
            out_specs=[VMEM] * 2,
            scratch_shapes=[pltpu.VMEM((LANES, ROWS, 128), F32)],
            cost_estimate=cost(5),
            compiler_params=pltpu.CompilerParams(vmem_limit_bytes=16 * MB),
        )(offsets, weighted, inv, oth_bias, rot, first_stats, direct, *quarters)
        theirs = lax.ppermute(mine, "core", CORE_SWAP)

    with jax.named_scope("sums"):
        parts = pl.pallas_call(
            sums_kernel,
            out_shape=[jax.ShapeDtypeStruct((4, 8, PROWS, 128), BF)] * 16,
            in_specs=[SMEM] + [VMEM] * 6,
            out_specs=[VMEM] * 16,
            scratch_shapes=[
                pltpu.VMEM((ROTS * 16, NP2), BF),
                pltpu.VMEM((WIDE // 128, ROTS * 16, 128), F32),
                pltpu.VMEM((ROTS * 16, 128), F32),
                pltpu.VMEM((16, 128), F32),
            ],
            cost_estimate=cost(6),
            compiler_params=pltpu.CompilerParams(vmem_limit_bytes=28 * MB),
        )(jnp.stack([x_hi, x_lo, y]), first, second, mine, theirs, own, oth)

    order = (3, 1, 2)
    sends = (to_x, to_y)
    firsts = [None] * 4
    with jax.named_scope("reduce1"):
        arrived = [[parts[4 * n]] for n in range(4)]
        for chunk in range(2):
            for s in order:
                for n in (2 * chunk, 2 * chunk + 1):
                    arrived[n].append(sends[n % 2](parts[4 * n + s], s))
        for n in range(4):
            firsts[n] = pl.pallas_call(
                first_sum_kernel,
                out_shape=[jax.ShapeDtypeStruct((8, PROWS, 128), F32)] * 4,
                in_specs=[VMEM] * 4,
                out_specs=[VMEM] * 4,
                compiler_params=pltpu.CompilerParams(vmem_limit_bytes=8 * MB),
            )(*arrived[n])
    chunks = []
    with jax.named_scope("reduce2"):
        for chunk in range(2):
            pieces = []
            for n in (2 * chunk, 2 * chunk + 1):
                pieces += [firsts[n][0]] + [sends[1 - n % 2](firsts[n][s], s) for s in order]
            both = pl.pallas_call(
                second_sum_kernel,
                out_shape=jax.ShapeDtypeStruct((8, 2 * PROWS, 128), F32),
                in_specs=[VMEM] * 8,
                out_specs=VMEM,
                compiler_params=pltpu.CompilerParams(vmem_limit_bytes=8 * MB),
            )(*pieces)
            chunks.append(lax.all_to_all(both, "z", 0, 0))

    with jax.named_scope("means"):
        d = (x_lo * 4 + y) * 8 + z
        return pl.pallas_call(
            final_kernel,
            out_shape=jax.ShapeDtypeStruct((8, 1920), F32),
            in_specs=[SMEM] + [VMEM] * 3,
            out_specs=VMEM,
            compiler_params=pltpu.CompilerParams(vmem_limit_bytes=8 * MB),
        )(d.reshape(1), sigma2.reshape(16, 128), *chunks)


def solution(mesh):
    fine = Mesh(mesh.devices.reshape(2, 4, 8, 2, 2), ("x_lo", "y", "z", "x_hi", "core"))
    dom, grp = ("x_lo", "y", "z"), ("x_hi", "core")
    return jax.shard_map(
        local,
        mesh=fine,
        in_specs=(P(dom + grp, None), P(dom + grp), P(None, dom + grp), P(grp, None, None), P(), P()),
        out_specs=P(grp, dom),
        check_vma=False,
    )
```

```python
import functools

import jax
import jax.numpy as jnp
from jax import lax
from jax.experimental import pallas as pl
from jax.experimental.pallas import tpu as pltpu
from jax.sharding import Mesh, PartitionSpec as P

HALFWIN = 6
BOX = 128
KXW = 32
KYW = 64
TWO_PI = 6.283185307179586
REG_WEIGHT = 0.05

F = 2048
WIDE = 2 * F
ROTS = 30
ROWS = ROTS * 8
NP = 448
PAD = 512
NP2 = 2 * PAD
LANES = NP2 // 128
DIRECT = 1024
QUART = 512
ZBASE = DIRECT + 4 * QUART
UNITS = 15
PART = 8
PROWS = PART * 8

BF = jnp.bfloat16
F32 = jnp.float32
MB = 1024 * 1024


def turn_cos_sin(turns):
    quarter = jnp.floor(4.0 * turns + 0.5)
    x = TWO_PI * (turns - 0.25 * quarter)
    q = quarter - 4.0 * jnp.floor(0.25 * quarter)
    x2 = x * x
    s = x * (1.0 + x2 * (-1.0 / 6 + x2 * (1.0 / 120 + x2 * (-1.0 / 5040 + x2 * (1.0 / 362880)))))
    c = 1.0 + x2 * (-0.5 + x2 * (1.0 / 24 + x2 * (-1.0 / 720 + x2 * (1.0 / 40320))))
    odd = (q == 1.0) | (q == 3.0)
    cos = jnp.where(odd, s, c)
    sin = jnp.where(odd, c, s)
    cos = jnp.where((q == 1.0) | (q == 2.0), -cos, cos)
    sin = jnp.where(q >= 2.0, -sin, sin)
    return cos, sin


def shift_kernel(sh_ref, p_ref, o_ref):
    rows = p_ref.shape[0]
    lane = lax.broadcasted_iota(jnp.int32, (rows, 128), 1)
    kx = (lane & (KXW - 1)).astype(F32)
    ky = ((lane >> 5) - KYW // 2).astype(F32)
    sx = sh_ref[:, 0:1]
    sy = sh_ref[:, 1:2]
    c, s = turn_cos_sin((sx * kx + sy * ky) * (1.0 / BOX))
    step = jnp.broadcast_to(sy * (128 // KXW), (rows, 128)) * (1.0 / BOX)
    dc, ds = turn_cos_sin(step)
    for b in range(F // 128):
        re = p_ref[:, b * 128 : (b + 1) * 128].astype(F32)
        im = p_ref[:, F + b * 128 : F + (b + 1) * 128].astype(F32)
        o_ref[:, b * 128 : (b + 1) * 128] = (re * c + im * s).astype(BF)
        o_ref[:, F + b * 128 : F + (b + 1) * 128] = (im * c - re * s).astype(BF)
        c, s = c * dc - s * ds, s * dc + c * ds


def shift_particles(particles, shifts):
    block = 64
    return pl.pallas_call(
        shift_kernel,
        grid=(NP // block,),
        out_shape=jax.ShapeDtypeStruct((NP, WIDE), BF),
        in_specs=[
            pl.BlockSpec((block, 2), lambda i: (i, 0)),
            pl.BlockSpec((block, WIDE), lambda i: (i, 0)),
        ],
        out_specs=pl.BlockSpec((block, WIDE), lambda i: (i, 0)),
        cost_estimate=cost(5),
            compiler_params=pltpu.CompilerParams(vmem_limit_bytes=8 * MB),
    )(shifts.T.astype(F32), particles)


def weigh(own_ref, oth_ref, inv_ref, w_ref):
    width = 512
    for start in range(0, WIDE, width):
        cols = slice(start, start + width)
        inv = inv_ref[:, cols]
        w_ref[0:NP, cols] = (own_ref[:, cols].astype(F32) * inv).astype(BF)
        w_ref[PAD : PAD + NP, cols] = (oth_ref[:, cols].astype(F32) * inv).astype(BF)
        w_ref[NP:PAD, cols] = jnp.zeros((PAD - NP, width), BF)
        w_ref[PAD + NP :, cols] = jnp.zeros((PAD - NP, width), BF)


def correlate(w_ref, inv_ref, bias_ref, pieces, acc_ref):
    energy = jnp.zeros((ROWS, 128), F32)
    first = True
    for piece, base, width in pieces:
        for start in range(0, piece.shape[1], width):
            cols = pl.ds(base + start, width)
            inv = inv_ref[:, cols]
            part = lax.dot_general(
                piece[:, start : start + width],
                w_ref[:, cols],
                (((1,), (1,)), ((), ())),
                preferred_element_type=F32,
            )
            for j in range(LANES):
                block = part[:, j * 128 : (j + 1) * 128]
                acc_ref[j] = block if first else acc_ref[j] + block
            first = False
            for lanes in range(0, width, 128):
                v = piece[:, start + lanes : start + lanes + 128].astype(F32)
                energy = energy + v * v * inv[:, lanes : lanes + 128]
    return bias_ref[...] - 0.5 * jnp.sum(energy, axis=1, keepdims=True)


def exponentiate(acc_ref, bias, rot_ref, out_ref, j):
    rot = rot_ref[:, j * 128 : (j + 1) * 128]
    low = jnp.full((8, 128), -jnp.inf, F32)
    top = low
    for r in range(ROTS):
        rows = slice(r * 8, r * 8 + 8)
        score = jnp.where(inside_window(r, rot), acc_ref[j, rows, :] + bias[rows, :], low)
        out_ref[j, rows, :] = score
        top = jnp.maximum(top, score)
    top = jnp.max(top, axis=0, keepdims=True)
    mass = jnp.zeros((8, 128), F32)
    for r in range(ROTS):
        rows = slice(r * 8, r * 8 + 8)
        raised = jnp.exp(out_ref[j, rows, :] - top)
        out_ref[j, rows, :] = raised
        mass = mass + raised
    return top, jnp.sum(mass, axis=0, keepdims=True)


def inside_window(rotation, rot):
    return jnp.abs(jnp.abs(rotation - rot) - ROTS // 2) >= ROTS // 2 - HALFWIN


def own_kernel(own_ref, oth_ref, inv_ref, bias_ref, refs_ref, rot_ref, w_ref, e_ref, stats_ref, acc_ref):
    weigh(own_ref, oth_ref, inv_ref, w_ref)
    bias = correlate(w_ref, inv_ref, bias_ref, [(refs_ref, 0, 512)], acc_ref)
    row = lax.broadcasted_iota(jnp.int32, (8, 128), 0)
    for j in range(LANES):
        top, mass = exponentiate(acc_ref, bias, rot_ref, e_ref, j)
        stats_ref[:, j * 128 : (j + 1) * 128] = jnp.where(row == 0, top, mass)


def other_kernel(
    where_ref, w_ref, inv_ref, bias_ref, rot_ref, first_ref, d_ref, q0, z0, q1, q2, q3, z1,
    e_ref, stats_ref, acc_ref,
):
    pieces = [(d_ref, 0, 512)]
    for s, q in enumerate((q0, z0, q1, q2, q3, z1)):
        pieces.append((q, pl.multiple_of(where_ref[s], 128), QUART))
    bias = correlate(w_ref, inv_ref, bias_ref, pieces, acc_ref)
    row = lax.broadcasted_iota(jnp.int32, (8, 128), 0)
    for j in range(LANES):
        lanes = slice(j * 128, (j + 1) * 128)
        top_b, mass_b = exponentiate(acc_ref, bias, rot_ref, e_ref, j)
        top_a, mass_a = first_ref[0:1, lanes], first_ref[1:2, lanes]
        top = jnp.maximum(top_a, top_b)
        mass = mass_a * jnp.exp(top_a - top) + mass_b * jnp.exp(top_b - top)
        tops = jnp.where(row == 2, top_a, top_b)
        stats_ref[:, lanes] = jnp.where(row == 0, top, jnp.where(row == 1, mass, tops))


def sums_kernel(where_ref, first_ref, second_ref, mine_ref, theirs_ref, own_ref, oth_ref, *refs):
    parts, (p_ref, acc_ref, mass_ref, extra_ref) = refs[:8], refs[8:]
    x_hi, x_lo, y = where_ref[0], where_ref[1], where_ref[2]
    mass_ref[...] = jnp.zeros_like(mass_ref)
    for j in range(LANES):
        lanes = slice(j * 128, (j + 1) * 128)
        facing = (j + LANES // 2) % LANES
        crossed = slice(facing * 128, (facing + 1) * 128)
        top_a, mass_a = mine_ref[0:1, lanes], mine_ref[1:2, lanes]
        top_b, mass_b = theirs_ref[0:1, crossed], theirs_ref[1:2, crossed]
        top = jnp.maximum(top_a, top_b)
        scale = 1.0 / (mass_a * jnp.exp(top_a - top) + mass_b * jnp.exp(top_b - top))
        scale_a = jnp.exp(mine_ref[2:3, lanes] - top) * scale
        scale_b = jnp.exp(mine_ref[3:4, lanes] - top) * scale
        if j % (LANES // 2) == LANES // 2 - 1:
            used = lax.broadcasted_iota(jnp.int32, (1, 128), 1) < 128 - (PAD - NP)
            scale_a = jnp.where(used, scale_a, 0.0)
            scale_b = jnp.where(used, scale_b, 0.0)
        for r in range(ROTS):
            rows = slice(r * 8, r * 8 + 8)
            p = first_ref[j, rows, :] * scale_a
            q = second_ref[j, rows, :] * scale_b
            low = jnp.where(x_hi == 0, p, q)
            high = jnp.where(x_hi == 0, q, p)
            both = jnp.concatenate([low, high], axis=0)
            p_ref[r * 16 : (r + 1) * 16, lanes] = both.astype(BF)
            mass_ref[r * 16 : (r + 1) * 16, :] += both
    lane = lax.broadcasted_iota(jnp.int32, (16, 128), 1)
    totals = jnp.zeros((16, 128), F32)
    for r in range(ROTS):
        row_sum = jnp.sum(mass_ref[r * 16 : (r + 1) * 16, :], axis=1, keepdims=True)
        totals = jnp.where(lane == r, row_sum, totals)
    coarse = totals.astype(BF).astype(F32)
    extra_ref[...] = jnp.where(lane < 32, coarse, pltpu.roll(totals - coarse, 32, 1))
    width = 512
    for cb in range(WIDE // width):
        cols = slice(cb * width, (cb + 1) * width)
        part = jnp.dot(p_ref[:, 0:NP], own_ref[:, cols], preferred_element_type=F32) + jnp.dot(
            p_ref[:, PAD : PAD + NP], oth_ref[:, cols], preferred_element_type=F32
        )
        for j in range(width // 128):
            fb = cb * (width // 128) + j
            for r in range(ROTS):
                for kx in range(2):
                    row = r * 16 + kx * 8
                    acc_ref[kx, 32 * r + fb] = part[row : row + 8, j * 128 : (j + 1) * 128]

    def place(dest_z, carry):
        for sx in range(4):
            kx, dest_x = x_hi ^ (sx >> 1), x_lo ^ (sx & 1)
            for sy in range(4):
                base = ((dest_x * 4 + ((y + sy) & 3)) * 8 + dest_z) * UNITS

                def tile(i):
                    if i == UNITS:
                        return extra_ref[pl.ds(pl.multiple_of(kx * 8, 8), 8), :]
                    return acc_ref[kx, base + i]

                for i in range(0, UNITS + 1, 2):
                    both = jnp.concatenate([tile(i), tile(i + 1)], axis=0).astype(BF)
                    number = i // PART
                    hop, rest = (sx, sy) if number % 2 == 0 else (sy, sx)
                    row = (i % PART) * 8
                    parts[number * 4 + hop][rest, dest_z, row : row + 16, :] = both
        return carry

    lax.fori_loop(0, 8, place, 0)


def first_sum_kernel(*refs):
    for rest, out_ref in enumerate(refs[4:]):
        for z in range(8):
            total = refs[0][rest, z].astype(F32)
            for ref in refs[1:4]:
                total = total + ref[rest, z].astype(F32)
            out_ref[z] = total


def second_sum_kernel(*refs):
    out_ref = refs[8]
    for half in range(2):
        for z in range(8):
            total = refs[4 * half][z]
            for ref in refs[4 * half + 1 : 4 * half + 4]:
                total = total + ref[z]
            out_ref[z, half * PROWS : (half + 1) * PROWS, :] = total


def final_kernel(where_ref, sigma_ref, *refs):
    d = where_ref[0]
    out_ref = refs[1]

    def rows_of(i):
        ref, row = refs[i // (2 * PART)], (i % (2 * PART)) * 8
        total = ref[0, row : row + 8, :]
        for source in range(1, 8):
            total = total + ref[source, row : row + 8, :]
        return total

    mass = rows_of(UNITS)
    mass = mass + pltpu.roll(mass, 128 - 32, 1)
    lane = lax.broadcasted_iota(jnp.int32, (8, 128), 1)
    for i in range(UNITS):
        unit = d * UNITS + i
        rotation = unit >> 5
        here = jnp.sum(jnp.where(lane == rotation, mass, 0.0), axis=1, keepdims=True)
        noise = sigma_ref[pl.ds(unit & 15, 1), :]
        out_ref[:, i * 128 : (i + 1) * 128] = rows_of(i) / (here + REG_WEIGHT * noise)


def cost(micros):
    return pl.CostEstimate(flops=int(micros * 1e9), bytes_accessed=0, transcendentals=0)


SMEM = pl.BlockSpec(memory_space=pltpu.SMEM)
VMEM = pl.BlockSpec(memory_space=pltpu.VMEM)


def ring(size, step):
    return [((i + step) % size, i) for i in range(size)]


X = ("x_lo", "x_hi")
X_SWAP = [(0, 3), (1, 2), (2, 1), (3, 0)]
CORE_SWAP = [(0, 1), (1, 0)]


def from_y(value, step):
    return lax.ppermute(value, "y", ring(4, step))


def to_x(value, flips):
    return lax.ppermute(value, X, [(i, i ^ (flips >> 1) ^ ((flips & 1) << 1)) for i in range(4)])


def to_y(value, step):
    return lax.ppermute(value, "y", ring(4, -step))


def local(particles, rot_center, shifts, references, class_prior, sigma2):
    x_lo, y, z = lax.axis_index("x_lo"), lax.axis_index("y"), lax.axis_index("z")
    x_hi, core = lax.axis_index("x_hi"), lax.axis_index("core")
    refs = jnp.transpose(references, (1, 0, 2)).reshape(ROWS, WIDE)

    with jax.named_scope("swap"):
        raw = lax.ppermute(particles, "core", CORE_SWAP)
        rot_oth = lax.ppermute(rot_center, "core", CORE_SWAP)
        shifts_oth = lax.ppermute(shifts, "core", CORE_SWAP)
    with jax.named_scope("references"):
        zp = z & 1
        quarter = lax.dynamic_slice_in_dim(refs, DIRECT + y * QUART, QUART, 1)
        crossed = lax.ppermute(quarter, X, X_SWAP)
        half, rot_oth = lax.optimization_barrier((lax.dynamic_slice_in_dim(refs, ZBASE + zp * QUART, QUART, 1), rot_oth))
        z_crossed = lax.ppermute(half, X, X_SWAP)
        direct, shifts_oth = lax.optimization_barrier((refs[:, :DIRECT], shifts_oth))
        direct = lax.ppermute(direct, X, X_SWAP)
        quarters = [from_y(crossed, s) for s in (1, 2, 3)]
        z_other = lax.ppermute(z_crossed, "z", [(i, i ^ 1) for i in range(8)])
    with jax.named_scope("shift"):
        own = shift_particles(particles, shifts)
        raw, crossed = lax.optimization_barrier((raw, crossed))
        oth = shift_particles(raw, shifts_oth)
    rot = jnp.concatenate([jnp.pad(r, (0, PAD - NP)) for r in (rot_center, rot_oth)]).reshape(1, NP2)

    inv = (1.0 / jnp.concatenate([sigma2, sigma2])).reshape(1, WIDE)
    log_prior = jnp.log(class_prior).reshape(2, 2, 8)
    own_bias = jnp.tile(log_prior[x_hi, core], ROTS).reshape(ROWS, 1)
    oth_bias = jnp.tile(log_prior[1 - x_hi, core], ROTS).reshape(ROWS, 1)

    raised = jax.ShapeDtypeStruct((LANES, ROWS, 128), F32)
    stats = jax.ShapeDtypeStruct((8, NP2), F32)
    with jax.named_scope("scores"):
        weighted, first, first_stats = pl.pallas_call(
            own_kernel,
            out_shape=[jax.ShapeDtypeStruct((NP2, WIDE), BF), raised, stats],
            in_specs=[VMEM] * 6,
            out_specs=[VMEM] * 3,
            scratch_shapes=[pltpu.VMEM((LANES, ROWS, 128), F32)],
            cost_estimate=cost(7),
            compiler_params=pltpu.CompilerParams(vmem_limit_bytes=24 * MB),
        )(own, oth, inv, own_bias, refs, rot)
        offsets = [DIRECT + ((y + s) & 3) * QUART for s in range(4)]
        offsets = jnp.stack([offsets[0], ZBASE + zp * QUART] + offsets[1:] + [ZBASE + (1 - zp) * QUART])
        second, mine = pl.pallas_call(
            other_kernel,
            out_shape=[raised, stats],
            in_specs=[SMEM] + [VMEM] * 12,
            out_specs=[VMEM] * 2,
            scratch_shapes=[pltpu.VMEM((LANES, ROWS, 128), F32)],
            cost_estimate=cost(5),
            compiler_params=pltpu.CompilerParams(vmem_limit_bytes=16 * MB),
        )(offsets, weighted, inv, oth_bias, rot, first_stats, direct, crossed, z_crossed, *quarters, z_other)
        theirs = lax.ppermute(mine, "core", CORE_SWAP)

    with jax.named_scope("sums"):
        parts = pl.pallas_call(
            sums_kernel,
            out_shape=[jax.ShapeDtypeStruct((4, 8, PROWS, 128), BF)] * 8,
            in_specs=[SMEM] + [VMEM] * 6,
            out_specs=[VMEM] * 8,
            scratch_shapes=[
                pltpu.VMEM((ROTS * 16, NP2), BF),
                pltpu.VMEM((2, ROTS * WIDE // 128, 8, 128), F32),
                pltpu.VMEM((ROTS * 16, 128), F32),
                pltpu.VMEM((16, 128), F32),
            ],
            cost_estimate=cost(6),
            compiler_params=pltpu.CompilerParams(vmem_limit_bytes=28 * MB),
        )(jnp.stack([x_hi, x_lo, y]), first, second, mine, theirs, own, oth)

    order = (3, 1, 2)
    sends = (to_x, to_y)
    with jax.named_scope("reduce1"):
        arrived = [[parts[0]], [parts[4]]]
        for s in order:
            for n in range(2):
                arrived[n].append(sends[n](parts[4 * n + s], s))
        firsts = [
            pl.pallas_call(
                first_sum_kernel,
                out_shape=[jax.ShapeDtypeStruct((8, PROWS, 128), F32)] * 4,
                in_specs=[VMEM] * 4,
                out_specs=[VMEM] * 4,
                compiler_params=pltpu.CompilerParams(vmem_limit_bytes=8 * MB),
            )(*arrived[n])
            for n in range(2)
        ]
    with jax.named_scope("reduce2"):
        pieces = [[firsts[0][0]], [firsts[1][0]]]
        for s in order:
            for n in range(2):
                pieces[n].append(sends[1 - n](firsts[n][s], s))
        both = pl.pallas_call(
            second_sum_kernel,
            out_shape=jax.ShapeDtypeStruct((8, 2 * PROWS, 128), F32),
            in_specs=[VMEM] * 8,
            out_specs=VMEM,
            compiler_params=pltpu.CompilerParams(vmem_limit_bytes=8 * MB),
        )(*pieces[0], *pieces[1])
    with jax.named_scope("reduce3"):
        owned = lax.all_to_all(both, "z", 0, 0)

    with jax.named_scope("means"):
        d = (x_lo * 4 + y) * 8 + z
        return pl.pallas_call(
            final_kernel,
            out_shape=jax.ShapeDtypeStruct((8, 1920), F32),
            in_specs=[SMEM] + [VMEM] * 2,
            out_specs=VMEM,
            compiler_params=pltpu.CompilerParams(vmem_limit_bytes=8 * MB),
        )(d.reshape(1), sigma2.reshape(16, 128), owned)


def solution(mesh):
    fine = Mesh(mesh.devices.reshape(2, 4, 8, 2, 2), ("x_lo", "y", "z", "x_hi", "core"))
    dom, grp = ("x_lo", "y", "z"), ("x_hi", "core")
    return jax.shard_map(
        local,
        mesh=fine,
        in_specs=(P(dom + grp, None), P(dom + grp), P(None, dom + grp), P(grp, None, None), P(), P()),
        out_specs=P(grp, dom),
        check_vma=False,
    )
```

```python
import functools

import jax
import jax.numpy as jnp
from jax import lax
from jax.experimental import pallas as pl
from jax.experimental.pallas import tpu as pltpu
from jax.sharding import Mesh, PartitionSpec as P

HALFWIN = 6
BOX = 128
KXW = 32
KYW = 64
TWO_PI = 6.283185307179586
REG_WEIGHT = 0.05

F = 2048
WIDE = 2 * F
ROTS = 30
ROWS = ROTS * 8
NP = 448
PAD = 512
NP2 = 2 * PAD
LANES = NP2 // 128
DIRECT = 1024
QUART = 512
ZBASE = DIRECT + 4 * QUART
UNITS = 15
PART = 8
PROWS = PART * 8

BF = jnp.bfloat16
F32 = jnp.float32
MB = 1024 * 1024


def turn_cos_sin(turns):
    quarter = jnp.floor(4.0 * turns + 0.5)
    x = TWO_PI * (turns - 0.25 * quarter)
    q = quarter - 4.0 * jnp.floor(0.25 * quarter)
    x2 = x * x
    s = x * (1.0 + x2 * (-1.0 / 6 + x2 * (1.0 / 120 + x2 * (-1.0 / 5040 + x2 * (1.0 / 362880)))))
    c = 1.0 + x2 * (-0.5 + x2 * (1.0 / 24 + x2 * (-1.0 / 720 + x2 * (1.0 / 40320))))
    odd = (q == 1.0) | (q == 3.0)
    cos = jnp.where(odd, s, c)
    sin = jnp.where(odd, c, s)
    cos = jnp.where((q == 1.0) | (q == 2.0), -cos, cos)
    sin = jnp.where(q >= 2.0, -sin, sin)
    return cos, sin


def shift_kernel(meta_ref, p_ref, o_ref, turned_ref):
    rows = p_ref.shape[0]
    step = pl.program_id(0)

    @pl.when(step == 0)
    def _():
        turned_ref[...] = jnp.transpose(meta_ref[...])

    shifts = turned_ref[pl.ds(pl.multiple_of(step * rows, rows), rows), :]
    lane = lax.broadcasted_iota(jnp.int32, (rows, 128), 1)
    kx = (lane & (KXW - 1)).astype(F32)
    ky = ((lane >> 5) - KYW // 2).astype(F32)
    sx = shifts[:, 0:1]
    sy = shifts[:, 1:2]
    c, s = turn_cos_sin((sx * kx + sy * ky) * (1.0 / BOX))
    dc, ds = turn_cos_sin(jnp.broadcast_to(sy * (128 // KXW), (rows, 128)) * (1.0 / BOX))
    for b in range(F // 128):
        re = p_ref[:, b * 128 : (b + 1) * 128].astype(F32)
        im = p_ref[:, F + b * 128 : F + (b + 1) * 128].astype(F32)
        o_ref[:, b * 128 : (b + 1) * 128] = (re * c + im * s).astype(BF)
        o_ref[:, F + b * 128 : F + (b + 1) * 128] = (im * c - re * s).astype(BF)
        c, s = c * dc - s * ds, s * dc + c * ds


def shift_particles(particles, meta):
    block = 64
    return pl.pallas_call(
        shift_kernel,
        grid=(NP // block,),
        out_shape=jax.ShapeDtypeStruct((NP, WIDE), BF),
        in_specs=[
            pl.BlockSpec((8, PAD), lambda i: (0, 0)),
            pl.BlockSpec((block, WIDE), lambda i: (i, 0)),
        ],
        out_specs=pl.BlockSpec((block, WIDE), lambda i: (i, 0)),
        scratch_shapes=[pltpu.VMEM((PAD, 8), F32)],
        cost_estimate=cost(5),
            compiler_params=pltpu.CompilerParams(vmem_limit_bytes=8 * MB),
    )(meta, particles)


def weigh(own_ref, oth_ref, inv_ref, w_ref):
    width = 512
    for start in range(0, WIDE, width):
        cols = slice(start, start + width)
        inv = inv_ref[:, cols]
        w_ref[0:NP, cols] = (own_ref[:, cols].astype(F32) * inv).astype(BF)
        w_ref[PAD : PAD + NP, cols] = (oth_ref[:, cols].astype(F32) * inv).astype(BF)
        w_ref[NP:PAD, cols] = jnp.zeros((PAD - NP, width), BF)
        w_ref[PAD + NP :, cols] = jnp.zeros((PAD - NP, width), BF)


def correlate(w_ref, inv_ref, bias_ref, pieces, acc_ref):
    energy = jnp.zeros((ROWS, 128), F32)
    first = True
    for piece, base, width in pieces:
        for start in range(0, piece.shape[1], width):
            cols = pl.ds(base + start, width)
            inv = inv_ref[:, cols]
            part = lax.dot_general(
                piece[:, start : start + width],
                w_ref[:, cols],
                (((1,), (1,)), ((), ())),
                preferred_element_type=F32,
            )
            for j in range(LANES):
                block = part[:, j * 128 : (j + 1) * 128]
                acc_ref[j] = block if first else acc_ref[j] + block
            first = False
            for lanes in range(0, width, 128):
                v = piece[:, start + lanes : start + lanes + 128].astype(F32)
                energy = energy + v * v * inv[:, lanes : lanes + 128]
    return bias_ref[...] - 0.5 * jnp.sum(energy, axis=1, keepdims=True)


def exponentiate(acc_ref, bias, metas, out_ref, j):
    half = LANES // 2
    rot = metas[j // half][2:3, (j % half) * 128 : (j % half + 1) * 128]
    low = jnp.full((8, 128), -jnp.inf, F32)
    top = low
    for r in range(ROTS):
        rows = slice(r * 8, r * 8 + 8)
        score = jnp.where(inside_window(r, rot), acc_ref[j, rows, :] + bias[rows, :], low)
        out_ref[j, rows, :] = score
        top = jnp.maximum(top, score)
    top = jnp.max(top, axis=0, keepdims=True)
    mass = jnp.zeros((8, 128), F32)
    for r in range(ROTS):
        rows = slice(r * 8, r * 8 + 8)
        raised = jnp.exp(out_ref[j, rows, :] - top)
        out_ref[j, rows, :] = raised
        mass = mass + raised
    return top, jnp.sum(mass, axis=0, keepdims=True)


def inside_window(rotation, rot):
    return jnp.abs(jnp.abs(float(rotation) - rot) - ROTS / 2) >= ROTS / 2 - HALFWIN


def own_kernel(own_ref, oth_ref, inv_ref, bias_ref, refs_ref, meta_a, meta_b, w_ref, e_ref, stats_ref, acc_ref):
    weigh(own_ref, oth_ref, inv_ref, w_ref)
    bias = correlate(w_ref, inv_ref, bias_ref, [(refs_ref, 0, 512)], acc_ref)
    row = lax.broadcasted_iota(jnp.int32, (8, 128), 0)
    for j in range(LANES):
        top, mass = exponentiate(acc_ref, bias, (meta_a, meta_b), e_ref, j)
        stats_ref[:, j * 128 : (j + 1) * 128] = jnp.where(row == 0, top, mass)


def other_kernel(
    where_ref, w_ref, inv_ref, bias_ref, meta_a, meta_b, first_ref, d_ref, q0, z0, q1, q2, q3, z1,
    e_ref, stats_ref, acc_ref,
):
    pieces = [(d_ref, 0, 512)]
    for s, q in enumerate((q0, z0, q1, q2, q3, z1)):
        pieces.append((q, pl.multiple_of(where_ref[s], 128), QUART))
    bias = correlate(w_ref, inv_ref, bias_ref, pieces, acc_ref)
    row = lax.broadcasted_iota(jnp.int32, (8, 128), 0)
    for j in range(LANES):
        lanes = slice(j * 128, (j + 1) * 128)
        top_b, mass_b = exponentiate(acc_ref, bias, (meta_a, meta_b), e_ref, j)
        top_a, mass_a = first_ref[0:1, lanes], first_ref[1:2, lanes]
        top = jnp.maximum(top_a, top_b)
        mass = mass_a * jnp.exp(top_a - top) + mass_b * jnp.exp(top_b - top)
        tops = jnp.where(row == 2, top_a, top_b)
        stats_ref[:, lanes] = jnp.where(row == 0, top, jnp.where(row == 1, mass, tops))


def sums_kernel(where_ref, first_ref, second_ref, mine_ref, theirs_ref, own_ref, oth_ref, *refs):
    parts, (p_ref, acc_ref, mass_ref, extra_ref) = refs[:8], refs[8:]
    x_hi, x_lo, y, z = where_ref[0], where_ref[1], where_ref[2], where_ref[3]
    mass_ref[...] = jnp.zeros_like(mass_ref)
    for j in range(LANES):
        lanes = slice(j * 128, (j + 1) * 128)
        facing = (j + LANES // 2) % LANES
        crossed = slice(facing * 128, (facing + 1) * 128)
        top_a, mass_a = mine_ref[0:1, lanes], mine_ref[1:2, lanes]
        top_b, mass_b = theirs_ref[0:1, crossed], theirs_ref[1:2, crossed]
        top = jnp.maximum(top_a, top_b)
        scale = 1.0 / (mass_a * jnp.exp(top_a - top) + mass_b * jnp.exp(top_b - top))
        scale_a = jnp.exp(mine_ref[2:3, lanes] - top) * scale
        scale_b = jnp.exp(mine_ref[3:4, lanes] - top) * scale
        if j % (LANES // 2) == LANES // 2 - 1:
            used = lax.broadcasted_iota(jnp.int32, (1, 128), 1) < 128 - (PAD - NP)
            scale_a = jnp.where(used, scale_a, 0.0)
            scale_b = jnp.where(used, scale_b, 0.0)
        for r in range(ROTS):
            rows = slice(r * 8, r * 8 + 8)
            p = first_ref[j, rows, :] * scale_a
            q = second_ref[j, rows, :] * scale_b
            low = jnp.where(x_hi == 0, p, q)
            high = jnp.where(x_hi == 0, q, p)
            both = jnp.concatenate([low, high], axis=0)
            p_ref[r * 16 : (r + 1) * 16, lanes] = both.astype(BF)
            mass_ref[r * 16 : (r + 1) * 16, :] += both
    lane = lax.broadcasted_iota(jnp.int32, (16, 128), 1)
    totals = jnp.zeros((16, 128), F32)
    for r in range(ROTS):
        row_sum = jnp.sum(mass_ref[r * 16 : (r + 1) * 16, :], axis=1, keepdims=True)
        totals = jnp.where(lane == r, row_sum, totals)
    coarse = totals.astype(BF).astype(F32)
    extra_ref[...] = jnp.where(lane < 32, coarse, pltpu.roll(totals - coarse, 32, 1))
    width = 512
    for cb in range(WIDE // width):
        cols = slice(cb * width, (cb + 1) * width)
        part = jnp.dot(p_ref[:, 0:NP], own_ref[:, cols], preferred_element_type=F32) + jnp.dot(
            p_ref[:, PAD : PAD + NP], oth_ref[:, cols], preferred_element_type=F32
        )
        for j in range(width // 128):
            fb = cb * (width // 128) + j
            for r in range(ROTS):
                for kx in range(2):
                    row = r * 16 + kx * 8
                    acc_ref[kx, 32 * r + fb] = part[row : row + 8, j * 128 : (j + 1) * 128]

    def place(sz, carry):
        dest_z = (z + sz) & 7
        for sx in range(4):
            kx, dest_x = x_hi ^ (sx >> 1), x_lo ^ (sx & 1)
            for sy in range(4):
                base = ((dest_x * 4 + ((y + sy) & 3)) * 8 + dest_z) * UNITS

                def tile(i):
                    if i == UNITS:
                        return extra_ref[pl.ds(pl.multiple_of(kx * 8, 8), 8), :]
                    return acc_ref[kx, base + i]

                for i in range(0, UNITS + 1, 2):
                    both = jnp.concatenate([tile(i), tile(i + 1)], axis=0).astype(BF)
                    number = i // PART
                    hop, rest = (sx, sy) if number % 2 == 0 else (sy, sx)
                    row = (i % PART) * 8
                    parts[number * 4 + hop][rest, sz, row : row + 16, :] = both
        return carry

    lax.fori_loop(0, 8, place, 0)


def first_sum_kernel(*refs):
    for half in range(2):
        arrived = refs[half:8:2]
        for rest in range(4):
            for z in range(8):
                total = arrived[0][rest, z].astype(F32)
                for ref in arrived[1:]:
                    total = total + ref[rest, z].astype(F32)
                refs[8 + 4 * half + rest][z] = total


def second_sum_kernel(*refs):
    for half in range(2):
        arrived = refs[half:8:2]
        for z in range(8):
            total = arrived[0][z]
            for ref in arrived[1:]:
                total = total + ref[z]
            refs[8 + z][half * PROWS : (half + 1) * PROWS, :] = total


def final_kernel(where_ref, sigma_ref, *refs):
    d = where_ref[0]
    out_ref = refs[8]

    def rows_of(i):
        rows = slice(i * 8, i * 8 + 8)
        total = refs[0][rows, :]
        for ref in refs[1:8]:
            total = total + ref[rows, :]
        return total

    mass = rows_of(UNITS)
    mass = mass + pltpu.roll(mass, 128 - 32, 1)
    lane = lax.broadcasted_iota(jnp.int32, (8, 128), 1)
    for i in range(UNITS):
        unit = d * UNITS + i
        rotation = unit >> 5
        here = jnp.sum(jnp.where(lane == rotation, mass, 0.0), axis=1, keepdims=True)
        noise = sigma_ref[pl.ds(unit & 15, 1), :]
        out_ref[:, i * 128 : (i + 1) * 128] = rows_of(i) / (here + REG_WEIGHT * noise)


def cost(micros):
    return pl.CostEstimate(flops=int(micros * 1e9), bytes_accessed=0, transcendentals=0)


SMEM = pl.BlockSpec(memory_space=pltpu.SMEM)
VMEM = pl.BlockSpec(memory_space=pltpu.VMEM)


def ring(size, step):
    return [((i + step) % size, i) for i in range(size)]


X = ("x_lo", "x_hi")
X_SWAP = [(0, 3), (1, 2), (2, 1), (3, 0)]
CORE_SWAP = [(0, 1), (1, 0)]


def from_y(value, step):
    return lax.ppermute(value, "y", ring(4, step))


def to_x(value, flips):
    return lax.ppermute(value, X, [(i, i ^ (flips >> 1) ^ ((flips & 1) << 1)) for i in range(4)])


def to_y(value, step):
    return lax.ppermute(value, "y", ring(4, -step))


def to_z(value, step):
    return lax.ppermute(value, "z", ring(8, -step))


def local(particles, rot_center, shifts, references, class_prior, sigma2):
    x_lo, y, z = lax.axis_index("x_lo"), lax.axis_index("y"), lax.axis_index("z")
    x_hi, core = lax.axis_index("x_hi"), lax.axis_index("core")
    refs = jnp.transpose(references, (1, 0, 2)).reshape(ROWS, WIDE)

    zp = z & 1
    with jax.named_scope("swap"):
        raw = lax.ppermute(particles, "core", CORE_SWAP)
    with jax.named_scope("references"):
        quarter = lax.dynamic_slice_in_dim(refs, DIRECT + y * QUART, QUART, 1)
        quarter, shifts, rot_center = lax.optimization_barrier((quarter, shifts, rot_center))
        crossed = lax.ppermute(quarter, X, X_SWAP)
    with jax.named_scope("swap"):
        meta = jnp.concatenate([shifts, rot_center[None]]).astype(F32)
        meta = jnp.pad(meta, ((0, 5), (0, PAD - NP)))
        meta_oth = lax.ppermute(meta, "core", CORE_SWAP)
    with jax.named_scope("references"):
        half = lax.dynamic_slice_in_dim(refs, ZBASE + zp * QUART, QUART, 1)
        half, meta_oth = lax.optimization_barrier((half, meta_oth))
        z_crossed = lax.ppermute(half, X, X_SWAP)
        direct, meta_oth = lax.optimization_barrier((refs[:, :DIRECT], meta_oth))
        direct = lax.ppermute(direct, X, X_SWAP)
    with jax.named_scope("shift"):
        own = shift_particles(particles, meta)
        raw, crossed = lax.optimization_barrier((raw, crossed))
        oth = shift_particles(raw, meta_oth)
    with jax.named_scope("references"):
        quarters = [from_y(crossed, s) for s in (1, 2, 3)]
        z_crossed, oth = lax.optimization_barrier((z_crossed, oth))
        z_other = lax.ppermute(z_crossed, "z", [(i, i ^ 1) for i in range(8)])
    inv = (1.0 / jnp.concatenate([sigma2, sigma2])).reshape(1, WIDE)
    log_prior = jnp.log(class_prior).reshape(2, 2, 8)
    own_bias = jnp.tile(log_prior[x_hi, core], ROTS).reshape(ROWS, 1)
    oth_bias = jnp.tile(log_prior[1 - x_hi, core], ROTS).reshape(ROWS, 1)

    raised = jax.ShapeDtypeStruct((LANES, ROWS, 128), F32)
    stats = jax.ShapeDtypeStruct((8, NP2), F32)
    with jax.named_scope("scores"):
        weighted, first, first_stats = pl.pallas_call(
            own_kernel,
            out_shape=[jax.ShapeDtypeStruct((NP2, WIDE), BF), raised, stats],
            in_specs=[VMEM] * 7,
            out_specs=[VMEM] * 3,
            scratch_shapes=[pltpu.VMEM((LANES, ROWS, 128), F32)],
            cost_estimate=cost(7),
            compiler_params=pltpu.CompilerParams(vmem_limit_bytes=24 * MB),
        )(own, oth, inv, own_bias, refs, meta, meta_oth)
        offsets = [DIRECT + ((y + s) & 3) * QUART for s in range(4)]
        offsets = jnp.stack([offsets[0], ZBASE + zp * QUART] + offsets[1:] + [ZBASE + (1 - zp) * QUART])
        second, mine = pl.pallas_call(
            other_kernel,
            out_shape=[raised, stats],
            in_specs=[SMEM] + [VMEM] * 13,
            out_specs=[VMEM] * 2,
            scratch_shapes=[pltpu.VMEM((LANES, ROWS, 128), F32)],
            cost_estimate=cost(5),
            compiler_params=pltpu.CompilerParams(vmem_limit_bytes=16 * MB),
        )(offsets, weighted, inv, oth_bias, meta, meta_oth, first_stats, direct, crossed, z_crossed, *quarters, z_other)
        theirs = lax.ppermute(mine, "core", CORE_SWAP)

    with jax.named_scope("sums"):
        parts = pl.pallas_call(
            sums_kernel,
            out_shape=[jax.ShapeDtypeStruct((4, 8, PROWS, 128), BF)] * 8,
            in_specs=[SMEM] + [VMEM] * 6,
            out_specs=[VMEM] * 8,
            scratch_shapes=[
                pltpu.VMEM((ROTS * 16, NP2), BF),
                pltpu.VMEM((2, ROTS * WIDE // 128, 8, 128), F32),
                pltpu.VMEM((ROTS * 16, 128), F32),
                pltpu.VMEM((16, 128), F32),
            ],
            cost_estimate=cost(6),
            compiler_params=pltpu.CompilerParams(vmem_limit_bytes=28 * MB),
        )(jnp.stack([x_hi, x_lo, y, z]), first, second, mine, theirs, own, oth)

    order = (3, 1, 2)
    sends = (to_x, to_y)
    with jax.named_scope("reduce1"):
        arrived = [[parts[0]], [parts[4]]]
        for s in order:
            for n in range(2):
                arrived[n].append(sends[n](parts[4 * n + s], s))
        firsts = pl.pallas_call(
            first_sum_kernel,
            out_shape=[jax.ShapeDtypeStruct((8, PROWS, 128), F32)] * 8,
            in_specs=[VMEM] * 8,
            out_specs=[VMEM] * 8,
            compiler_params=pltpu.CompilerParams(vmem_limit_bytes=12 * MB),
        )(*[piece for pair in zip(*arrived) for piece in pair])
    with jax.named_scope("reduce2"):
        pieces = [[firsts[0]], [firsts[4]]]
        for s in order:
            for n in range(2):
                pieces[n].append(sends[1 - n](firsts[4 * n + s], s))
        slots = pl.pallas_call(
            second_sum_kernel,
            out_shape=[jax.ShapeDtypeStruct((2 * PROWS, 128), F32)] * 8,
            in_specs=[VMEM] * 8,
            out_specs=[VMEM] * 8,
            compiler_params=pltpu.CompilerParams(vmem_limit_bytes=8 * MB),
        )(*[piece for pair in zip(*pieces) for piece in pair])
    with jax.named_scope("reduce3"):
        owned = [slots[0]] + [to_z(slots[s], s) for s in (4, 3, 5, 2, 6, 1, 7)]

    with jax.named_scope("means"):
        d = (x_lo * 4 + y) * 8 + z
        return pl.pallas_call(
            final_kernel,
            out_shape=jax.ShapeDtypeStruct((8, 1920), F32),
            in_specs=[SMEM] + [VMEM] * 9,
            out_specs=VMEM,
            compiler_params=pltpu.CompilerParams(vmem_limit_bytes=8 * MB),
        )(d.reshape(1), sigma2.reshape(16, 128), *owned)


def solution(mesh):
    fine = Mesh(mesh.devices.reshape(2, 4, 8, 2, 2), ("x_lo", "y", "z", "x_hi", "core"))
    dom, grp = ("x_lo", "y", "z"), ("x_hi", "core")
    return jax.shard_map(
        local,
        mesh=fine,
        in_specs=(P(dom + grp, None), P(dom + grp), P(None, dom + grp), P(grp, None, None), P(), P()),
        out_specs=P(grp, dom),
        check_vma=False,
    )
```

```python
import functools

import jax
import jax.numpy as jnp
from jax import lax
from jax.experimental import pallas as pl
from jax.experimental.pallas import tpu as pltpu
from jax.sharding import Mesh, PartitionSpec as P

HALFWIN = 6
BOX = 128
KXW = 32
KYW = 64
TWO_PI = 6.283185307179586
REG_WEIGHT = 0.05

F = 2048
WIDE = 2 * F
ROTS = 30
ROWS = ROTS * 8
NP = 448
PAD = 512
NP2 = 2 * PAD
LANES = NP2 // 128
DIRECT = 1024
QUART = 512
ZBASE = DIRECT + 4 * QUART
UNITS = 15
PART = 8
PROWS = PART * 8

BF = jnp.bfloat16
F32 = jnp.float32
MB = 1024 * 1024


def turn_cos_sin(turns):
    quarter = jnp.floor(4.0 * turns + 0.5)
    x = TWO_PI * (turns - 0.25 * quarter)
    q = quarter - 4.0 * jnp.floor(0.25 * quarter)
    x2 = x * x
    s = x * (1.0 + x2 * (-1.0 / 6 + x2 * (1.0 / 120 + x2 * (-1.0 / 5040 + x2 * (1.0 / 362880)))))
    c = 1.0 + x2 * (-0.5 + x2 * (1.0 / 24 + x2 * (-1.0 / 720 + x2 * (1.0 / 40320))))
    odd = (q == 1.0) | (q == 3.0)
    cos = jnp.where(odd, s, c)
    sin = jnp.where(odd, c, s)
    cos = jnp.where((q == 1.0) | (q == 2.0), -cos, cos)
    sin = jnp.where(q >= 2.0, -sin, sin)
    return cos, sin


def shift_kernel(meta_ref, p_ref, o_ref, turned_ref):
    rows = p_ref.shape[0]
    step = pl.program_id(0)

    @pl.when(step == 0)
    def _():
        turned_ref[...] = jnp.transpose(meta_ref[...])

    shifts = turned_ref[pl.ds(pl.multiple_of(step * rows, rows), rows), :]
    lane = lax.broadcasted_iota(jnp.int32, (rows, 128), 1)
    kx = (lane & (KXW - 1)).astype(F32)
    ky = ((lane >> 5) - KYW // 2).astype(F32)
    sx = shifts[:, 0:1]
    sy = shifts[:, 1:2]
    c, s = turn_cos_sin((sx * kx + sy * ky) * (1.0 / BOX))
    dc, ds = turn_cos_sin(jnp.broadcast_to(sy * (128 // KXW), (rows, 128)) * (1.0 / BOX))
    for b in range(F // 128):
        re = p_ref[:, b * 128 : (b + 1) * 128].astype(F32)
        im = p_ref[:, F + b * 128 : F + (b + 1) * 128].astype(F32)
        o_ref[:, b * 128 : (b + 1) * 128] = (re * c + im * s).astype(BF)
        o_ref[:, F + b * 128 : F + (b + 1) * 128] = (im * c - re * s).astype(BF)
        c, s = c * dc - s * ds, s * dc + c * ds


def shift_particles(particles, meta):
    block = 64
    return pl.pallas_call(
        shift_kernel,
        grid=(NP // block,),
        out_shape=jax.ShapeDtypeStruct((NP, WIDE), BF),
        in_specs=[
            pl.BlockSpec((8, PAD), lambda i: (0, 0)),
            pl.BlockSpec((block, WIDE), lambda i: (i, 0)),
        ],
        out_specs=pl.BlockSpec((block, WIDE), lambda i: (i, 0)),
        scratch_shapes=[pltpu.VMEM((PAD, 8), F32)],
        cost_estimate=cost(5),
            compiler_params=pltpu.CompilerParams(vmem_limit_bytes=8 * MB),
    )(meta, particles)


def weigh(own_ref, oth_ref, inv_ref, w_ref):
    width = 512
    for start in range(0, WIDE, width):
        cols = slice(start, start + width)
        inv = inv_ref[:, cols]
        w_ref[0:NP, cols] = (own_ref[:, cols].astype(F32) * inv).astype(BF)
        w_ref[PAD : PAD + NP, cols] = (oth_ref[:, cols].astype(F32) * inv).astype(BF)
        w_ref[NP:PAD, cols] = jnp.zeros((PAD - NP, width), BF)
        w_ref[PAD + NP :, cols] = jnp.zeros((PAD - NP, width), BF)


def correlate(w_ref, inv_ref, bias_ref, pieces, acc_ref):
    energy = jnp.zeros((ROWS, 128), F32)
    first = True
    for piece, base, width in pieces:
        for start in range(0, piece.shape[1], width):
            cols = pl.ds(base + start, width)
            inv = inv_ref[:, cols]
            part = lax.dot_general(
                piece[:, start : start + width],
                w_ref[:, cols],
                (((1,), (1,)), ((), ())),
                preferred_element_type=F32,
            )
            for j in range(LANES):
                block = part[:, j * 128 : (j + 1) * 128]
                acc_ref[j] = block if first else acc_ref[j] + block
            first = False
            for lanes in range(0, width, 128):
                v = piece[:, start + lanes : start + lanes + 128].astype(F32)
                energy = energy + v * v * inv[:, lanes : lanes + 128]
    return bias_ref[...] - 0.5 * jnp.sum(energy, axis=1, keepdims=True)


def exponentiate(acc_ref, bias, metas, out_ref, j):
    half = LANES // 2
    rot = metas[j // half][2:3, (j % half) * 128 : (j % half + 1) * 128]
    low = jnp.full((8, 128), -jnp.inf, F32)
    top = low
    for r in range(ROTS):
        rows = slice(r * 8, r * 8 + 8)
        score = jnp.where(inside_window(r, rot), acc_ref[j, rows, :] + bias[rows, :], low)
        out_ref[j, rows, :] = score
        top = jnp.maximum(top, score)
    top = jnp.max(top, axis=0, keepdims=True)
    mass = jnp.zeros((8, 128), F32)
    for r in range(ROTS):
        rows = slice(r * 8, r * 8 + 8)
        raised = jnp.exp(out_ref[j, rows, :] - top)
        out_ref[j, rows, :] = raised
        mass = mass + raised
    return top, jnp.sum(mass, axis=0, keepdims=True)


def inside_window(rotation, rot):
    return jnp.abs(jnp.abs(float(rotation) - rot) - ROTS / 2) >= ROTS / 2 - HALFWIN


def own_kernel(own_ref, oth_ref, inv_ref, bias_ref, refs_ref, meta_a, meta_b, w_ref, e_ref, stats_ref, acc_ref):
    weigh(own_ref, oth_ref, inv_ref, w_ref)
    bias = correlate(w_ref, inv_ref, bias_ref, [(refs_ref, 0, 512)], acc_ref)
    row = lax.broadcasted_iota(jnp.int32, (8, 128), 0)
    for j in range(LANES):
        top, mass = exponentiate(acc_ref, bias, (meta_a, meta_b), e_ref, j)
        stats_ref[:, j * 128 : (j + 1) * 128] = jnp.where(row == 0, top, mass)


def other_kernel(
    where_ref, w_ref, inv_ref, bias_ref, meta_a, meta_b, first_ref, d_ref, q0, z0, q1, q2, q3, z1,
    e_ref, stats_ref, acc_ref,
):
    pieces = [(d_ref, 0, 512)]
    for s, q in enumerate((q0, z0, q1, q2, q3, z1)):
        pieces.append((q, pl.multiple_of(where_ref[s], 128), QUART))
    bias = correlate(w_ref, inv_ref, bias_ref, pieces, acc_ref)
    row = lax.broadcasted_iota(jnp.int32, (8, 128), 0)
    for j in range(LANES):
        lanes = slice(j * 128, (j + 1) * 128)
        top_b, mass_b = exponentiate(acc_ref, bias, (meta_a, meta_b), e_ref, j)
        top_a, mass_a = first_ref[0:1, lanes], first_ref[1:2, lanes]
        top = jnp.maximum(top_a, top_b)
        mass = mass_a * jnp.exp(top_a - top) + mass_b * jnp.exp(top_b - top)
        tops = jnp.where(row == 2, top_a, top_b)
        stats_ref[:, lanes] = jnp.where(row == 0, top, jnp.where(row == 1, mass, tops))


def sums_kernel(where_ref, first_ref, second_ref, mine_ref, theirs_ref, own_ref, oth_ref, *refs):
    parts, (p_ref, acc_ref, mass_ref, extra_ref) = refs[:8], refs[8:]
    x_hi, x_lo, y = where_ref[0], where_ref[1], where_ref[2]
    mass_ref[...] = jnp.zeros_like(mass_ref)
    for j in range(LANES):
        lanes = slice(j * 128, (j + 1) * 128)
        facing = (j + LANES // 2) % LANES
        crossed = slice(facing * 128, (facing + 1) * 128)
        top_a, mass_a = mine_ref[0:1, lanes], mine_ref[1:2, lanes]
        top_b, mass_b = theirs_ref[0:1, crossed], theirs_ref[1:2, crossed]
        top = jnp.maximum(top_a, top_b)
        scale = 1.0 / (mass_a * jnp.exp(top_a - top) + mass_b * jnp.exp(top_b - top))
        scale_a = jnp.exp(mine_ref[2:3, lanes] - top) * scale
        scale_b = jnp.exp(mine_ref[3:4, lanes] - top) * scale
        if j % (LANES // 2) == LANES // 2 - 1:
            used = lax.broadcasted_iota(jnp.int32, (1, 128), 1) < 128 - (PAD - NP)
            scale_a = jnp.where(used, scale_a, 0.0)
            scale_b = jnp.where(used, scale_b, 0.0)
        for r in range(ROTS):
            rows = slice(r * 8, r * 8 + 8)
            p = first_ref[j, rows, :] * scale_a
            q = second_ref[j, rows, :] * scale_b
            low = jnp.where(x_hi == 0, p, q)
            high = jnp.where(x_hi == 0, q, p)
            both = jnp.concatenate([low, high], axis=0)
            p_ref[r * 16 : (r + 1) * 16, lanes] = both.astype(BF)
            mass_ref[r * 16 : (r + 1) * 16, :] += both
    lane = lax.broadcasted_iota(jnp.int32, (16, 128), 1)
    totals = jnp.zeros((16, 128), F32)
    for r in range(ROTS):
        row_sum = jnp.sum(mass_ref[r * 16 : (r + 1) * 16, :], axis=1, keepdims=True)
        totals = jnp.where(lane == r, row_sum, totals)
    coarse = totals.astype(BF).astype(F32)
    extra_ref[...] = jnp.where(lane < 32, coarse, pltpu.roll(totals - coarse, 32, 1))
    width = 512
    for cb in range(WIDE // width):
        cols = slice(cb * width, (cb + 1) * width)
        part = jnp.dot(p_ref[:, 0:NP], own_ref[:, cols], preferred_element_type=F32) + jnp.dot(
            p_ref[:, PAD : PAD + NP], oth_ref[:, cols], preferred_element_type=F32
        )
        for j in range(width // 128):
            fb = cb * (width // 128) + j
            for r in range(ROTS):
                for kx in range(2):
                    row = r * 16 + kx * 8
                    acc_ref[kx, 32 * r + fb] = part[row : row + 8, j * 128 : (j + 1) * 128]

    def place(sz, carry):
        dest_z = where_ref[3 + sz]
        for sx in range(4):
            kx, dest_x = x_hi ^ (sx >> 1), x_lo ^ (sx & 1)
            for sy in range(4):
                base = ((dest_x * 4 + ((y + sy) & 3)) * 8 + dest_z) * UNITS

                def tile(i):
                    if i == UNITS:
                        return extra_ref[pl.ds(pl.multiple_of(kx * 8, 8), 8), :]
                    return acc_ref[kx, base + i]

                for i in range(0, UNITS + 1, 2):
                    both = jnp.concatenate([tile(i), tile(i + 1)], axis=0).astype(BF)
                    number = i // PART
                    hop, rest = (sx, sy) if number % 2 == 0 else (sy, sx)
                    row = (i % PART) * 8
                    parts[number * 4 + hop][rest, sz, row : row + 16, :] = both
        return carry

    lax.fori_loop(0, 8, place, 0)


def first_sum_kernel(*refs):
    for half in range(2):
        arrived = refs[half:8:2]
        for rest in range(4):
            for z in range(8):
                total = arrived[0][rest, z].astype(F32)
                for ref in arrived[1:]:
                    total = total + ref[rest, z].astype(F32)
                refs[8 + 8 * half + 2 * rest + z // 4][z % 4] = total


def second_sum_kernel(*refs):
    for half in range(2):
        arrived = refs[half:8:2]
        for z in range(4):
            total = arrived[0][z]
            for ref in arrived[1:]:
                total = total + ref[z]
            refs[8 + z][half * PROWS : (half + 1) * PROWS, :] = total


def final_kernel(where_ref, sigma_ref, *refs):
    d = where_ref[0]
    out_ref = refs[8]

    def rows_of(i):
        rows = slice(i * 8, i * 8 + 8)
        total = refs[0][rows, :]
        for ref in refs[1:8]:
            total = total + ref[rows, :]
        return total

    mass = rows_of(UNITS)
    mass = mass + pltpu.roll(mass, 128 - 32, 1)
    lane = lax.broadcasted_iota(jnp.int32, (8, 128), 1)
    for i in range(UNITS):
        unit = d * UNITS + i
        rotation = unit >> 5
        here = jnp.sum(jnp.where(lane == rotation, mass, 0.0), axis=1, keepdims=True)
        noise = sigma_ref[pl.ds(unit & 15, 1), :]
        out_ref[:, i * 128 : (i + 1) * 128] = rows_of(i) / (here + REG_WEIGHT * noise)


def cost(micros):
    return pl.CostEstimate(flops=int(micros * 1e9), bytes_accessed=0, transcendentals=0)


SMEM = pl.BlockSpec(memory_space=pltpu.SMEM)
VMEM = pl.BlockSpec(memory_space=pltpu.VMEM)


def ring(size, step):
    return [((i + step) % size, i) for i in range(size)]


X = ("x_lo", "x_hi")
X_SWAP = [(0, 3), (1, 2), (2, 1), (3, 0)]
CORE_SWAP = [(0, 1), (1, 0)]


def from_y(value, step):
    return lax.ppermute(value, "y", ring(4, step))


def to_x(value, flips):
    return lax.ppermute(value, X, [(i, i ^ (flips >> 1) ^ ((flips & 1) << 1)) for i in range(4)])


def to_y(value, step):
    return lax.ppermute(value, "y", ring(4, -step))


Z_ORDER = (4, 3, 5, 2, 6, 1, 7, 0)


def to_z(value, step):
    return lax.ppermute(value, "z", ring(8, -step))


def local(particles, rot_center, shifts, references, class_prior, sigma2):
    x_lo, y, z = lax.axis_index("x_lo"), lax.axis_index("y"), lax.axis_index("z")
    x_hi, core = lax.axis_index("x_hi"), lax.axis_index("core")
    refs = jnp.transpose(references, (1, 0, 2)).reshape(ROWS, WIDE)

    zp = z & 1
    with jax.named_scope("swap"):
        raw = lax.ppermute(particles, "core", CORE_SWAP)
    with jax.named_scope("references"):
        quarter = lax.dynamic_slice_in_dim(refs, DIRECT + y * QUART, QUART, 1)
        quarter, shifts, rot_center = lax.optimization_barrier((quarter, shifts, rot_center))
        crossed = lax.ppermute(quarter, X, X_SWAP)
    with jax.named_scope("swap"):
        meta = jnp.concatenate([shifts, rot_center[None]]).astype(F32)
        meta = jnp.pad(meta, ((0, 5), (0, PAD - NP)))
        meta_oth = lax.ppermute(meta, "core", CORE_SWAP)
    with jax.named_scope("references"):
        half = lax.dynamic_slice_in_dim(refs, ZBASE + zp * QUART, QUART, 1)
        half, meta_oth = lax.optimization_barrier((half, meta_oth))
        z_crossed = lax.ppermute(half, X, X_SWAP)
        direct, meta_oth = lax.optimization_barrier((refs[:, :DIRECT], meta_oth))
        direct = lax.ppermute(direct, X, X_SWAP)
    with jax.named_scope("shift"):
        own = shift_particles(particles, meta)
        raw, crossed = lax.optimization_barrier((raw, crossed))
        oth = shift_particles(raw, meta_oth)
    with jax.named_scope("references"):
        quarters = [from_y(crossed, s) for s in (1, 2, 3)]
        z_crossed, oth = lax.optimization_barrier((z_crossed, oth))
        z_other = lax.ppermute(z_crossed, "z", [(i, i ^ 1) for i in range(8)])
    inv = (1.0 / jnp.concatenate([sigma2, sigma2])).reshape(1, WIDE)
    log_prior = jnp.log(class_prior).reshape(2, 2, 8)
    own_bias = jnp.tile(log_prior[x_hi, core], ROTS).reshape(ROWS, 1)
    oth_bias = jnp.tile(log_prior[1 - x_hi, core], ROTS).reshape(ROWS, 1)

    raised = jax.ShapeDtypeStruct((LANES, ROWS, 128), F32)
    stats = jax.ShapeDtypeStruct((8, NP2), F32)
    with jax.named_scope("scores"):
        weighted, first, first_stats = pl.pallas_call(
            own_kernel,
            out_shape=[jax.ShapeDtypeStruct((NP2, WIDE), BF), raised, stats],
            in_specs=[VMEM] * 7,
            out_specs=[VMEM] * 3,
            scratch_shapes=[pltpu.VMEM((LANES, ROWS, 128), F32)],
            cost_estimate=cost(7),
            compiler_params=pltpu.CompilerParams(vmem_limit_bytes=24 * MB),
        )(own, oth, inv, own_bias, refs, meta, meta_oth)
        offsets = [DIRECT + ((y + s) & 3) * QUART for s in range(4)]
        offsets = jnp.stack([offsets[0], ZBASE + zp * QUART] + offsets[1:] + [ZBASE + (1 - zp) * QUART])
        second, mine = pl.pallas_call(
            other_kernel,
            out_shape=[raised, stats],
            in_specs=[SMEM] + [VMEM] * 13,
            out_specs=[VMEM] * 2,
            scratch_shapes=[pltpu.VMEM((LANES, ROWS, 128), F32)],
            cost_estimate=cost(5),
            compiler_params=pltpu.CompilerParams(vmem_limit_bytes=16 * MB),
        )(offsets, weighted, inv, oth_bias, meta, meta_oth, first_stats, direct, crossed, z_crossed, *quarters, z_other)
        theirs = lax.ppermute(mine, "core", CORE_SWAP)

    with jax.named_scope("sums"):
        parts = pl.pallas_call(
            sums_kernel,
            out_shape=[jax.ShapeDtypeStruct((4, 8, PROWS, 128), BF)] * 8,
            in_specs=[SMEM] + [VMEM] * 6,
            out_specs=[VMEM] * 8,
            scratch_shapes=[
                pltpu.VMEM((ROTS * 16, NP2), BF),
                pltpu.VMEM((2, ROTS * WIDE // 128, 8, 128), F32),
                pltpu.VMEM((ROTS * 16, 128), F32),
                pltpu.VMEM((16, 128), F32),
            ],
            cost_estimate=cost(6),
            compiler_params=pltpu.CompilerParams(vmem_limit_bytes=28 * MB),
        )(jnp.stack([x_hi, x_lo, y] + [(z + s) & 7 for s in Z_ORDER]), first, second, mine, theirs, own, oth)

    order = (2, 3, 1)
    sends = (to_x, to_y)
    with jax.named_scope("reduce1"):
        arrived = [[parts[0]], [parts[4]]]
        for s in order:
            for n in range(2):
                arrived[n].append(sends[n](parts[4 * n + s], s))
        firsts = pl.pallas_call(
            first_sum_kernel,
            out_shape=[jax.ShapeDtypeStruct((4, PROWS, 128), F32)] * 16,
            in_specs=[VMEM] * 8,
            out_specs=[VMEM] * 16,
            compiler_params=pltpu.CompilerParams(vmem_limit_bytes=12 * MB),
        )(*[piece for pair in zip(*arrived) for piece in pair])
    slots = []
    for far in range(2):
        with jax.named_scope("reduce2"):
            pieces = [[firsts[far]], [firsts[8 + far]]]
            for s in order:
                for n in range(2):
                    pieces[n].append(sends[1 - n](firsts[8 * n + 2 * s + far], s))
            slots += pl.pallas_call(
                second_sum_kernel,
                out_shape=[jax.ShapeDtypeStruct((2 * PROWS, 128), F32)] * 4,
                in_specs=[VMEM] * 8,
                out_specs=[VMEM] * 4,
                compiler_params=pltpu.CompilerParams(vmem_limit_bytes=8 * MB),
            )(*[piece for pair in zip(*pieces) for piece in pair])
    with jax.named_scope("reduce3"):
        owned = [to_z(slot, s) if s else slot for slot, s in zip(slots, Z_ORDER)]

    with jax.named_scope("means"):
        d = (x_lo * 4 + y) * 8 + z
        return pl.pallas_call(
            final_kernel,
            out_shape=jax.ShapeDtypeStruct((8, 1920), F32),
            in_specs=[SMEM] + [VMEM] * 9,
            out_specs=VMEM,
            compiler_params=pltpu.CompilerParams(vmem_limit_bytes=8 * MB),
        )(d.reshape(1), sigma2.reshape(16, 128), *owned)


def solution(mesh):
    fine = Mesh(mesh.devices.reshape(2, 4, 8, 2, 2), ("x_lo", "y", "z", "x_hi", "core"))
    dom, grp = ("x_lo", "y", "z"), ("x_hi", "core")
    return jax.shard_map(
        local,
        mesh=fine,
        in_specs=(P(dom + grp, None), P(dom + grp), P(None, dom + grp), P(grp, None, None), P(), P()),
        out_specs=P(grp, dom),
        check_vma=False,
    )
```

```python
import functools

import jax
import jax.numpy as jnp
from jax import lax
from jax.experimental import pallas as pl
from jax.experimental.pallas import tpu as pltpu
from jax.sharding import Mesh, PartitionSpec as P

HALFWIN = 6
BOX = 128
KXW = 32
KYW = 64
TWO_PI = 6.283185307179586
REG_WEIGHT = 0.05

F = 2048
WIDE = 2 * F
ROTS = 30
ROWS = ROTS * 8
NP = 448
PAD = 512
NP2 = 2 * PAD
LANES = NP2 // 128
DIRECT = 1024
QUART = 512
ZBASE = DIRECT + 4 * QUART
UNITS = 15
PART = 8
PROWS = PART * 8

BF = jnp.bfloat16
F32 = jnp.float32
MB = 1024 * 1024


def turn_cos_sin(turns):
    quarter = jnp.floor(4.0 * turns + 0.5)
    x = TWO_PI * (turns - 0.25 * quarter)
    q = quarter - 4.0 * jnp.floor(0.25 * quarter)
    x2 = x * x
    s = x * (1.0 + x2 * (-1.0 / 6 + x2 * (1.0 / 120 + x2 * (-1.0 / 5040 + x2 * (1.0 / 362880)))))
    c = 1.0 + x2 * (-0.5 + x2 * (1.0 / 24 + x2 * (-1.0 / 720 + x2 * (1.0 / 40320))))
    odd = (q == 1.0) | (q == 3.0)
    cos = jnp.where(odd, s, c)
    sin = jnp.where(odd, c, s)
    cos = jnp.where((q == 1.0) | (q == 2.0), -cos, cos)
    sin = jnp.where(q >= 2.0, -sin, sin)
    return cos, sin


def shift_kernel(meta_ref, p_ref, o_ref, turned_ref):
    rows = p_ref.shape[0]
    step = pl.program_id(0)

    @pl.when(step == 0)
    def _():
        turned_ref[...] = jnp.transpose(meta_ref[...])

    shifts = turned_ref[pl.ds(pl.multiple_of(step * rows, rows), rows), :]
    lane = lax.broadcasted_iota(jnp.int32, (rows, 128), 1)
    kx = (lane & (KXW - 1)).astype(F32)
    ky = ((lane >> 5) - KYW // 2).astype(F32)
    sx = shifts[:, 0:1]
    sy = shifts[:, 1:2]
    c, s = turn_cos_sin((sx * kx + sy * ky) * (1.0 / BOX))
    dc, ds = turn_cos_sin(jnp.broadcast_to(sy * (128 // KXW), (rows, 128)) * (1.0 / BOX))
    for b in range(F // 128):
        re = p_ref[:, b * 128 : (b + 1) * 128].astype(F32)
        im = p_ref[:, F + b * 128 : F + (b + 1) * 128].astype(F32)
        o_ref[:, b * 128 : (b + 1) * 128] = (re * c + im * s).astype(BF)
        o_ref[:, F + b * 128 : F + (b + 1) * 128] = (im * c - re * s).astype(BF)
        c, s = c * dc - s * ds, s * dc + c * ds


def shift_particles(particles, meta):
    block = 64
    return pl.pallas_call(
        shift_kernel,
        grid=(NP // block,),
        out_shape=jax.ShapeDtypeStruct((NP, WIDE), BF),
        in_specs=[
            pl.BlockSpec((8, PAD), lambda i: (0, 0)),
            pl.BlockSpec((block, WIDE), lambda i: (i, 0)),
        ],
        out_specs=pl.BlockSpec((block, WIDE), lambda i: (i, 0)),
        scratch_shapes=[pltpu.VMEM((PAD, 8), F32)],
        cost_estimate=cost(5),
            compiler_params=pltpu.CompilerParams(vmem_limit_bytes=4 * MB),
    )(meta, particles)


def weigh(own_ref, oth_ref, inv_ref, w_ref):
    width = 512
    for start in range(0, WIDE, width):
        cols = slice(start, start + width)
        inv = inv_ref[:, cols]
        w_ref[0:NP, cols] = (own_ref[:, cols].astype(F32) * inv).astype(BF)
        w_ref[PAD : PAD + NP, cols] = (oth_ref[:, cols].astype(F32) * inv).astype(BF)
        w_ref[NP:PAD, cols] = jnp.zeros((PAD - NP, width), BF)
        w_ref[PAD + NP :, cols] = jnp.zeros((PAD - NP, width), BF)


def correlate(w_ref, inv_ref, bias_ref, pieces, acc_ref):
    energy = jnp.zeros((ROWS, 128), F32)
    first = True
    for piece, base, width in pieces:
        for start in range(0, piece.shape[1], width):
            cols = pl.ds(base + start, width)
            inv = inv_ref[:, cols]
            part = lax.dot_general(
                piece[:, start : start + width],
                w_ref[:, cols],
                (((1,), (1,)), ((), ())),
                preferred_element_type=F32,
            )
            for j in range(LANES):
                block = part[:, j * 128 : (j + 1) * 128]
                acc_ref[j] = block if first else acc_ref[j] + block
            first = False
            for lanes in range(0, width, 128):
                v = piece[:, start + lanes : start + lanes + 128].astype(F32)
                energy = energy + v * v * inv[:, lanes : lanes + 128]
    return bias_ref[...] - 0.5 * jnp.sum(energy, axis=1, keepdims=True)


def exponentiate(acc_ref, bias, metas, out_ref, j):
    half = LANES // 2
    rot = metas[j // half][2:3, (j % half) * 128 : (j % half + 1) * 128]
    low = jnp.full((8, 128), -jnp.inf, F32)
    top = low
    for r in range(ROTS):
        rows = slice(r * 8, r * 8 + 8)
        score = jnp.where(inside_window(r, rot), acc_ref[j, rows, :] + bias[rows, :], low)
        out_ref[j, rows, :] = score
        top = jnp.maximum(top, score)
    top = jnp.max(top, axis=0, keepdims=True)
    mass = jnp.zeros((8, 128), F32)
    for r in range(ROTS):
        rows = slice(r * 8, r * 8 + 8)
        raised = jnp.exp(out_ref[j, rows, :] - top)
        out_ref[j, rows, :] = raised
        mass = mass + raised
    return top, jnp.sum(mass, axis=0, keepdims=True)


def inside_window(rotation, rot):
    return jnp.abs(jnp.abs(float(rotation) - rot) - ROTS / 2) >= ROTS / 2 - HALFWIN


def own_kernel(own_ref, oth_ref, inv_ref, bias_ref, refs_ref, meta_a, meta_b, w_ref, e_ref, stats_ref, acc_ref):
    weigh(own_ref, oth_ref, inv_ref, w_ref)
    bias = correlate(w_ref, inv_ref, bias_ref, [(refs_ref, 0, 512)], acc_ref)
    row = lax.broadcasted_iota(jnp.int32, (8, 128), 0)
    for j in range(LANES):
        top, mass = exponentiate(acc_ref, bias, (meta_a, meta_b), e_ref, j)
        stats_ref[:, j * 128 : (j + 1) * 128] = jnp.where(row == 0, top, mass)


def other_kernel(
    where_ref, w_ref, inv_ref, bias_ref, meta_a, meta_b, first_ref, d_ref, q0, z0, q1, q2, q3, z1,
    e_ref, stats_ref, acc_ref,
):
    pieces = [(d_ref, 0, 512)]
    for s, q in enumerate((q0, z0, q1, q2, q3, z1)):
        pieces.append((q, pl.multiple_of(where_ref[s], 128), QUART))
    bias = correlate(w_ref, inv_ref, bias_ref, pieces, acc_ref)
    row = lax.broadcasted_iota(jnp.int32, (8, 128), 0)
    for j in range(LANES):
        lanes = slice(j * 128, (j + 1) * 128)
        top_b, mass_b = exponentiate(acc_ref, bias, (meta_a, meta_b), e_ref, j)
        top_a, mass_a = first_ref[0:1, lanes], first_ref[1:2, lanes]
        top = jnp.maximum(top_a, top_b)
        mass = mass_a * jnp.exp(top_a - top) + mass_b * jnp.exp(top_b - top)
        tops = jnp.where(row == 2, top_a, top_b)
        stats_ref[:, lanes] = jnp.where(row == 0, top, jnp.where(row == 1, mass, tops))


def sums_kernel(where_ref, first_ref, second_ref, mine_ref, theirs_ref, own_ref, oth_ref, *refs):
    parts, (p_ref, acc_ref, mass_ref, extra_ref) = refs[:8], refs[8:]
    x_hi, x_lo, y, z = where_ref[0], where_ref[1], where_ref[2], where_ref[3]
    mass_ref[...] = jnp.zeros_like(mass_ref)
    for j in range(LANES):
        lanes = slice(j * 128, (j + 1) * 128)
        facing = (j + LANES // 2) % LANES
        crossed = slice(facing * 128, (facing + 1) * 128)
        top_a, mass_a = mine_ref[0:1, lanes], mine_ref[1:2, lanes]
        top_b, mass_b = theirs_ref[0:1, crossed], theirs_ref[1:2, crossed]
        top = jnp.maximum(top_a, top_b)
        scale = 1.0 / (mass_a * jnp.exp(top_a - top) + mass_b * jnp.exp(top_b - top))
        scale_a = jnp.exp(mine_ref[2:3, lanes] - top) * scale
        scale_b = jnp.exp(mine_ref[3:4, lanes] - top) * scale
        if j % (LANES // 2) == LANES // 2 - 1:
            used = lax.broadcasted_iota(jnp.int32, (1, 128), 1) < 128 - (PAD - NP)
            scale_a = jnp.where(used, scale_a, 0.0)
            scale_b = jnp.where(used, scale_b, 0.0)
        for r in range(ROTS):
            rows = slice(r * 8, r * 8 + 8)
            p = first_ref[j, rows, :] * scale_a
            q = second_ref[j, rows, :] * scale_b
            low = jnp.where(x_hi == 0, p, q)
            high = jnp.where(x_hi == 0, q, p)
            both = jnp.concatenate([low, high], axis=0)
            p_ref[r * 16 : (r + 1) * 16, lanes] = both.astype(BF)
            mass_ref[r * 16 : (r + 1) * 16, :] += both
    lane = lax.broadcasted_iota(jnp.int32, (16, 128), 1)
    totals = jnp.zeros((16, 128), F32)
    for r in range(ROTS):
        row_sum = jnp.sum(mass_ref[r * 16 : (r + 1) * 16, :], axis=1, keepdims=True)
        totals = jnp.where(lane == r, row_sum, totals)
    coarse = totals.astype(BF).astype(F32)
    extra_ref[...] = jnp.where(lane < 32, coarse, pltpu.roll(totals - coarse, 32, 1))
    width = 512
    for cb in range(WIDE // width):
        cols = slice(cb * width, (cb + 1) * width)
        part = jnp.dot(p_ref[:, 0:NP], own_ref[:, cols], preferred_element_type=F32) + jnp.dot(
            p_ref[:, PAD : PAD + NP], oth_ref[:, cols], preferred_element_type=F32
        )
        for j in range(width // 128):
            fb = cb * (width // 128) + j
            for r in range(ROTS):
                for kx in range(2):
                    row = r * 16 + kx * 8
                    acc_ref[kx, 32 * r + fb] = part[row : row + 8, j * 128 : (j + 1) * 128]

    def place(sz, carry):
        dest_z = (z + sz) & 7
        for sx in range(4):
            kx, dest_x = x_hi ^ (sx >> 1), x_lo ^ (sx & 1)
            for sy in range(4):
                base = ((dest_x * 4 + ((y + sy) & 3)) * 8 + dest_z) * UNITS

                def tile(i):
                    if i == UNITS:
                        return extra_ref[pl.ds(pl.multiple_of(kx * 8, 8), 8), :]
                    return acc_ref[kx, base + i]

                for i in range(0, UNITS + 1, 2):
                    both = jnp.concatenate([tile(i), tile(i + 1)], axis=0)
                    number = i // PART
                    hop, rest = (sx, sy) if number % 2 == 0 else (sy, sx)
                    row = (i % PART) * 8
                    part_ref = parts[number * 4 + hop]
                    part_ref[rest, sz, row : row + 16, :] = both.astype(part_ref.dtype)
        return carry

    lax.fori_loop(0, 8, place, 0)


def first_sum_kernel(*refs):
    for half in range(2):
        arrived = refs[half:8:2]
        for rest in range(4):
            for z in range(8):
                total = arrived[0][rest, z].astype(F32)
                for ref in arrived[1:]:
                    total = total + ref[rest, z].astype(F32)
                out_ref = refs[8 + 4 * half + rest]
                out_ref[z] = total.astype(out_ref.dtype)


def second_sum_kernel(*refs):
    for half in range(2):
        arrived = refs[half:8:2]
        for z in range(8):
            total = arrived[0][z]
            for ref in arrived[1:]:
                total = total + ref[z].astype(F32)
            refs[8 + z][half * PROWS : (half + 1) * PROWS, :] = total


def final_kernel(where_ref, sigma_ref, *refs):
    d = where_ref[0]
    out_ref = refs[8]

    def rows_of(i):
        rows = slice(i * 8, i * 8 + 8)
        total = refs[0][rows, :]
        for ref in refs[1:8]:
            total = total + ref[rows, :]
        return total

    mass = rows_of(UNITS)
    mass = mass + pltpu.roll(mass, 128 - 32, 1)
    lane = lax.broadcasted_iota(jnp.int32, (8, 128), 1)
    for i in range(UNITS):
        unit = d * UNITS + i
        rotation = unit >> 5
        here = jnp.sum(jnp.where(lane == rotation, mass, 0.0), axis=1, keepdims=True)
        noise = sigma_ref[pl.ds(unit & 15, 1), :]
        out_ref[:, i * 128 : (i + 1) * 128] = rows_of(i) / (here + REG_WEIGHT * noise)


def cost(micros):
    return pl.CostEstimate(flops=int(micros * 1e9), bytes_accessed=0, transcendentals=0)


SMEM = pl.BlockSpec(memory_space=pltpu.SMEM)
VMEM = pl.BlockSpec(memory_space=pltpu.VMEM)


def ring(size, step):
    return [((i + step) % size, i) for i in range(size)]


X = ("x_lo", "x_hi")
X_SWAP = [(0, 3), (1, 2), (2, 1), (3, 0)]
CORE_SWAP = [(0, 1), (1, 0)]


def from_y(value, step):
    return lax.ppermute(value, "y", ring(4, step))


def to_x(value, flips):
    return lax.ppermute(value, X, [(i, i ^ (flips >> 1) ^ ((flips & 1) << 1)) for i in range(4)])


def to_y(value, step):
    return lax.ppermute(value, "y", ring(4, -step))


def to_z(value, step):
    return lax.ppermute(value, "z", ring(8, -step))


def local(particles, rot_center, shifts, references, class_prior, sigma2):
    x_lo, y, z = lax.axis_index("x_lo"), lax.axis_index("y"), lax.axis_index("z")
    x_hi, core = lax.axis_index("x_hi"), lax.axis_index("core")
    refs = jnp.transpose(references, (1, 0, 2)).reshape(ROWS, WIDE)

    zp = z & 1
    with jax.named_scope("swap"):
        raw = lax.ppermute(particles, "core", CORE_SWAP)
    with jax.named_scope("references"):
        quarter = lax.dynamic_slice_in_dim(refs, DIRECT + y * QUART, QUART, 1)
        quarter, shifts, rot_center = lax.optimization_barrier((quarter, shifts, rot_center))
        crossed = lax.ppermute(quarter, X, X_SWAP)
    with jax.named_scope("swap"):
        meta = jnp.concatenate([shifts, rot_center[None]]).astype(F32)
        meta = jnp.pad(meta, ((0, 5), (0, PAD - NP)))
        meta_oth = lax.ppermute(meta, "core", CORE_SWAP)
    with jax.named_scope("references"):
        half = lax.dynamic_slice_in_dim(refs, ZBASE + zp * QUART, QUART, 1)
        half, meta_oth = lax.optimization_barrier((half, meta_oth))
        z_crossed = lax.ppermute(half, X, X_SWAP)
        direct, meta_oth = lax.optimization_barrier((refs[:, :DIRECT], meta_oth))
        direct = lax.ppermute(direct, X, X_SWAP)
    with jax.named_scope("shift"):
        own = shift_particles(particles, meta)
        raw, crossed = lax.optimization_barrier((raw, crossed))
        oth = shift_particles(raw, meta_oth)
    with jax.named_scope("references"):
        quarters = [from_y(crossed, s) for s in (1, 2, 3)]
        z_crossed, oth = lax.optimization_barrier((z_crossed, oth))
        z_other = lax.ppermute(z_crossed, "z", [(i, i ^ 1) for i in range(8)])
    inv = (1.0 / jnp.concatenate([sigma2, sigma2])).reshape(1, WIDE)
    log_prior = jnp.log(class_prior).reshape(2, 2, 8)
    own_bias = jnp.tile(log_prior[x_hi, core], ROTS).reshape(ROWS, 1)
    oth_bias = jnp.tile(log_prior[1 - x_hi, core], ROTS).reshape(ROWS, 1)

    raised = jax.ShapeDtypeStruct((LANES, ROWS, 128), F32)
    stats = jax.ShapeDtypeStruct((8, NP2), F32)
    with jax.named_scope("scores"):
        weighted, first, first_stats = pl.pallas_call(
            own_kernel,
            out_shape=[jax.ShapeDtypeStruct((NP2, WIDE), BF), raised, stats],
            in_specs=[VMEM] * 7,
            out_specs=[VMEM] * 3,
            scratch_shapes=[pltpu.VMEM((LANES, ROWS, 128), F32)],
            cost_estimate=cost(7),
            compiler_params=pltpu.CompilerParams(vmem_limit_bytes=6 * MB),
        )(own, oth, inv, own_bias, refs, meta, meta_oth)
        offsets = [DIRECT + ((y + s) & 3) * QUART for s in range(4)]
        offsets = jnp.stack([offsets[0], ZBASE + zp * QUART] + offsets[1:] + [ZBASE + (1 - zp) * QUART])
        second, mine = pl.pallas_call(
            other_kernel,
            out_shape=[raised, stats],
            in_specs=[SMEM] + [VMEM] * 13,
            out_specs=[VMEM] * 2,
            scratch_shapes=[pltpu.VMEM((LANES, ROWS, 128), F32)],
            cost_estimate=cost(5),
            compiler_params=pltpu.CompilerParams(vmem_limit_bytes=6 * MB),
        )(offsets, weighted, inv, oth_bias, meta, meta_oth, first_stats, direct, crossed, z_crossed, *quarters, z_other)
        theirs = lax.ppermute(mine, "core", CORE_SWAP)

    with jax.named_scope("sums"):
        parts = pl.pallas_call(
            sums_kernel,
            out_shape=([jax.ShapeDtypeStruct((4, 8, PROWS, 128), F32)] + [jax.ShapeDtypeStruct((4, 8, PROWS, 128), BF)] * 3) * 2,
            in_specs=[SMEM] + [VMEM] * 6,
            out_specs=[VMEM] * 8,
            scratch_shapes=[
                pltpu.VMEM((ROTS * 16, NP2), BF),
                pltpu.VMEM((2, ROTS * WIDE // 128, 8, 128), F32),
                pltpu.VMEM((ROTS * 16, 128), F32),
                pltpu.VMEM((16, 128), F32),
            ],
            cost_estimate=cost(6),
            compiler_params=pltpu.CompilerParams(vmem_limit_bytes=14 * MB),
        )(jnp.stack([x_hi, x_lo, y, z]), first, second, mine, theirs, own, oth)

    order = (2, 3, 1)
    sends = (to_x, to_y)
    with jax.named_scope("reduce1"):
        arrived = [[parts[0]], [parts[4]]]
        for s in order:
            for n in range(2):
                arrived[n].append(sends[n](parts[4 * n + s], s))
        firsts = pl.pallas_call(
            first_sum_kernel,
            out_shape=([jax.ShapeDtypeStruct((8, PROWS, 128), F32)] + [jax.ShapeDtypeStruct((8, PROWS, 128), BF)] * 3) * 2,
            in_specs=[VMEM] * 8,
            out_specs=[VMEM] * 8,
            compiler_params=pltpu.CompilerParams(vmem_limit_bytes=4 * MB),
        )(*[piece for pair in zip(*arrived) for piece in pair])
    with jax.named_scope("reduce2"):
        pieces = [[firsts[0]], [firsts[4]]]
        for s in order:
            for n in range(2):
                pieces[n].append(sends[1 - n](firsts[4 * n + s], s))
        slots = pl.pallas_call(
            second_sum_kernel,
            out_shape=[jax.ShapeDtypeStruct((2 * PROWS, 128), F32)] * 8,
            in_specs=[VMEM] * 8,
            out_specs=[VMEM] * 8,
            compiler_params=pltpu.CompilerParams(vmem_limit_bytes=4 * MB),
        )(*[piece for pair in zip(*pieces) for piece in pair])
    with jax.named_scope("reduce3"):
        owned = [slots[0]] + [to_z(slots[s], s) for s in (4, 3, 5, 2, 6, 1, 7)]

    with jax.named_scope("means"):
        d = (x_lo * 4 + y) * 8 + z
        return pl.pallas_call(
            final_kernel,
            out_shape=jax.ShapeDtypeStruct((8, 1920), F32),
            in_specs=[SMEM] + [VMEM] * 9,
            out_specs=VMEM,
            compiler_params=pltpu.CompilerParams(vmem_limit_bytes=4 * MB),
        )(d.reshape(1), sigma2.reshape(16, 128), *owned)


def solution(mesh):
    fine = Mesh(mesh.devices.reshape(2, 4, 8, 2, 2), ("x_lo", "y", "z", "x_hi", "core"))
    dom, grp = ("x_lo", "y", "z"), ("x_hi", "core")
    return jax.shard_map(
        local,
        mesh=fine,
        in_specs=(P(dom + grp, None), P(dom + grp), P(None, dom + grp), P(grp, None, None), P(), P()),
        out_specs=P(grp, dom),
        check_vma=False,
    )
```

```python
import functools

import jax
import jax.numpy as jnp
from jax import lax
from jax.experimental import pallas as pl
from jax.experimental.pallas import tpu as pltpu
from jax.sharding import Mesh, PartitionSpec as P

HALFWIN = 6
BOX = 128
KXW = 32
KYW = 64
TWO_PI = 6.283185307179586
REG_WEIGHT = 0.05

F = 2048
WIDE = 2 * F
ROTS = 30
ROWS = ROTS * 8
NP = 448
PAD = 512
NP2 = 2 * PAD
LANES = NP2 // 128
DIRECT = 1024
QUART = 512
ZBASE = DIRECT + 4 * QUART
UNITS = 15
PART = 8
PROWS = PART * 8

BF = jnp.bfloat16
F32 = jnp.float32
MB = 1024 * 1024


def turn_cos_sin(turns):
    quarter = jnp.floor(4.0 * turns + 0.5)
    x = TWO_PI * (turns - 0.25 * quarter)
    q = quarter - 4.0 * jnp.floor(0.25 * quarter)
    x2 = x * x
    s = x * (1.0 + x2 * (-1.0 / 6 + x2 * (1.0 / 120 + x2 * (-1.0 / 5040 + x2 * (1.0 / 362880)))))
    c = 1.0 + x2 * (-0.5 + x2 * (1.0 / 24 + x2 * (-1.0 / 720 + x2 * (1.0 / 40320))))
    odd = (q == 1.0) | (q == 3.0)
    cos = jnp.where(odd, s, c)
    sin = jnp.where(odd, c, s)
    cos = jnp.where((q == 1.0) | (q == 2.0), -cos, cos)
    sin = jnp.where(q >= 2.0, -sin, sin)
    return cos, sin


def shift_kernel(meta_ref, p_ref, o_ref, turned_ref):
    rows = p_ref.shape[0]
    step = pl.program_id(0)

    @pl.when(step == 0)
    def _():
        turned_ref[...] = jnp.transpose(meta_ref[...])

    shifts = turned_ref[pl.ds(pl.multiple_of(step * rows, rows), rows), :]
    lane = lax.broadcasted_iota(jnp.int32, (rows, 128), 1)
    kx = (lane & (KXW - 1)).astype(F32)
    ky = ((lane >> 5) - KYW // 2).astype(F32)
    sx = shifts[:, 0:1]
    sy = shifts[:, 1:2]
    c, s = turn_cos_sin((sx * kx + sy * ky) * (1.0 / BOX))
    dc, ds = turn_cos_sin(jnp.broadcast_to(sy * (128 // KXW), (rows, 128)) * (1.0 / BOX))
    for b in range(F // 128):
        re = p_ref[:, b * 128 : (b + 1) * 128].astype(F32)
        im = p_ref[:, F + b * 128 : F + (b + 1) * 128].astype(F32)
        o_ref[:, b * 128 : (b + 1) * 128] = (re * c + im * s).astype(BF)
        o_ref[:, F + b * 128 : F + (b + 1) * 128] = (im * c - re * s).astype(BF)
        c, s = c * dc - s * ds, s * dc + c * ds


def shift_particles(particles, meta):
    block = 64
    return pl.pallas_call(
        shift_kernel,
        grid=(NP // block,),
        out_shape=jax.ShapeDtypeStruct((NP, WIDE), BF),
        in_specs=[
            pl.BlockSpec((8, PAD), lambda i: (0, 0)),
            pl.BlockSpec((block, WIDE), lambda i: (i, 0)),
        ],
        out_specs=pl.BlockSpec((block, WIDE), lambda i: (i, 0)),
        scratch_shapes=[pltpu.VMEM((PAD, 8), F32)],
        cost_estimate=cost(5),
            compiler_params=pltpu.CompilerParams(vmem_limit_bytes=4 * MB),
    )(meta, particles)


def weigh(own_ref, oth_ref, inv_ref, w_ref):
    width = 512
    for start in range(0, WIDE, width):
        cols = slice(start, start + width)
        inv = inv_ref[:, cols]
        w_ref[0:NP, cols] = (own_ref[:, cols].astype(F32) * inv).astype(BF)
        w_ref[PAD : PAD + NP, cols] = (oth_ref[:, cols].astype(F32) * inv).astype(BF)
        w_ref[NP:PAD, cols] = jnp.zeros((PAD - NP, width), BF)
        w_ref[PAD + NP :, cols] = jnp.zeros((PAD - NP, width), BF)


def correlate(w_ref, inv_ref, pieces, acc_ref, begun=None):
    energy = jnp.zeros((ROWS, 128), F32)
    for piece, base, width in pieces:
        for start in range(0, piece.shape[1], width):
            cols = pl.ds(base + start, width)
            inv = inv_ref[:, cols]
            part = lax.dot_general(
                piece[:, start : start + width],
                w_ref[:, cols],
                (((1,), (1,)), ((), ())),
                preferred_element_type=F32,
            )
            for j in range(LANES):
                block = part[:, j * 128 : (j + 1) * 128]
                acc_ref[j] = block if begun is None else begun[j] + block
            begun = acc_ref
            for lanes in range(0, width, 128):
                v = piece[:, start + lanes : start + lanes + 128].astype(F32)
                energy = energy + v * v * inv[:, lanes : lanes + 128]
    return energy


def offset(bias_ref, energy):
    return bias_ref[...] - 0.5 * jnp.sum(energy, axis=1, keepdims=True)


def exponentiate(acc_ref, bias, metas, out_ref, j):
    half = LANES // 2
    rot = metas[j // half][2:3, (j % half) * 128 : (j % half + 1) * 128]
    low = jnp.full((8, 128), -jnp.inf, F32)
    top = low
    for r in range(ROTS):
        rows = slice(r * 8, r * 8 + 8)
        score = jnp.where(inside_window(r, rot), acc_ref[j, rows, :] + bias[rows, :], low)
        out_ref[j, rows, :] = score
        top = jnp.maximum(top, score)
    top = jnp.max(top, axis=0, keepdims=True)
    mass = jnp.zeros((8, 128), F32)
    for r in range(ROTS):
        rows = slice(r * 8, r * 8 + 8)
        raised = jnp.exp(out_ref[j, rows, :] - top)
        out_ref[j, rows, :] = raised
        mass = mass + raised
    return top, jnp.sum(mass, axis=0, keepdims=True)


def inside_window(rotation, rot):
    return jnp.abs(jnp.abs(float(rotation) - rot) - ROTS / 2) >= ROTS / 2 - HALFWIN


def own_kernel(
    where_ref, own_ref, oth_ref, inv_ref, bias_ref, refs_ref, meta_a, meta_b, q0, z0,
    w_ref, e_ref, stats_ref, begun_ref, energy_ref, acc_ref,
):
    weigh(own_ref, oth_ref, inv_ref, w_ref)
    bias = offset(bias_ref, correlate(w_ref, inv_ref, [(refs_ref, 0, 512)], acc_ref))
    pieces = [(q, pl.multiple_of(where_ref[s], 128), QUART) for s, q in enumerate((q0, z0))]
    energy_ref[...] = correlate(w_ref, inv_ref, pieces, begun_ref)
    row = lax.broadcasted_iota(jnp.int32, (8, 128), 0)
    for j in range(LANES):
        top, mass = exponentiate(acc_ref, bias, (meta_a, meta_b), e_ref, j)
        stats_ref[:, j * 128 : (j + 1) * 128] = jnp.where(row == 0, top, mass)


def other_kernel(
    where_ref, w_ref, inv_ref, bias_ref, meta_a, meta_b, first_ref, begun_ref, energy_ref, d_ref, q1, q2, q3, z1,
    e_ref, stats_ref, acc_ref,
):
    pieces = [(d_ref, 0, 512)]
    for s, q in enumerate((q1, q2, q3, z1)):
        pieces.append((q, pl.multiple_of(where_ref[s], 128), QUART))
    bias = offset(bias_ref, energy_ref[...] + correlate(w_ref, inv_ref, pieces, acc_ref, begun_ref))
    row = lax.broadcasted_iota(jnp.int32, (8, 128), 0)
    for j in range(LANES):
        lanes = slice(j * 128, (j + 1) * 128)
        top_b, mass_b = exponentiate(acc_ref, bias, (meta_a, meta_b), e_ref, j)
        top_a, mass_a = first_ref[0:1, lanes], first_ref[1:2, lanes]
        top = jnp.maximum(top_a, top_b)
        mass = mass_a * jnp.exp(top_a - top) + mass_b * jnp.exp(top_b - top)
        tops = jnp.where(row == 2, top_a, top_b)
        stats_ref[:, lanes] = jnp.where(row == 0, top, jnp.where(row == 1, mass, tops))


def sums_kernel(where_ref, first_ref, second_ref, mine_ref, theirs_ref, own_ref, oth_ref, *refs):
    parts, (p_ref, acc_ref, mass_ref, extra_ref) = refs[:8], refs[8:]
    x_hi, x_lo, y, z = where_ref[0], where_ref[1], where_ref[2], where_ref[3]
    mass_ref[...] = jnp.zeros_like(mass_ref)
    for j in range(LANES):
        lanes = slice(j * 128, (j + 1) * 128)
        facing = (j + LANES // 2) % LANES
        crossed = slice(facing * 128, (facing + 1) * 128)
        top_a, mass_a = mine_ref[0:1, lanes], mine_ref[1:2, lanes]
        top_b, mass_b = theirs_ref[0:1, crossed], theirs_ref[1:2, crossed]
        top = jnp.maximum(top_a, top_b)
        scale = 1.0 / (mass_a * jnp.exp(top_a - top) + mass_b * jnp.exp(top_b - top))
        scale_a = jnp.exp(mine_ref[2:3, lanes] - top) * scale
        scale_b = jnp.exp(mine_ref[3:4, lanes] - top) * scale
        if j % (LANES // 2) == LANES // 2 - 1:
            used = lax.broadcasted_iota(jnp.int32, (1, 128), 1) < 128 - (PAD - NP)
            scale_a = jnp.where(used, scale_a, 0.0)
            scale_b = jnp.where(used, scale_b, 0.0)
        for r in range(ROTS):
            rows = slice(r * 8, r * 8 + 8)
            p = first_ref[j, rows, :] * scale_a
            q = second_ref[j, rows, :] * scale_b
            low = jnp.where(x_hi == 0, p, q)
            high = jnp.where(x_hi == 0, q, p)
            both = jnp.concatenate([low, high], axis=0)
            p_ref[r * 16 : (r + 1) * 16, lanes] = both.astype(BF)
            mass_ref[r * 16 : (r + 1) * 16, :] += both
    lane = lax.broadcasted_iota(jnp.int32, (16, 128), 1)
    totals = jnp.zeros((16, 128), F32)
    for r in range(ROTS):
        row_sum = jnp.sum(mass_ref[r * 16 : (r + 1) * 16, :], axis=1, keepdims=True)
        totals = jnp.where(lane == r, row_sum, totals)
    coarse = totals.astype(BF).astype(F32)
    extra_ref[...] = jnp.where(lane < 32, coarse, pltpu.roll(totals - coarse, 32, 1))
    width = 512
    for cb in range(WIDE // width):
        cols = slice(cb * width, (cb + 1) * width)
        part = jnp.dot(p_ref[:, 0:NP], own_ref[:, cols], preferred_element_type=F32) + jnp.dot(
            p_ref[:, PAD : PAD + NP], oth_ref[:, cols], preferred_element_type=F32
        )
        for j in range(width // 128):
            fb = cb * (width // 128) + j
            for r in range(ROTS):
                for kx in range(2):
                    row = r * 16 + kx * 8
                    acc_ref[kx, 32 * r + fb] = part[row : row + 8, j * 128 : (j + 1) * 128]

    def place(sz, carry):
        dest_z = (z + sz) & 7
        for sx in range(4):
            kx, dest_x = x_hi ^ (sx >> 1), x_lo ^ (sx & 1)
            for sy in range(4):
                base = ((dest_x * 4 + ((y + sy) & 3)) * 8 + dest_z) * UNITS

                def tile(i):
                    if i == UNITS:
                        return extra_ref[pl.ds(pl.multiple_of(kx * 8, 8), 8), :]
                    return acc_ref[kx, base + i]

                for i in range(0, UNITS + 1, 2):
                    both = jnp.concatenate([tile(i), tile(i + 1)], axis=0)
                    number = i // PART
                    hop, rest = (sx, sy) if number % 2 == 0 else (sy, sx)
                    row = (i % PART) * 8
                    part_ref = parts[number * 4 + hop]
                    part_ref[rest, sz, row : row + 16, :] = both.astype(part_ref.dtype)
        return carry

    lax.fori_loop(0, 8, place, 0)


def first_sum_kernel(*refs):
    for half in range(2):
        arrived = refs[half:8:2]
        for rest in range(4):
            for z in range(8):
                total = arrived[0][rest, z].astype(F32)
                for ref in arrived[1:]:
                    total = total + ref[rest, z].astype(F32)
                out_ref = refs[8 + 4 * half + rest]
                out_ref[z] = total.astype(out_ref.dtype)


def second_sum_kernel(*refs):
    for half in range(2):
        arrived = refs[half:8:2]
        for z in range(8):
            total = arrived[0][z]
            for ref in arrived[1:]:
                total = total + ref[z].astype(F32)
            refs[8 + z][half * PROWS : (half + 1) * PROWS, :] = total


def final_kernel(where_ref, sigma_ref, *refs):
    d = where_ref[0]
    out_ref = refs[8]

    def rows_of(i):
        rows = slice(i * 8, i * 8 + 8)
        total = refs[0][rows, :]
        for ref in refs[1:8]:
            total = total + ref[rows, :]
        return total

    mass = rows_of(UNITS)
    mass = mass + pltpu.roll(mass, 128 - 32, 1)
    lane = lax.broadcasted_iota(jnp.int32, (8, 128), 1)
    for i in range(UNITS):
        unit = d * UNITS + i
        rotation = unit >> 5
        here = jnp.sum(jnp.where(lane == rotation, mass, 0.0), axis=1, keepdims=True)
        noise = sigma_ref[pl.ds(unit & 15, 1), :]
        out_ref[:, i * 128 : (i + 1) * 128] = rows_of(i) / (here + REG_WEIGHT * noise)


def cost(micros):
    return pl.CostEstimate(flops=int(micros * 1e9), bytes_accessed=0, transcendentals=0)


SMEM = pl.BlockSpec(memory_space=pltpu.SMEM)
VMEM = pl.BlockSpec(memory_space=pltpu.VMEM)


def ring(size, step):
    return [((i + step) % size, i) for i in range(size)]


X = ("x_lo", "x_hi")
X_SWAP = [(0, 3), (1, 2), (2, 1), (3, 0)]
CORE_SWAP = [(0, 1), (1, 0)]


def from_y(value, step):
    return lax.ppermute(value, "y", ring(4, step))


def to_x(value, flips):
    return lax.ppermute(value, X, [(i, i ^ (flips >> 1) ^ ((flips & 1) << 1)) for i in range(4)])


def to_y(value, step):
    return lax.ppermute(value, "y", ring(4, -step))


def to_z(value, step):
    return lax.ppermute(value, "z", ring(8, -step))


def local(particles, rot_center, shifts, references, class_prior, sigma2):
    x_lo, y, z = lax.axis_index("x_lo"), lax.axis_index("y"), lax.axis_index("z")
    x_hi, core = lax.axis_index("x_hi"), lax.axis_index("core")
    refs = jnp.transpose(references, (1, 0, 2)).reshape(ROWS, WIDE)

    zp = z & 1
    with jax.named_scope("swap"):
        raw = lax.ppermute(particles, "core", CORE_SWAP)
    with jax.named_scope("references"):
        quarter = lax.dynamic_slice_in_dim(refs, DIRECT + y * QUART, QUART, 1)
        half = lax.dynamic_slice_in_dim(refs, ZBASE + zp * QUART, QUART, 1)
        direct = refs[:, :DIRECT]
        quarter, half, direct, shifts, rot_center = lax.optimization_barrier(
            (quarter, half, direct, shifts, rot_center)
        )
        crossed = lax.ppermute(quarter, X, X_SWAP)
    with jax.named_scope("swap"):
        meta = jnp.concatenate([shifts, rot_center[None]]).astype(F32)
        meta = jnp.pad(meta, ((0, 5), (0, PAD - NP)))
        meta_oth = lax.ppermute(meta, "core", CORE_SWAP)
    with jax.named_scope("references"):
        half, meta, meta_oth = lax.optimization_barrier((half, meta, meta_oth))
        z_crossed = lax.ppermute(half, X, X_SWAP)
        direct, meta_oth = lax.optimization_barrier((direct, meta_oth))
        direct = lax.ppermute(direct, X, X_SWAP)
    with jax.named_scope("shift"):
        own = shift_particles(particles, meta)
        raw, crossed = lax.optimization_barrier((raw, crossed))
        oth = shift_particles(raw, meta_oth)
    with jax.named_scope("references"):
        quarters = [from_y(crossed, s) for s in (1, 2, 3)]
        z_crossed, oth = lax.optimization_barrier((z_crossed, oth))
        z_other = lax.ppermute(z_crossed, "z", [(i, i ^ 1) for i in range(8)])
    inv = (1.0 / jnp.concatenate([sigma2, sigma2])).reshape(1, WIDE)
    log_prior = jnp.log(class_prior).reshape(2, 2, 8)
    own_bias = jnp.tile(log_prior[x_hi, core], ROTS).reshape(ROWS, 1)
    oth_bias = jnp.tile(log_prior[1 - x_hi, core], ROTS).reshape(ROWS, 1)

    raised = jax.ShapeDtypeStruct((LANES, ROWS, 128), F32)
    stats = jax.ShapeDtypeStruct((8, NP2), F32)
    with jax.named_scope("scores"):
        offsets = [DIRECT + ((y + s) & 3) * QUART for s in range(4)]
        z_offsets = [ZBASE + zp * QUART, ZBASE + (1 - zp) * QUART]
        energies = jax.ShapeDtypeStruct((ROWS, 128), F32)
        weighted, first, first_stats, begun, energy = pl.pallas_call(
            own_kernel,
            out_shape=[jax.ShapeDtypeStruct((NP2, WIDE), BF), raised, stats, raised, energies],
            in_specs=[SMEM] + [VMEM] * 9,
            out_specs=[VMEM] * 5,
            scratch_shapes=[pltpu.VMEM((LANES, ROWS, 128), F32)],
            cost_estimate=cost(7),
            compiler_params=pltpu.CompilerParams(vmem_limit_bytes=6 * MB),
        )(jnp.stack([offsets[0], z_offsets[0]]), own, oth, inv, own_bias, refs, meta, meta_oth, crossed, z_crossed)
        second, mine = pl.pallas_call(
            other_kernel,
            out_shape=[raised, stats],
            in_specs=[SMEM] + [VMEM] * 13,
            out_specs=[VMEM] * 2,
            scratch_shapes=[pltpu.VMEM((LANES, ROWS, 128), F32)],
            cost_estimate=cost(5),
            compiler_params=pltpu.CompilerParams(vmem_limit_bytes=6 * MB),
        )(
            jnp.stack(offsets[1:] + z_offsets[1:]), weighted, inv, oth_bias, meta, meta_oth, first_stats,
            begun, energy, direct, *quarters, z_other,
        )
        theirs = lax.ppermute(mine, "core", CORE_SWAP)

    with jax.named_scope("sums"):
        parts = pl.pallas_call(
            sums_kernel,
            out_shape=([jax.ShapeDtypeStruct((4, 8, PROWS, 128), F32)] + [jax.ShapeDtypeStruct((4, 8, PROWS, 128), BF)] * 3) * 2,
            in_specs=[SMEM] + [VMEM] * 6,
            out_specs=[VMEM] * 8,
            scratch_shapes=[
                pltpu.VMEM((ROTS * 16, NP2), BF),
                pltpu.VMEM((2, ROTS * WIDE // 128, 8, 128), F32),
                pltpu.VMEM((ROTS * 16, 128), F32),
                pltpu.VMEM((16, 128), F32),
            ],
            cost_estimate=cost(6),
            compiler_params=pltpu.CompilerParams(vmem_limit_bytes=14 * MB),
        )(jnp.stack([x_hi, x_lo, y, z]), first, second, mine, theirs, own, oth)

    order = (2, 3, 1)
    sends = (to_x, to_y)
    with jax.named_scope("reduce1"):
        arrived = [[parts[0]], [parts[4]]]
        for s in order:
            for n in range(2):
                arrived[n].append(sends[n](parts[4 * n + s], s))
        firsts = pl.pallas_call(
            first_sum_kernel,
            out_shape=([jax.ShapeDtypeStruct((8, PROWS, 128), F32)] + [jax.ShapeDtypeStruct((8, PROWS, 128), BF)] * 3) * 2,
            in_specs=[VMEM] * 8,
            out_specs=[VMEM] * 8,
            compiler_params=pltpu.CompilerParams(vmem_limit_bytes=4 * MB),
        )(*[piece for pair in zip(*arrived) for piece in pair])
    with jax.named_scope("reduce2"):
        pieces = [[firsts[0]], [firsts[4]]]
        for s in order:
            for n in range(2):
                pieces[n].append(sends[1 - n](firsts[4 * n + s], s))
        slots = pl.pallas_call(
            second_sum_kernel,
            out_shape=[jax.ShapeDtypeStruct((2 * PROWS, 128), F32)] * 8,
            in_specs=[VMEM] * 8,
            out_specs=[VMEM] * 8,
            compiler_params=pltpu.CompilerParams(vmem_limit_bytes=4 * MB),
        )(*[piece for pair in zip(*pieces) for piece in pair])
    with jax.named_scope("reduce3"):
        owned = [slots[0]] + [to_z(slots[s], s) for s in (4, 3, 5, 2, 6, 1, 7)]

    with jax.named_scope("means"):
        d = (x_lo * 4 + y) * 8 + z
        return pl.pallas_call(
            final_kernel,
            out_shape=jax.ShapeDtypeStruct((8, 1920), F32),
            in_specs=[SMEM] + [VMEM] * 9,
            out_specs=VMEM,
            compiler_params=pltpu.CompilerParams(vmem_limit_bytes=4 * MB),
        )(d.reshape(1), sigma2.reshape(16, 128), *owned)


def solution(mesh):
    fine = Mesh(mesh.devices.reshape(2, 4, 8, 2, 2), ("x_lo", "y", "z", "x_hi", "core"))
    dom, grp = ("x_lo", "y", "z"), ("x_hi", "core")
    return jax.shard_map(
        local,
        mesh=fine,
        in_specs=(P(dom + grp, None), P(dom + grp), P(None, dom + grp), P(grp, None, None), P(), P()),
        out_specs=P(grp, dom),
        check_vma=False,
    )
```

```python
import functools

import jax
import jax.numpy as jnp
from jax import lax
from jax.experimental import pallas as pl
from jax.experimental.pallas import tpu as pltpu
from jax.sharding import Mesh, PartitionSpec as P

HALFWIN = 6
BOX = 128
KXW = 32
KYW = 64
TWO_PI = 6.283185307179586
REG_WEIGHT = 0.05

F = 2048
WIDE = 2 * F
ROTS = 30
ROWS = ROTS * 8
NP = 448
PAD = 512
NP2 = 2 * PAD
LANES = NP2 // 128
DIRECT = 1024
QUART = 512
ZBASE = DIRECT + 4 * QUART
UNITS = 15
PART = 8
PROWS = PART * 8

BF = jnp.bfloat16
F32 = jnp.float32
MB = 1024 * 1024


def turn_cos_sin(turns):
    quarter = jnp.floor(4.0 * turns + 0.5)
    x = TWO_PI * (turns - 0.25 * quarter)
    q = quarter - 4.0 * jnp.floor(0.25 * quarter)
    x2 = x * x
    s = x * (1.0 + x2 * (-1.0 / 6 + x2 * (1.0 / 120 + x2 * (-1.0 / 5040 + x2 * (1.0 / 362880)))))
    c = 1.0 + x2 * (-0.5 + x2 * (1.0 / 24 + x2 * (-1.0 / 720 + x2 * (1.0 / 40320))))
    odd = (q == 1.0) | (q == 3.0)
    cos = jnp.where(odd, s, c)
    sin = jnp.where(odd, c, s)
    cos = jnp.where((q == 1.0) | (q == 2.0), -cos, cos)
    sin = jnp.where(q >= 2.0, -sin, sin)
    return cos, sin


SHIFT_ROWS = 64
SHIFT_STEPS = NP // SHIFT_ROWS


def shift_kernel(meta_ref, p_ref, o_ref, held_ref, turned_ref, sems):
    def copy(step):
        rows = pl.ds(step * SHIFT_ROWS, SHIFT_ROWS)
        return pltpu.make_async_copy(p_ref.at[rows, :], held_ref.at[rows, :], sems.at[step])

    for step in range(SHIFT_STEPS):
        copy(step).start()
    turned_ref[...] = jnp.transpose(meta_ref[...])
    lane = lax.broadcasted_iota(jnp.int32, (SHIFT_ROWS, 128), 1)
    kx = (lane & (KXW - 1)).astype(F32)
    ky = ((lane >> 5) - KYW // 2).astype(F32)
    for step in range(SHIFT_STEPS):
        rows = slice(step * SHIFT_ROWS, (step + 1) * SHIFT_ROWS)
        sx = turned_ref[rows, 0:1]
        sy = turned_ref[rows, 1:2]
        c, s = turn_cos_sin((sx * kx + sy * ky) * (1.0 / BOX))
        dc, ds = turn_cos_sin(jnp.broadcast_to(sy * (128 // KXW), (SHIFT_ROWS, 128)) * (1.0 / BOX))
        copy(step).wait()
        for b in range(F // 128):
            re = held_ref[rows, b * 128 : (b + 1) * 128].astype(F32)
            im = held_ref[rows, F + b * 128 : F + (b + 1) * 128].astype(F32)
            o_ref[rows, b * 128 : (b + 1) * 128] = (re * c + im * s).astype(BF)
            o_ref[rows, F + b * 128 : F + (b + 1) * 128] = (im * c - re * s).astype(BF)
            c, s = c * dc - s * ds, s * dc + c * ds


def shift_particles(particles, meta, megabytes):
    return pl.pallas_call(
        shift_kernel,
        out_shape=jax.ShapeDtypeStruct((NP, WIDE), BF),
        in_specs=[VMEM, pl.BlockSpec(memory_space=pl.ANY)],
        out_specs=VMEM,
        scratch_shapes=[
            pltpu.VMEM((NP, WIDE), BF),
            pltpu.VMEM((PAD, 8), F32),
            pltpu.SemaphoreType.DMA((SHIFT_STEPS,)),
        ],
        cost_estimate=cost(5),
        compiler_params=pltpu.CompilerParams(vmem_limit_bytes=megabytes * MB),
    )(meta, particles)


def weigh(own_ref, oth_ref, inv_ref, w_ref):
    width = 512
    for start in range(0, WIDE, width):
        cols = slice(start, start + width)
        inv = inv_ref[:, cols]
        w_ref[0:NP, cols] = (own_ref[:, cols].astype(F32) * inv).astype(BF)
        w_ref[PAD : PAD + NP, cols] = (oth_ref[:, cols].astype(F32) * inv).astype(BF)
        w_ref[NP:PAD, cols] = jnp.zeros((PAD - NP, width), BF)
        w_ref[PAD + NP :, cols] = jnp.zeros((PAD - NP, width), BF)


def correlate(w_ref, inv_ref, pieces, acc_ref, begun=None):
    energy = jnp.zeros((ROWS, 128), F32)
    for piece, base, width in pieces:
        for start in range(0, piece.shape[1], width):
            cols = pl.ds(base + start, width)
            inv = inv_ref[:, cols]
            part = lax.dot_general(
                piece[:, start : start + width],
                w_ref[:, cols],
                (((1,), (1,)), ((), ())),
                preferred_element_type=F32,
            )
            for j in range(LANES):
                block = part[:, j * 128 : (j + 1) * 128]
                acc_ref[j] = block if begun is None else begun[j] + block
            begun = acc_ref
            for lanes in range(0, width, 128):
                v = piece[:, start + lanes : start + lanes + 128].astype(F32)
                energy = energy + v * v * inv[:, lanes : lanes + 128]
    return energy


def offset(bias_ref, energy):
    return bias_ref[...] - 0.5 * jnp.sum(energy, axis=1, keepdims=True)


def exponentiate(acc_ref, bias, metas, out_ref, j):
    half = LANES // 2
    rot = metas[j // half][2:3, (j % half) * 128 : (j % half + 1) * 128]
    low = jnp.full((8, 128), -jnp.inf, F32)
    top = low
    for r in range(ROTS):
        rows = slice(r * 8, r * 8 + 8)
        score = jnp.where(inside_window(r, rot), acc_ref[j, rows, :] + bias[rows, :], low)
        out_ref[j, rows, :] = score
        top = jnp.maximum(top, score)
    top = jnp.max(top, axis=0, keepdims=True)
    mass = jnp.zeros((8, 128), F32)
    for r in range(ROTS):
        rows = slice(r * 8, r * 8 + 8)
        raised = jnp.exp(out_ref[j, rows, :] - top)
        out_ref[j, rows, :] = raised
        mass = mass + raised
    return top, jnp.sum(mass, axis=0, keepdims=True)


def inside_window(rotation, rot):
    return jnp.abs(jnp.abs(float(rotation) - rot) - ROTS / 2) >= ROTS / 2 - HALFWIN


def own_kernel(
    where_ref, own_ref, oth_ref, inv_ref, bias_ref, refs_ref, meta_a, meta_b, q0, z0,
    w_ref, e_ref, stats_ref, begun_ref, energy_ref, acc_ref,
):
    weigh(own_ref, oth_ref, inv_ref, w_ref)
    bias = offset(bias_ref, correlate(w_ref, inv_ref, [(refs_ref, 0, 512)], acc_ref))
    pieces = [(q, pl.multiple_of(where_ref[s], 128), QUART) for s, q in enumerate((q0, z0))]
    energy_ref[...] = correlate(w_ref, inv_ref, pieces, begun_ref)
    row = lax.broadcasted_iota(jnp.int32, (8, 128), 0)
    for j in range(LANES):
        top, mass = exponentiate(acc_ref, bias, (meta_a, meta_b), e_ref, j)
        stats_ref[:, j * 128 : (j + 1) * 128] = jnp.where(row == 0, top, mass)


def other_kernel(
    where_ref, w_ref, inv_ref, bias_ref, meta_a, meta_b, first_ref, begun_ref, energy_ref, d_ref, q1, q2, q3, z1,
    e_ref, stats_ref, acc_ref,
):
    pieces = [(d_ref, 0, 512)]
    for s, q in enumerate((q1, q2, q3, z1)):
        pieces.append((q, pl.multiple_of(where_ref[s], 128), QUART))
    bias = offset(bias_ref, energy_ref[...] + correlate(w_ref, inv_ref, pieces, acc_ref, begun_ref))
    row = lax.broadcasted_iota(jnp.int32, (8, 128), 0)
    for j in range(LANES):
        lanes = slice(j * 128, (j + 1) * 128)
        top_b, mass_b = exponentiate(acc_ref, bias, (meta_a, meta_b), e_ref, j)
        top_a, mass_a = first_ref[0:1, lanes], first_ref[1:2, lanes]
        top = jnp.maximum(top_a, top_b)
        mass = mass_a * jnp.exp(top_a - top) + mass_b * jnp.exp(top_b - top)
        tops = jnp.where(row == 2, top_a, top_b)
        stats_ref[:, lanes] = jnp.where(row == 0, top, jnp.where(row == 1, mass, tops))


def sums_kernel(where_ref, first_ref, second_ref, mine_ref, theirs_ref, own_ref, oth_ref, *refs):
    parts, (p_ref, acc_ref, mass_ref, extra_ref) = refs[:8], refs[8:]
    x_hi, x_lo, y, z = where_ref[0], where_ref[1], where_ref[2], where_ref[3]
    mass_ref[...] = jnp.zeros_like(mass_ref)
    for j in range(LANES):
        lanes = slice(j * 128, (j + 1) * 128)
        facing = (j + LANES // 2) % LANES
        crossed = slice(facing * 128, (facing + 1) * 128)
        top_a, mass_a = mine_ref[0:1, lanes], mine_ref[1:2, lanes]
        top_b, mass_b = theirs_ref[0:1, crossed], theirs_ref[1:2, crossed]
        top = jnp.maximum(top_a, top_b)
        scale = 1.0 / (mass_a * jnp.exp(top_a - top) + mass_b * jnp.exp(top_b - top))
        scale_a = jnp.exp(mine_ref[2:3, lanes] - top) * scale
        scale_b = jnp.exp(mine_ref[3:4, lanes] - top) * scale
        if j % (LANES // 2) == LANES // 2 - 1:
            used = lax.broadcasted_iota(jnp.int32, (1, 128), 1) < 128 - (PAD - NP)
            scale_a = jnp.where(used, scale_a, 0.0)
            scale_b = jnp.where(used, scale_b, 0.0)
        for r in range(ROTS):
            rows = slice(r * 8, r * 8 + 8)
            p = first_ref[j, rows, :] * scale_a
            q = second_ref[j, rows, :] * scale_b
            low = jnp.where(x_hi == 0, p, q)
            high = jnp.where(x_hi == 0, q, p)
            both = jnp.concatenate([low, high], axis=0)
            p_ref[r * 16 : (r + 1) * 16, lanes] = both.astype(BF)
            mass_ref[r * 16 : (r + 1) * 16, :] += both
    lane = lax.broadcasted_iota(jnp.int32, (16, 128), 1)
    totals = jnp.zeros((16, 128), F32)
    for r in range(ROTS):
        row_sum = jnp.sum(mass_ref[r * 16 : (r + 1) * 16, :], axis=1, keepdims=True)
        totals = jnp.where(lane == r, row_sum, totals)
    coarse = totals.astype(BF).astype(F32)
    extra_ref[...] = jnp.where(lane < 32, coarse, pltpu.roll(totals - coarse, 32, 1))
    width = 512
    for cb in range(WIDE // width):
        cols = slice(cb * width, (cb + 1) * width)
        part = jnp.dot(p_ref[:, 0:NP], own_ref[:, cols], preferred_element_type=F32) + jnp.dot(
            p_ref[:, PAD : PAD + NP], oth_ref[:, cols], preferred_element_type=F32
        )
        for j in range(width // 128):
            fb = cb * (width // 128) + j
            for r in range(ROTS):
                for kx in range(2):
                    row = r * 16 + kx * 8
                    acc_ref[kx, 32 * r + fb] = part[row : row + 8, j * 128 : (j + 1) * 128]

    def place(sz, carry):
        dest_z = (z + sz) & 7
        for sx in range(4):
            kx, dest_x = x_hi ^ (sx >> 1), x_lo ^ (sx & 1)
            for sy in range(4):
                base = ((dest_x * 4 + ((y + sy) & 3)) * 8 + dest_z) * UNITS

                def tile(i):
                    if i == UNITS:
                        return extra_ref[pl.ds(pl.multiple_of(kx * 8, 8), 8), :]
                    return acc_ref[kx, base + i]

                for i in range(0, UNITS + 1, 2):
                    both = jnp.concatenate([tile(i), tile(i + 1)], axis=0)
                    number = i // PART
                    hop, rest = (sx, sy) if number % 2 == 0 else (sy, sx)
                    row = (i % PART) * 8
                    part_ref = parts[number * 4 + hop]
                    part_ref[rest, sz, row : row + 16, :] = both.astype(part_ref.dtype)
        return carry

    lax.fori_loop(0, 8, place, 0)


def first_sum_kernel(*refs):
    for half in range(2):
        arrived = refs[half:8:2]
        for rest in range(4):
            for z in range(8):
                total = arrived[0][rest, z].astype(F32)
                for ref in arrived[1:]:
                    total = total + ref[rest, z].astype(F32)
                out_ref = refs[8 + 4 * half + rest]
                out_ref[z] = total.astype(out_ref.dtype)


def second_sum_kernel(*refs):
    for half in range(2):
        arrived = refs[half:8:2]
        for z in range(8):
            total = arrived[0][z]
            for ref in arrived[1:]:
                total = total + ref[z].astype(F32)
            refs[8 + z][half * PROWS : (half + 1) * PROWS, :] = total


def final_kernel(where_ref, sigma_ref, *refs):
    d = where_ref[0]
    out_ref = refs[8]

    def rows_of(i):
        rows = slice(i * 8, i * 8 + 8)
        total = refs[0][rows, :]
        for ref in refs[1:8]:
            total = total + ref[rows, :]
        return total

    mass = rows_of(UNITS)
    mass = mass + pltpu.roll(mass, 128 - 32, 1)
    lane = lax.broadcasted_iota(jnp.int32, (8, 128), 1)
    for i in range(UNITS):
        unit = d * UNITS + i
        rotation = unit >> 5
        here = jnp.sum(jnp.where(lane == rotation, mass, 0.0), axis=1, keepdims=True)
        noise = sigma_ref[pl.ds(unit & 15, 1), :]
        out_ref[:, i * 128 : (i + 1) * 128] = rows_of(i) / (here + REG_WEIGHT * noise)


def cost(micros):
    return pl.CostEstimate(flops=int(micros * 1e9), bytes_accessed=0, transcendentals=0)


SMEM = pl.BlockSpec(memory_space=pltpu.SMEM)
VMEM = pl.BlockSpec(memory_space=pltpu.VMEM)


def ring(size, step):
    return [((i + step) % size, i) for i in range(size)]


X = ("x_lo", "x_hi")
X_SWAP = [(0, 3), (1, 2), (2, 1), (3, 0)]
CORE_SWAP = [(0, 1), (1, 0)]


def from_y(value, step):
    return lax.ppermute(value, "y", ring(4, step))


def to_x(value, flips):
    return lax.ppermute(value, X, [(i, i ^ (flips >> 1) ^ ((flips & 1) << 1)) for i in range(4)])


def to_y(value, step):
    return lax.ppermute(value, "y", ring(4, -step))


def to_z(value, step):
    return lax.ppermute(value, "z", ring(8, -step))


def local(particles, rot_center, shifts, references, class_prior, sigma2):
    x_lo, y, z = lax.axis_index("x_lo"), lax.axis_index("y"), lax.axis_index("z")
    x_hi, core = lax.axis_index("x_hi"), lax.axis_index("core")
    refs = jnp.transpose(references, (1, 0, 2)).reshape(ROWS, WIDE)

    zp = z & 1
    with jax.named_scope("swap"):
        raw = lax.ppermute(particles, "core", CORE_SWAP)
    with jax.named_scope("references"):
        quarter = lax.dynamic_slice_in_dim(refs, DIRECT + y * QUART, QUART, 1)
        half = lax.dynamic_slice_in_dim(refs, ZBASE + zp * QUART, QUART, 1)
        quarter, half, shifts, rot_center = lax.optimization_barrier((quarter, half, shifts, rot_center))
        crossed = lax.ppermute(quarter, X, X_SWAP)
    with jax.named_scope("swap"):
        meta = jnp.concatenate([shifts, rot_center[None]]).astype(F32)
        meta = jnp.pad(meta, ((0, 5), (0, PAD - NP)))
        meta_oth = lax.ppermute(meta, "core", CORE_SWAP)
    with jax.named_scope("references"):
        half, meta_oth = lax.optimization_barrier((half, meta_oth))
        z_crossed = lax.ppermute(half, X, X_SWAP)
        later_refs, meta = lax.optimization_barrier((refs, meta))
        direct, meta_oth = lax.optimization_barrier((later_refs[:, :DIRECT], meta_oth))
        direct = lax.ppermute(direct, X, X_SWAP)
    with jax.named_scope("shift"):
        own = shift_particles(particles, meta, 48)
        raw, crossed = lax.optimization_barrier((raw, crossed))
        oth = shift_particles(raw, meta_oth, 12)
    with jax.named_scope("references"):
        quarters = [from_y(crossed, s) for s in (1, 2, 3)]
        z_crossed, oth = lax.optimization_barrier((z_crossed, oth))
        z_other = lax.ppermute(z_crossed, "z", [(i, i ^ 1) for i in range(8)])
    inv = (1.0 / jnp.concatenate([sigma2, sigma2])).reshape(1, WIDE)
    log_prior = jnp.log(class_prior).reshape(2, 2, 8)
    own_bias = jnp.tile(log_prior[x_hi, core], ROTS).reshape(ROWS, 1)
    oth_bias = jnp.tile(log_prior[1 - x_hi, core], ROTS).reshape(ROWS, 1)

    raised = jax.ShapeDtypeStruct((LANES, ROWS, 128), F32)
    stats = jax.ShapeDtypeStruct((8, NP2), F32)
    with jax.named_scope("scores"):
        offsets = [DIRECT + ((y + s) & 3) * QUART for s in range(4)]
        z_offsets = [ZBASE + zp * QUART, ZBASE + (1 - zp) * QUART]
        energies = jax.ShapeDtypeStruct((ROWS, 128), F32)
        weighted, first, first_stats, begun, energy = pl.pallas_call(
            own_kernel,
            out_shape=[jax.ShapeDtypeStruct((NP2, WIDE), BF), raised, stats, raised, energies],
            in_specs=[SMEM] + [VMEM] * 9,
            out_specs=[VMEM] * 5,
            scratch_shapes=[pltpu.VMEM((LANES, ROWS, 128), F32)],
            cost_estimate=cost(7),
            compiler_params=pltpu.CompilerParams(vmem_limit_bytes=6 * MB),
        )(jnp.stack([offsets[0], z_offsets[0]]), own, oth, inv, own_bias, refs, meta, meta_oth, crossed, z_crossed)
        second, mine = pl.pallas_call(
            other_kernel,
            out_shape=[raised, stats],
            in_specs=[SMEM] + [VMEM] * 13,
            out_specs=[VMEM] * 2,
            scratch_shapes=[pltpu.VMEM((LANES, ROWS, 128), F32)],
            cost_estimate=cost(5),
            compiler_params=pltpu.CompilerParams(vmem_limit_bytes=6 * MB),
        )(
            jnp.stack(offsets[1:] + z_offsets[1:]), weighted, inv, oth_bias, meta, meta_oth, first_stats,
            begun, energy, direct, *quarters, z_other,
        )
        theirs = lax.ppermute(mine, "core", CORE_SWAP)

    with jax.named_scope("sums"):
        parts = pl.pallas_call(
            sums_kernel,
            out_shape=([jax.ShapeDtypeStruct((4, 8, PROWS, 128), F32)] + [jax.ShapeDtypeStruct((4, 8, PROWS, 128), BF)] * 3) * 2,
            in_specs=[SMEM] + [VMEM] * 6,
            out_specs=[VMEM] * 8,
            scratch_shapes=[
                pltpu.VMEM((ROTS * 16, NP2), BF),
                pltpu.VMEM((2, ROTS * WIDE // 128, 8, 128), F32),
                pltpu.VMEM((ROTS * 16, 128), F32),
                pltpu.VMEM((16, 128), F32),
            ],
            cost_estimate=cost(6),
            compiler_params=pltpu.CompilerParams(vmem_limit_bytes=14 * MB),
        )(jnp.stack([x_hi, x_lo, y, z]), first, second, mine, theirs, own, oth)

    order = (2, 3, 1)
    sends = (to_x, to_y)
    with jax.named_scope("reduce1"):
        arrived = [[parts[0]], [parts[4]]]
        for s in order:
            for n in range(2):
                arrived[n].append(sends[n](parts[4 * n + s], s))
        firsts = pl.pallas_call(
            first_sum_kernel,
            out_shape=([jax.ShapeDtypeStruct((8, PROWS, 128), F32)] + [jax.ShapeDtypeStruct((8, PROWS, 128), BF)] * 3) * 2,
            in_specs=[VMEM] * 8,
            out_specs=[VMEM] * 8,
            compiler_params=pltpu.CompilerParams(vmem_limit_bytes=4 * MB),
        )(*[piece for pair in zip(*arrived) for piece in pair])
    with jax.named_scope("reduce2"):
        pieces = [[firsts[0]], [firsts[4]]]
        for s in order:
            for n in range(2):
                pieces[n].append(sends[1 - n](firsts[4 * n + s], s))
        slots = pl.pallas_call(
            second_sum_kernel,
            out_shape=[jax.ShapeDtypeStruct((2 * PROWS, 128), F32)] * 8,
            in_specs=[VMEM] * 8,
            out_specs=[VMEM] * 8,
            compiler_params=pltpu.CompilerParams(vmem_limit_bytes=4 * MB),
        )(*[piece for pair in zip(*pieces) for piece in pair])
    with jax.named_scope("reduce3"):
        owned = [slots[0]] + [to_z(slots[s], s) for s in (4, 3, 5, 2, 6, 1, 7)]

    with jax.named_scope("means"):
        d = (x_lo * 4 + y) * 8 + z
        return pl.pallas_call(
            final_kernel,
            out_shape=jax.ShapeDtypeStruct((8, 1920), F32),
            in_specs=[SMEM] + [VMEM] * 9,
            out_specs=VMEM,
            compiler_params=pltpu.CompilerParams(vmem_limit_bytes=4 * MB),
        )(d.reshape(1), sigma2.reshape(16, 128), *owned)


def solution(mesh):
    fine = Mesh(mesh.devices.reshape(2, 4, 8, 2, 2), ("x_lo", "y", "z", "x_hi", "core"))
    dom, grp = ("x_lo", "y", "z"), ("x_hi", "core")
    return jax.shard_map(
        local,
        mesh=fine,
        in_specs=(P(dom + grp, None), P(dom + grp), P(None, dom + grp), P(grp, None, None), P(), P()),
        out_specs=P(grp, dom),
        check_vma=False,
    )
```

```python
import functools

import jax
import jax.numpy as jnp
from jax import lax
from jax.experimental import pallas as pl
from jax.experimental.pallas import tpu as pltpu
from jax.sharding import Mesh, PartitionSpec as P

HALFWIN = 6
BOX = 128
KXW = 32
KYW = 64
TWO_PI = 6.283185307179586
REG_WEIGHT = 0.05

F = 2048
WIDE = 2 * F
ROTS = 30
ROWS = ROTS * 8
NP = 448
PAD = 512
NP2 = 2 * PAD
LANES = NP2 // 128
DIRECT = 1024
QUART = 512
ZBASE = DIRECT + 4 * QUART
UNITS = 15
PART = 8
PROWS = PART * 8

BF = jnp.bfloat16
F32 = jnp.float32
MB = 1024 * 1024


def turn_cos_sin(turns):
    quarter = jnp.floor(4.0 * turns + 0.5)
    x = TWO_PI * (turns - 0.25 * quarter)
    q = quarter - 4.0 * jnp.floor(0.25 * quarter)
    x2 = x * x
    s = x * (1.0 + x2 * (-1.0 / 6 + x2 * (1.0 / 120 + x2 * (-1.0 / 5040 + x2 * (1.0 / 362880)))))
    c = 1.0 + x2 * (-0.5 + x2 * (1.0 / 24 + x2 * (-1.0 / 720 + x2 * (1.0 / 40320))))
    odd = (q == 1.0) | (q == 3.0)
    cos = jnp.where(odd, s, c)
    sin = jnp.where(odd, c, s)
    cos = jnp.where((q == 1.0) | (q == 2.0), -cos, cos)
    sin = jnp.where(q >= 2.0, -sin, sin)
    return cos, sin


SHIFT_ROWS = 64
SHIFT_STEPS = NP // SHIFT_ROWS


def shift_kernel(meta_ref, p_ref, o_ref, held_ref, turned_ref, sems):
    def copy(step):
        rows = pl.ds(step * SHIFT_ROWS, SHIFT_ROWS)
        return pltpu.make_async_copy(p_ref.at[rows, :], held_ref.at[rows, :], sems.at[step])

    for step in range(SHIFT_STEPS):
        copy(step).start()
    turned_ref[...] = jnp.transpose(meta_ref[...])
    lane = lax.broadcasted_iota(jnp.int32, (SHIFT_ROWS, 128), 1)
    kx = (lane & (KXW - 1)).astype(F32)
    ky = ((lane >> 5) - KYW // 2).astype(F32)
    for step in range(SHIFT_STEPS):
        rows = slice(step * SHIFT_ROWS, (step + 1) * SHIFT_ROWS)
        sx = turned_ref[rows, 0:1]
        sy = turned_ref[rows, 1:2]
        c, s = turn_cos_sin((sx * kx + sy * ky) * (1.0 / BOX))
        dc, ds = turn_cos_sin(jnp.broadcast_to(sy * (128 // KXW), (SHIFT_ROWS, 128)) * (1.0 / BOX))
        copy(step).wait()
        for b in range(F // 128):
            re = held_ref[rows, b * 128 : (b + 1) * 128].astype(F32)
            im = held_ref[rows, F + b * 128 : F + (b + 1) * 128].astype(F32)
            o_ref[rows, b * 128 : (b + 1) * 128] = (re * c + im * s).astype(BF)
            o_ref[rows, F + b * 128 : F + (b + 1) * 128] = (im * c - re * s).astype(BF)
            c, s = c * dc - s * ds, s * dc + c * ds


def shift_particles(particles, meta, megabytes):
    return pl.pallas_call(
        shift_kernel,
        out_shape=jax.ShapeDtypeStruct((NP, WIDE), BF),
        in_specs=[VMEM, pl.BlockSpec(memory_space=pl.ANY)],
        out_specs=VMEM,
        scratch_shapes=[
            pltpu.VMEM((NP, WIDE), BF),
            pltpu.VMEM((PAD, 8), F32),
            pltpu.SemaphoreType.DMA((SHIFT_STEPS,)),
        ],
        cost_estimate=cost(5),
        compiler_params=pltpu.CompilerParams(vmem_limit_bytes=megabytes * MB),
    )(meta, particles)


def weigh(own_ref, oth_ref, inv_ref, w_ref):
    width = 512
    for start in range(0, WIDE, width):
        cols = slice(start, start + width)
        inv = inv_ref[:, cols]
        w_ref[0:NP, cols] = (own_ref[:, cols].astype(F32) * inv).astype(BF)
        w_ref[PAD : PAD + NP, cols] = (oth_ref[:, cols].astype(F32) * inv).astype(BF)
        w_ref[NP:PAD, cols] = jnp.zeros((PAD - NP, width), BF)
        w_ref[PAD + NP :, cols] = jnp.zeros((PAD - NP, width), BF)


def correlate(w_ref, inv_ref, pieces, acc_ref, begun=None):
    energy = jnp.zeros((ROWS, 128), F32)
    for piece, base, width in pieces:
        for start in range(0, piece.shape[1], width):
            cols = pl.ds(base + start, width)
            inv = inv_ref[:, cols]
            part = lax.dot_general(
                piece[:, start : start + width],
                w_ref[:, cols],
                (((1,), (1,)), ((), ())),
                preferred_element_type=F32,
            )
            for j in range(LANES):
                block = part[:, j * 128 : (j + 1) * 128]
                acc_ref[j] = block if begun is None else begun[j] + block
            begun = acc_ref
            for lanes in range(0, width, 128):
                v = piece[:, start + lanes : start + lanes + 128].astype(F32)
                energy = energy + v * v * inv[:, lanes : lanes + 128]
    return energy


def offset(bias_ref, energy):
    return bias_ref[...] - 0.5 * jnp.sum(energy, axis=1, keepdims=True)


def exponentiate(acc_ref, bias, metas, out_ref, j):
    half = LANES // 2
    rot = metas[j // half][2:3, (j % half) * 128 : (j % half + 1) * 128]
    low = jnp.full((8, 128), -jnp.inf, F32)
    top = low
    for r in range(ROTS):
        rows = slice(r * 8, r * 8 + 8)
        score = jnp.where(inside_window(r, rot), acc_ref[j, rows, :] + bias[rows, :], low)
        out_ref[j, rows, :] = score
        top = jnp.maximum(top, score)
    top = jnp.max(top, axis=0, keepdims=True)
    mass = jnp.zeros((8, 128), F32)
    for r in range(ROTS):
        rows = slice(r * 8, r * 8 + 8)
        raised = jnp.exp(out_ref[j, rows, :] - top)
        out_ref[j, rows, :] = raised
        mass = mass + raised
    return top, jnp.sum(mass, axis=0, keepdims=True)


def inside_window(rotation, rot):
    return jnp.abs(jnp.abs(float(rotation) - rot) - ROTS / 2) >= ROTS / 2 - HALFWIN


def own_kernel(
    where_ref, own_ref, oth_ref, inv_ref, bias_ref, refs_ref, meta_a, meta_b, q0, z0,
    w_ref, e_ref, stats_ref, begun_ref, energy_ref, acc_ref,
):
    weigh(own_ref, oth_ref, inv_ref, w_ref)
    bias = offset(bias_ref, correlate(w_ref, inv_ref, [(refs_ref, 0, 512)], acc_ref))
    pieces = [(q, pl.multiple_of(where_ref[s], 128), QUART) for s, q in enumerate((q0, z0))]
    energy_ref[...] = correlate(w_ref, inv_ref, pieces, begun_ref)
    row = lax.broadcasted_iota(jnp.int32, (8, 128), 0)
    for j in range(LANES):
        top, mass = exponentiate(acc_ref, bias, (meta_a, meta_b), e_ref, j)
        stats_ref[:, j * 128 : (j + 1) * 128] = jnp.where(row == 0, top, mass)


def other_kernel(
    where_ref, w_ref, inv_ref, bias_ref, meta_a, meta_b, first_ref, begun_ref, energy_ref, d_ref, q1, q2, q3, z1,
    e_ref, stats_ref, acc_ref,
):
    pieces = [(d_ref, 0, 512)]
    for s, q in enumerate((q1, q2, q3, z1)):
        pieces.append((q, pl.multiple_of(where_ref[s], 128), QUART))
    bias = offset(bias_ref, energy_ref[...] + correlate(w_ref, inv_ref, pieces, acc_ref, begun_ref))
    row = lax.broadcasted_iota(jnp.int32, (8, 128), 0)
    for j in range(LANES):
        lanes = slice(j * 128, (j + 1) * 128)
        top_b, mass_b = exponentiate(acc_ref, bias, (meta_a, meta_b), e_ref, j)
        top_a, mass_a = first_ref[0:1, lanes], first_ref[1:2, lanes]
        top = jnp.maximum(top_a, top_b)
        mass = mass_a * jnp.exp(top_a - top) + mass_b * jnp.exp(top_b - top)
        tops = jnp.where(row == 2, top_a, top_b)
        stats_ref[:, lanes] = jnp.where(row == 0, top, jnp.where(row == 1, mass, tops))


def sums_kernel(where_ref, first_ref, second_ref, mine_ref, theirs_ref, own_ref, oth_ref, *refs):
    parts, (p_ref, acc_ref, mass_ref, extra_ref) = refs[:8], refs[8:]
    x_hi, x_lo, y, z = where_ref[0], where_ref[1], where_ref[2], where_ref[3]
    mass_ref[...] = jnp.zeros_like(mass_ref)
    for j in range(LANES):
        lanes = slice(j * 128, (j + 1) * 128)
        facing = (j + LANES // 2) % LANES
        crossed = slice(facing * 128, (facing + 1) * 128)
        top_a, mass_a = mine_ref[0:1, lanes], mine_ref[1:2, lanes]
        top_b, mass_b = theirs_ref[0:1, crossed], theirs_ref[1:2, crossed]
        top = jnp.maximum(top_a, top_b)
        scale = 1.0 / (mass_a * jnp.exp(top_a - top) + mass_b * jnp.exp(top_b - top))
        scale_a = jnp.exp(mine_ref[2:3, lanes] - top) * scale
        scale_b = jnp.exp(mine_ref[3:4, lanes] - top) * scale
        if j % (LANES // 2) == LANES // 2 - 1:
            used = lax.broadcasted_iota(jnp.int32, (1, 128), 1) < 128 - (PAD - NP)
            scale_a = jnp.where(used, scale_a, 0.0)
            scale_b = jnp.where(used, scale_b, 0.0)
        for r in range(ROTS):
            rows = slice(r * 8, r * 8 + 8)
            p = first_ref[j, rows, :] * scale_a
            q = second_ref[j, rows, :] * scale_b
            low = jnp.where(x_hi == 0, p, q)
            high = jnp.where(x_hi == 0, q, p)
            both = jnp.concatenate([low, high], axis=0)
            p_ref[r * 16 : (r + 1) * 16, lanes] = both.astype(BF)
            mass_ref[r * 16 : (r + 1) * 16, :] += both
    lane = lax.broadcasted_iota(jnp.int32, (16, 128), 1)
    totals = jnp.zeros((16, 128), F32)
    for r in range(ROTS):
        row_sum = jnp.sum(mass_ref[r * 16 : (r + 1) * 16, :], axis=1, keepdims=True)
        totals = jnp.where(lane == r, row_sum, totals)
    coarse = totals.astype(BF).astype(F32)
    extra_ref[...] = jnp.where(lane < 32, coarse, pltpu.roll(totals - coarse, 32, 1))
    width = 512
    for cb in range(WIDE // width):
        cols = slice(cb * width, (cb + 1) * width)
        part = jnp.dot(p_ref[:, 0:NP], own_ref[:, cols], preferred_element_type=F32) + jnp.dot(
            p_ref[:, PAD : PAD + NP], oth_ref[:, cols], preferred_element_type=F32
        )
        for j in range(width // 128):
            fb = cb * (width // 128) + j
            for r in range(ROTS):
                for kx in range(2):
                    row = r * 16 + kx * 8
                    acc_ref[kx, 32 * r + fb] = part[row : row + 8, j * 128 : (j + 1) * 128]

    def place(sz, carry):
        dest_z = (z + sz) & 7
        for sx in range(4):
            kx, dest_x = x_hi ^ (sx >> 1), x_lo ^ (sx & 1)
            for sy in range(4):
                base = ((dest_x * 4 + ((y + sy) & 3)) * 8 + dest_z) * UNITS

                def tile(i):
                    if i == UNITS:
                        return extra_ref[pl.ds(pl.multiple_of(kx * 8, 8), 8), :]
                    return acc_ref[kx, base + i]

                for i in range(0, UNITS + 1, 2):
                    both = jnp.concatenate([tile(i), tile(i + 1)], axis=0)
                    number = i // PART
                    hop, rest = (sx, sy) if number % 2 == 0 else (sy, sx)
                    row = (i % PART) * 8
                    part_ref = parts[number * 4 + hop]
                    part_ref[rest, sz, row : row + 16, :] = both.astype(part_ref.dtype)
        return carry

    lax.fori_loop(0, 8, place, 0)


def first_sum_kernel(*refs):
    for half in range(2):
        arrived = refs[half:8:2]
        for rest in range(4):
            for z in range(8):
                total = arrived[0][rest, z].astype(F32)
                for ref in arrived[1:]:
                    total = total + ref[rest, z].astype(F32)
                out_ref = refs[8 + 4 * half + rest]
                out_ref[z] = total.astype(out_ref.dtype)


def second_sum_kernel(*refs):
    for half in range(2):
        arrived = refs[half:8:2]
        for z in range(8):
            total = arrived[0][z]
            for ref in arrived[1:]:
                total = total + ref[z].astype(F32)
            refs[8 + z][half * PROWS : (half + 1) * PROWS, :] = total


def final_kernel(where_ref, sigma_ref, *refs):
    d = where_ref[0]
    out_ref = refs[8]

    def rows_of(i):
        rows = slice(i * 8, i * 8 + 8)
        total = refs[0][rows, :]
        for ref in refs[1:8]:
            total = total + ref[rows, :]
        return total

    mass = rows_of(UNITS)
    mass = mass + pltpu.roll(mass, 128 - 32, 1)
    lane = lax.broadcasted_iota(jnp.int32, (8, 128), 1)
    for i in range(UNITS):
        unit = d * UNITS + i
        rotation = unit >> 5
        here = jnp.sum(jnp.where(lane == rotation, mass, 0.0), axis=1, keepdims=True)
        noise = sigma_ref[pl.ds(unit & 15, 1), :]
        out_ref[:, i * 128 : (i + 1) * 128] = rows_of(i) / (here + REG_WEIGHT * noise)


def cost(micros):
    return pl.CostEstimate(flops=int(micros * 1e9), bytes_accessed=0, transcendentals=0)


SMEM = pl.BlockSpec(memory_space=pltpu.SMEM)
VMEM = pl.BlockSpec(memory_space=pltpu.VMEM)


def ring(size, step):
    return [((i + step) % size, i) for i in range(size)]


X = ("x_lo", "x_hi")
X_SWAP = [(0, 3), (1, 2), (2, 1), (3, 0)]
CORE_SWAP = [(0, 1), (1, 0)]


def from_y(value, step):
    return lax.ppermute(value, "y", ring(4, step))


def to_x(value, flips):
    return lax.ppermute(value, X, [(i, i ^ (flips >> 1) ^ ((flips & 1) << 1)) for i in range(4)])


def to_y(value, step):
    return lax.ppermute(value, "y", ring(4, -step))


def to_z(value, step):
    return lax.ppermute(value, "z", ring(8, -step))


def local(particles, rot_center, shifts, references, class_prior, sigma2):
    x_lo, y, z = lax.axis_index("x_lo"), lax.axis_index("y"), lax.axis_index("z")
    x_hi, core = lax.axis_index("x_hi"), lax.axis_index("core")
    refs = jnp.transpose(references, (1, 0, 2)).reshape(ROWS, WIDE)

    zp = z & 1
    with jax.named_scope("swap"):
        raw = lax.ppermute(particles, "core", CORE_SWAP)
    with jax.named_scope("references"):
        quarter = lax.dynamic_slice_in_dim(refs, DIRECT + y * QUART, QUART, 1)
        half = lax.dynamic_slice_in_dim(refs, ZBASE + zp * QUART, QUART, 1)
        quarter, half, shifts, rot_center = lax.optimization_barrier((quarter, half, shifts, rot_center))
        crossed = lax.ppermute(quarter, X, X_SWAP)
    with jax.named_scope("swap"):
        meta = jnp.concatenate([shifts, rot_center[None]]).astype(F32)
        meta = jnp.pad(meta, ((0, 5), (0, PAD - NP)))
        meta_oth = lax.ppermute(meta, "core", CORE_SWAP)
    with jax.named_scope("references"):
        half, meta, meta_oth = lax.optimization_barrier((half, meta, meta_oth))
        z_crossed = lax.ppermute(half, X, X_SWAP)
        later_refs, meta = lax.optimization_barrier((refs, meta))
        direct, meta_oth = lax.optimization_barrier((later_refs[:, :DIRECT], meta_oth))
        direct = lax.ppermute(direct, X, X_SWAP)
    with jax.named_scope("shift"):
        own = shift_particles(particles, meta, 48)
        raw, crossed = lax.optimization_barrier((raw, crossed))
        oth = shift_particles(raw, meta_oth, 12)
    with jax.named_scope("references"):
        quarters = [from_y(crossed, s) for s in (1, 2, 3)]
        z_crossed, oth = lax.optimization_barrier((z_crossed, oth))
        z_other = lax.ppermute(z_crossed, "z", [(i, i ^ 1) for i in range(8)])
    inv = (1.0 / jnp.concatenate([sigma2, sigma2])).reshape(1, WIDE)
    log_prior = jnp.log(class_prior).reshape(2, 2, 8)
    own_bias = jnp.tile(log_prior[x_hi, core], ROTS).reshape(ROWS, 1)
    oth_bias = jnp.tile(log_prior[1 - x_hi, core], ROTS).reshape(ROWS, 1)

    raised = jax.ShapeDtypeStruct((LANES, ROWS, 128), F32)
    stats = jax.ShapeDtypeStruct((8, NP2), F32)
    with jax.named_scope("scores"):
        offsets = [DIRECT + ((y + s) & 3) * QUART for s in range(4)]
        z_offsets = [ZBASE + zp * QUART, ZBASE + (1 - zp) * QUART]
        energies = jax.ShapeDtypeStruct((ROWS, 128), F32)
        weighted, first, first_stats, begun, energy = pl.pallas_call(
            own_kernel,
            out_shape=[jax.ShapeDtypeStruct((NP2, WIDE), BF), raised, stats, raised, energies],
            in_specs=[SMEM] + [VMEM] * 9,
            out_specs=[VMEM] * 5,
            scratch_shapes=[pltpu.VMEM((LANES, ROWS, 128), F32)],
            cost_estimate=cost(7),
            compiler_params=pltpu.CompilerParams(vmem_limit_bytes=6 * MB),
        )(jnp.stack([offsets[0], z_offsets[0]]), own, oth, inv, own_bias, refs, meta, meta_oth, crossed, z_crossed)
        second, mine = pl.pallas_call(
            other_kernel,
            out_shape=[raised, stats],
            in_specs=[SMEM] + [VMEM] * 13,
            out_specs=[VMEM] * 2,
            scratch_shapes=[pltpu.VMEM((LANES, ROWS, 128), F32)],
            cost_estimate=cost(5),
            compiler_params=pltpu.CompilerParams(vmem_limit_bytes=6 * MB),
        )(
            jnp.stack(offsets[1:] + z_offsets[1:]), weighted, inv, oth_bias, meta, meta_oth, first_stats,
            begun, energy, direct, *quarters, z_other,
        )
        theirs = lax.ppermute(mine, "core", CORE_SWAP)

    with jax.named_scope("sums"):
        parts = pl.pallas_call(
            sums_kernel,
            out_shape=([jax.ShapeDtypeStruct((4, 8, PROWS, 128), F32)] + [jax.ShapeDtypeStruct((4, 8, PROWS, 128), BF)] * 3) * 2,
            in_specs=[SMEM] + [VMEM] * 6,
            out_specs=[VMEM] * 8,
            scratch_shapes=[
                pltpu.VMEM((ROTS * 16, NP2), BF),
                pltpu.VMEM((2, ROTS * WIDE // 128, 8, 128), F32),
                pltpu.VMEM((ROTS * 16, 128), F32),
                pltpu.VMEM((16, 128), F32),
            ],
            cost_estimate=cost(6),
            compiler_params=pltpu.CompilerParams(vmem_limit_bytes=14 * MB),
        )(jnp.stack([x_hi, x_lo, y, z]), first, second, mine, theirs, own, oth)

    order = (2, 3, 1)
    sends = (to_x, to_y)
    with jax.named_scope("reduce1"):
        arrived = [[parts[0]], [parts[4]]]
        for s in order:
            for n in range(2):
                arrived[n].append(sends[n](parts[4 * n + s], s))
        firsts = pl.pallas_call(
            first_sum_kernel,
            out_shape=([jax.ShapeDtypeStruct((8, PROWS, 128), F32)] + [jax.ShapeDtypeStruct((8, PROWS, 128), BF)] * 3) * 2,
            in_specs=[VMEM] * 8,
            out_specs=[VMEM] * 8,
            compiler_params=pltpu.CompilerParams(vmem_limit_bytes=4 * MB),
        )(*[piece for pair in zip(*arrived) for piece in pair])
    with jax.named_scope("reduce2"):
        pieces = [[firsts[0]], [firsts[4]]]
        for s in order:
            for n in range(2):
                pieces[n].append(sends[1 - n](firsts[4 * n + s], s))
        slots = pl.pallas_call(
            second_sum_kernel,
            out_shape=[jax.ShapeDtypeStruct((2 * PROWS, 128), F32)] * 8,
            in_specs=[VMEM] * 8,
            out_specs=[VMEM] * 8,
            compiler_params=pltpu.CompilerParams(vmem_limit_bytes=4 * MB),
        )(*[piece for pair in zip(*pieces) for piece in pair])
    with jax.named_scope("reduce3"):
        owned = [slots[0]] + [to_z(slots[s], s) for s in (4, 3, 5, 2, 6, 1, 7)]

    with jax.named_scope("means"):
        d = (x_lo * 4 + y) * 8 + z
        return pl.pallas_call(
            final_kernel,
            out_shape=jax.ShapeDtypeStruct((8, 1920), F32),
            in_specs=[SMEM] + [VMEM] * 9,
            out_specs=VMEM,
            compiler_params=pltpu.CompilerParams(vmem_limit_bytes=4 * MB),
        )(d.reshape(1), sigma2.reshape(16, 128), *owned)


def solution(mesh):
    fine = Mesh(mesh.devices.reshape(2, 4, 8, 2, 2), ("x_lo", "y", "z", "x_hi", "core"))
    dom, grp = ("x_lo", "y", "z"), ("x_hi", "core")
    return jax.shard_map(
        local,
        mesh=fine,
        in_specs=(P(dom + grp, None), P(dom + grp), P(None, dom + grp), P(grp, None, None), P(), P()),
        out_specs=P(grp, dom),
        check_vma=False,
    )
```

```python
import functools

import jax
import jax.numpy as jnp
from jax import lax
from jax.experimental import pallas as pl
from jax.experimental.pallas import tpu as pltpu
from jax.sharding import Mesh, PartitionSpec as P

HALFWIN = 6
BOX = 128
KXW = 32
KYW = 64
TWO_PI = 6.283185307179586
REG_WEIGHT = 0.05

F = 2048
WIDE = 2 * F
ROTS = 30
ROWS = ROTS * 8
NP = 448
PAD = 512
NP2 = 2 * PAD
LANES = NP2 // 128
DIRECT = 1024
QUART = 512
ZBASE = DIRECT + 4 * QUART
UNITS = 15
PART = 8
PROWS = PART * 8

BF = jnp.bfloat16
F32 = jnp.float32
MB = 1024 * 1024


def turn_cos_sin(turns):
    quarter = jnp.floor(4.0 * turns + 0.5)
    x = TWO_PI * (turns - 0.25 * quarter)
    q = quarter - 4.0 * jnp.floor(0.25 * quarter)
    x2 = x * x
    s = x * (1.0 + x2 * (-1.0 / 6 + x2 * (1.0 / 120 + x2 * (-1.0 / 5040 + x2 * (1.0 / 362880)))))
    c = 1.0 + x2 * (-0.5 + x2 * (1.0 / 24 + x2 * (-1.0 / 720 + x2 * (1.0 / 40320))))
    odd = (q == 1.0) | (q == 3.0)
    cos = jnp.where(odd, s, c)
    sin = jnp.where(odd, c, s)
    cos = jnp.where((q == 1.0) | (q == 2.0), -cos, cos)
    sin = jnp.where(q >= 2.0, -sin, sin)
    return cos, sin


SHIFT_ROWS = 64
SHIFT_STEPS = NP // SHIFT_ROWS


def shift_kernel(meta_ref, p_ref, o_ref, held_ref, turned_ref, sems):
    def copy(step):
        rows = pl.ds(step * SHIFT_ROWS, SHIFT_ROWS)
        return pltpu.make_async_copy(p_ref.at[rows, :], held_ref.at[rows, :], sems.at[step])

    for step in range(SHIFT_STEPS):
        copy(step).start()
    turned_ref[...] = jnp.transpose(meta_ref[...])
    lane = lax.broadcasted_iota(jnp.int32, (SHIFT_ROWS, 128), 1)
    kx = (lane & (KXW - 1)).astype(F32)
    ky = ((lane >> 5) - KYW // 2).astype(F32)
    for step in range(SHIFT_STEPS):
        rows = slice(step * SHIFT_ROWS, (step + 1) * SHIFT_ROWS)
        sx = turned_ref[rows, 0:1]
        sy = turned_ref[rows, 1:2]
        c, s = turn_cos_sin((sx * kx + sy * ky) * (1.0 / BOX))
        dc, ds = turn_cos_sin(jnp.broadcast_to(sy * (128 // KXW), (SHIFT_ROWS, 128)) * (1.0 / BOX))
        copy(step).wait()
        for b in range(F // 128):
            re = held_ref[rows, b * 128 : (b + 1) * 128].astype(F32)
            im = held_ref[rows, F + b * 128 : F + (b + 1) * 128].astype(F32)
            o_ref[rows, b * 128 : (b + 1) * 128] = (re * c + im * s).astype(BF)
            o_ref[rows, F + b * 128 : F + (b + 1) * 128] = (im * c - re * s).astype(BF)
            c, s = c * dc - s * ds, s * dc + c * ds


def shift_particles(particles, meta, megabytes):
    return pl.pallas_call(
        shift_kernel,
        out_shape=jax.ShapeDtypeStruct((NP, WIDE), BF),
        in_specs=[VMEM, pl.BlockSpec(memory_space=pl.ANY)],
        out_specs=VMEM,
        scratch_shapes=[
            pltpu.VMEM((NP, WIDE), BF),
            pltpu.VMEM((PAD, 8), F32),
            pltpu.SemaphoreType.DMA((SHIFT_STEPS,)),
        ],
        cost_estimate=cost(5),
        compiler_params=pltpu.CompilerParams(vmem_limit_bytes=megabytes * MB),
    )(meta, particles)


def weigh(own_ref, oth_ref, inv_ref, w_ref):
    width = 512
    for start in range(0, WIDE, width):
        cols = slice(start, start + width)
        inv = inv_ref[:, cols]
        w_ref[0:NP, cols] = (own_ref[:, cols].astype(F32) * inv).astype(BF)
        w_ref[PAD : PAD + NP, cols] = (oth_ref[:, cols].astype(F32) * inv).astype(BF)
        w_ref[NP:PAD, cols] = jnp.zeros((PAD - NP, width), BF)
        w_ref[PAD + NP :, cols] = jnp.zeros((PAD - NP, width), BF)


def correlate(w_ref, inv_ref, pieces, acc_ref, begun=None):
    energy = jnp.zeros((ROWS, 128), F32)
    for piece, base, width in pieces:
        for start in range(0, piece.shape[1], width):
            cols = pl.ds(base + start, width)
            inv = inv_ref[:, cols]
            part = lax.dot_general(
                piece[:, start : start + width],
                w_ref[:, cols],
                (((1,), (1,)), ((), ())),
                preferred_element_type=F32,
            )
            for j in range(LANES):
                block = part[:, j * 128 : (j + 1) * 128]
                acc_ref[j] = block if begun is None else begun[j] + block
            begun = acc_ref
            for lanes in range(0, width, 128):
                v = piece[:, start + lanes : start + lanes + 128].astype(F32)
                energy = energy + v * v * inv[:, lanes : lanes + 128]
    return energy


def offset(bias_ref, energy):
    return bias_ref[...] - 0.5 * jnp.sum(energy, axis=1, keepdims=True)


def exponentiate(acc_ref, bias, metas, out_ref, j):
    half = LANES // 2
    rot = metas[j // half][2:3, (j % half) * 128 : (j % half + 1) * 128]
    low = jnp.full((8, 128), -jnp.inf, F32)
    top = low
    for r in range(ROTS):
        rows = slice(r * 8, r * 8 + 8)
        score = jnp.where(inside_window(r, rot), acc_ref[j, rows, :] + bias[rows, :], low)
        out_ref[j, rows, :] = score
        top = jnp.maximum(top, score)
    top = jnp.max(top, axis=0, keepdims=True)
    mass = jnp.zeros((8, 128), F32)
    for r in range(ROTS):
        rows = slice(r * 8, r * 8 + 8)
        raised = jnp.exp(out_ref[j, rows, :] - top)
        out_ref[j, rows, :] = raised
        mass = mass + raised
    return top, jnp.sum(mass, axis=0, keepdims=True)


def inside_window(rotation, rot):
    return jnp.abs(jnp.abs(float(rotation) - rot) - ROTS / 2) >= ROTS / 2 - HALFWIN


def own_kernel(
    where_ref, own_ref, oth_ref, inv_ref, bias_ref, refs_ref, meta_a, meta_b, q0, z0,
    w_ref, e_ref, stats_ref, begun_ref, energy_ref, acc_ref,
):
    weigh(own_ref, oth_ref, inv_ref, w_ref)
    bias = offset(bias_ref, correlate(w_ref, inv_ref, [(refs_ref, 0, 512)], acc_ref))
    pieces = [(q, pl.multiple_of(where_ref[s], 128), QUART) for s, q in enumerate((q0, z0))]
    energy_ref[...] = correlate(w_ref, inv_ref, pieces, begun_ref)
    row = lax.broadcasted_iota(jnp.int32, (8, 128), 0)
    for j in range(LANES):
        top, mass = exponentiate(acc_ref, bias, (meta_a, meta_b), e_ref, j)
        stats_ref[:, j * 128 : (j + 1) * 128] = jnp.where(row == 0, top, mass)


def other_kernel(
    where_ref, w_ref, inv_ref, bias_ref, meta_a, meta_b, first_ref, begun_ref, energy_ref, d_ref, q1, q2, q3, z1,
    e_ref, stats_ref, acc_ref,
):
    pieces = [(d_ref, 0, 512)]
    for s, q in enumerate((q1, q2, q3, z1)):
        pieces.append((q, pl.multiple_of(where_ref[s], 128), QUART))
    bias = offset(bias_ref, energy_ref[...] + correlate(w_ref, inv_ref, pieces, acc_ref, begun_ref))
    row = lax.broadcasted_iota(jnp.int32, (8, 128), 0)
    for j in range(LANES):
        lanes = slice(j * 128, (j + 1) * 128)
        top_b, mass_b = exponentiate(acc_ref, bias, (meta_a, meta_b), e_ref, j)
        top_a, mass_a = first_ref[0:1, lanes], first_ref[1:2, lanes]
        top = jnp.maximum(top_a, top_b)
        mass = mass_a * jnp.exp(top_a - top) + mass_b * jnp.exp(top_b - top)
        tops = jnp.where(row == 2, top_a, top_b)
        stats_ref[:, lanes] = jnp.where(row == 0, top, jnp.where(row == 1, mass, tops))


def sums_kernel(where_ref, first_ref, second_ref, mine_ref, theirs_ref, own_ref, oth_ref, *refs):
    parts, (p_ref, acc_ref, mass_ref, extra_ref) = refs[:8], refs[8:]
    x_hi, x_lo, y, z = where_ref[0], where_ref[1], where_ref[2], where_ref[3]
    mass_ref[...] = jnp.zeros_like(mass_ref)
    for j in range(LANES):
        lanes = slice(j * 128, (j + 1) * 128)
        facing = (j + LANES // 2) % LANES
        crossed = slice(facing * 128, (facing + 1) * 128)
        top_a, mass_a = mine_ref[0:1, lanes], mine_ref[1:2, lanes]
        top_b, mass_b = theirs_ref[0:1, crossed], theirs_ref[1:2, crossed]
        top = jnp.maximum(top_a, top_b)
        scale = 1.0 / (mass_a * jnp.exp(top_a - top) + mass_b * jnp.exp(top_b - top))
        scale_a = jnp.exp(mine_ref[2:3, lanes] - top) * scale
        scale_b = jnp.exp(mine_ref[3:4, lanes] - top) * scale
        if j % (LANES // 2) == LANES // 2 - 1:
            used = lax.broadcasted_iota(jnp.int32, (1, 128), 1) < 128 - (PAD - NP)
            scale_a = jnp.where(used, scale_a, 0.0)
            scale_b = jnp.where(used, scale_b, 0.0)
        for r in range(ROTS):
            rows = slice(r * 8, r * 8 + 8)
            p = first_ref[j, rows, :] * scale_a
            q = second_ref[j, rows, :] * scale_b
            low = jnp.where(x_hi == 0, p, q)
            high = jnp.where(x_hi == 0, q, p)
            both = jnp.concatenate([low, high], axis=0)
            p_ref[r * 16 : (r + 1) * 16, lanes] = both.astype(BF)
            mass_ref[r * 16 : (r + 1) * 16, :] += both
    lane = lax.broadcasted_iota(jnp.int32, (16, 128), 1)
    totals = jnp.zeros((16, 128), F32)
    for r in range(ROTS):
        row_sum = jnp.sum(mass_ref[r * 16 : (r + 1) * 16, :], axis=1, keepdims=True)
        totals = jnp.where(lane == r, row_sum, totals)
    coarse = totals.astype(BF).astype(F32)
    extra_ref[...] = jnp.where(lane < 32, coarse, pltpu.roll(totals - coarse, 32, 1))
    width = 512
    for cb in range(WIDE // width):
        cols = slice(cb * width, (cb + 1) * width)
        part = jnp.dot(p_ref[:, 0:NP], own_ref[:, cols], preferred_element_type=F32) + jnp.dot(
            p_ref[:, PAD : PAD + NP], oth_ref[:, cols], preferred_element_type=F32
        )
        for j in range(width // 128):
            fb = cb * (width // 128) + j
            for r in range(ROTS):
                for kx in range(2):
                    row = r * 16 + kx * 8
                    acc_ref[kx, 32 * r + fb] = part[row : row + 8, j * 128 : (j + 1) * 128]

    def place(sz, carry):
        dest_z = (z + sz) & 7
        for sx in range(4):
            kx, dest_x = x_hi ^ (sx >> 1), x_lo ^ (sx & 1)
            for sy in range(4):
                base = ((dest_x * 4 + ((y + sy) & 3)) * 8 + dest_z) * UNITS

                def tile(i):
                    if i == UNITS:
                        return extra_ref[pl.ds(pl.multiple_of(kx * 8, 8), 8), :]
                    return acc_ref[kx, base + i]

                for i in range(0, UNITS + 1, 2):
                    both = jnp.concatenate([tile(i), tile(i + 1)], axis=0)
                    number = i // PART
                    hop, rest = (sx, sy) if number % 2 == 0 else (sy, sx)
                    row = (i % PART) * 8
                    part_ref = parts[number * 4 + hop]
                    part_ref[rest, sz, row : row + 16, :] = both.astype(part_ref.dtype)
        return carry

    lax.fori_loop(0, 8, place, 0)


def first_sum_kernel(*refs):
    for half in range(2):
        arrived = refs[half:8:2]
        for rest in range(4):
            for z in range(8):
                total = arrived[0][rest, z].astype(F32)
                for ref in arrived[1:]:
                    total = total + ref[rest, z].astype(F32)
                out_ref = refs[8 + 4 * half + rest]
                out_ref[z] = total.astype(out_ref.dtype)


def second_sum_kernel(*refs):
    for half in range(2):
        arrived = refs[half:8:2]
        for z in range(8):
            total = arrived[0][z]
            for ref in arrived[1:]:
                total = total + ref[z].astype(F32)
            refs[8 + z][half * PROWS : (half + 1) * PROWS, :] = total


def final_kernel(where_ref, sigma_ref, *refs):
    d = where_ref[0]
    out_ref = refs[8]

    def rows_of(i):
        rows = slice(i * 8, i * 8 + 8)
        total = refs[0][rows, :]
        for ref in refs[1:8]:
            total = total + ref[rows, :]
        return total

    mass = rows_of(UNITS)
    mass = mass + pltpu.roll(mass, 128 - 32, 1)
    lane = lax.broadcasted_iota(jnp.int32, (8, 128), 1)
    for i in range(UNITS):
        unit = d * UNITS + i
        rotation = unit >> 5
        here = jnp.sum(jnp.where(lane == rotation, mass, 0.0), axis=1, keepdims=True)
        noise = sigma_ref[pl.ds(unit & 15, 1), :]
        out_ref[:, i * 128 : (i + 1) * 128] = rows_of(i) / (here + REG_WEIGHT * noise)


def cost(micros):
    return pl.CostEstimate(flops=int(micros * 1e9), bytes_accessed=0, transcendentals=0)


SMEM = pl.BlockSpec(memory_space=pltpu.SMEM)
VMEM = pl.BlockSpec(memory_space=pltpu.VMEM)


def ring(size, step):
    return [((i + step) % size, i) for i in range(size)]


X = ("x_lo", "x_hi")
X_SWAP = [(0, 3), (1, 2), (2, 1), (3, 0)]
CORE_SWAP = [(0, 1), (1, 0)]


def from_y(value, step):
    return lax.ppermute(value, "y", ring(4, step))


def to_x(value, flips):
    return lax.ppermute(value, X, [(i, i ^ (flips >> 1) ^ ((flips & 1) << 1)) for i in range(4)])


def to_y(value, step):
    return lax.ppermute(value, "y", ring(4, -step))


def to_z(value, step):
    return lax.ppermute(value, "z", ring(8, -step))


def local(particles, rot_center, shifts, references, class_prior, sigma2):
    x_lo, y, z = lax.axis_index("x_lo"), lax.axis_index("y"), lax.axis_index("z")
    x_hi, core = lax.axis_index("x_hi"), lax.axis_index("core")
    refs = jnp.transpose(references, (1, 0, 2)).reshape(ROWS, WIDE)

    zp = z & 1
    with jax.named_scope("swap"):
        raw = lax.ppermute(particles, "core", CORE_SWAP)
    with jax.named_scope("references"):
        quarter = lax.dynamic_slice_in_dim(refs, DIRECT + y * QUART, QUART, 1)
        half = lax.dynamic_slice_in_dim(refs, ZBASE + zp * QUART, QUART, 1)
        quarter, half, shifts, rot_center = lax.optimization_barrier((quarter, half, shifts, rot_center))
        crossed = lax.ppermute(quarter, X, X_SWAP)
    with jax.named_scope("swap"):
        meta = jnp.concatenate([shifts, rot_center[None]]).astype(F32)
        meta = jnp.pad(meta, ((0, 5), (0, PAD - NP)))
        meta_oth = lax.ppermute(meta, "core", CORE_SWAP)
    with jax.named_scope("references"):
        half, meta, meta_oth = lax.optimization_barrier((half, meta, meta_oth))
        z_crossed = lax.ppermute(half, X, X_SWAP)
        later_refs, meta = lax.optimization_barrier((refs, meta))
        direct, meta_oth = lax.optimization_barrier((later_refs[:, :DIRECT], meta_oth))
        direct = lax.ppermute(direct, X, X_SWAP)
    with jax.named_scope("shift"):
        raw, crossed, meta = lax.optimization_barrier((raw, crossed, meta))
        own = shift_particles(particles, meta, 48)
        oth = shift_particles(raw, meta_oth, 12)
    with jax.named_scope("references"):
        quarters = [from_y(crossed, s) for s in (1, 2, 3)]
        z_crossed, oth = lax.optimization_barrier((z_crossed, oth))
        z_other = lax.ppermute(z_crossed, "z", [(i, i ^ 1) for i in range(8)])
    inv = (1.0 / jnp.concatenate([sigma2, sigma2])).reshape(1, WIDE)
    log_prior = jnp.log(class_prior).reshape(2, 2, 8)
    own_bias = jnp.tile(log_prior[x_hi, core], ROTS).reshape(ROWS, 1)
    oth_bias = jnp.tile(log_prior[1 - x_hi, core], ROTS).reshape(ROWS, 1)

    raised = jax.ShapeDtypeStruct((LANES, ROWS, 128), F32)
    stats = jax.ShapeDtypeStruct((8, NP2), F32)
    with jax.named_scope("scores"):
        offsets = [DIRECT + ((y + s) & 3) * QUART for s in range(4)]
        z_offsets = [ZBASE + zp * QUART, ZBASE + (1 - zp) * QUART]
        energies = jax.ShapeDtypeStruct((ROWS, 128), F32)
        weighted, first, first_stats, begun, energy = pl.pallas_call(
            own_kernel,
            out_shape=[jax.ShapeDtypeStruct((NP2, WIDE), BF), raised, stats, raised, energies],
            in_specs=[SMEM] + [VMEM] * 9,
            out_specs=[VMEM] * 5,
            scratch_shapes=[pltpu.VMEM((LANES, ROWS, 128), F32)],
            cost_estimate=cost(7),
            compiler_params=pltpu.CompilerParams(vmem_limit_bytes=6 * MB),
        )(jnp.stack([offsets[0], z_offsets[0]]), own, oth, inv, own_bias, refs, meta, meta_oth, crossed, z_crossed)
        second, mine = pl.pallas_call(
            other_kernel,
            out_shape=[raised, stats],
            in_specs=[SMEM] + [VMEM] * 13,
            out_specs=[VMEM] * 2,
            scratch_shapes=[pltpu.VMEM((LANES, ROWS, 128), F32)],
            cost_estimate=cost(5),
            compiler_params=pltpu.CompilerParams(vmem_limit_bytes=6 * MB),
        )(
            jnp.stack(offsets[1:] + z_offsets[1:]), weighted, inv, oth_bias, meta, meta_oth, first_stats,
            begun, energy, direct, *quarters, z_other,
        )
        theirs = lax.ppermute(mine, "core", CORE_SWAP)

    with jax.named_scope("sums"):
        parts = pl.pallas_call(
            sums_kernel,
            out_shape=([jax.ShapeDtypeStruct((4, 8, PROWS, 128), F32)] + [jax.ShapeDtypeStruct((4, 8, PROWS, 128), BF)] * 3) * 2,
            in_specs=[SMEM] + [VMEM] * 6,
            out_specs=[VMEM] * 8,
            scratch_shapes=[
                pltpu.VMEM((ROTS * 16, NP2), BF),
                pltpu.VMEM((2, ROTS * WIDE // 128, 8, 128), F32),
                pltpu.VMEM((ROTS * 16, 128), F32),
                pltpu.VMEM((16, 128), F32),
            ],
            cost_estimate=cost(6),
            compiler_params=pltpu.CompilerParams(vmem_limit_bytes=14 * MB),
        )(jnp.stack([x_hi, x_lo, y, z]), first, second, mine, theirs, own, oth)

    order = (2, 3, 1)
    sends = (to_x, to_y)
    with jax.named_scope("reduce1"):
        arrived = [[parts[0]], [parts[4]]]
        for s in order:
            for n in range(2):
                arrived[n].append(sends[n](parts[4 * n + s], s))
        firsts = pl.pallas_call(
            first_sum_kernel,
            out_shape=([jax.ShapeDtypeStruct((8, PROWS, 128), F32)] + [jax.ShapeDtypeStruct((8, PROWS, 128), BF)] * 3) * 2,
            in_specs=[VMEM] * 8,
            out_specs=[VMEM] * 8,
            compiler_params=pltpu.CompilerParams(vmem_limit_bytes=4 * MB),
        )(*[piece for pair in zip(*arrived) for piece in pair])
    with jax.named_scope("reduce2"):
        pieces = [[firsts[0]], [firsts[4]]]
        for s in order:
            for n in range(2):
                pieces[n].append(sends[1 - n](firsts[4 * n + s], s))
        slots = pl.pallas_call(
            second_sum_kernel,
            out_shape=[jax.ShapeDtypeStruct((2 * PROWS, 128), F32)] * 8,
            in_specs=[VMEM] * 8,
            out_specs=[VMEM] * 8,
            compiler_params=pltpu.CompilerParams(vmem_limit_bytes=4 * MB),
        )(*[piece for pair in zip(*pieces) for piece in pair])
    with jax.named_scope("reduce3"):
        owned = [slots[0]] + [to_z(slots[s], s) for s in (4, 3, 5, 2, 6, 1, 7)]

    with jax.named_scope("means"):
        d = (x_lo * 4 + y) * 8 + z
        return pl.pallas_call(
            final_kernel,
            out_shape=jax.ShapeDtypeStruct((8, 1920), F32),
            in_specs=[SMEM] + [VMEM] * 9,
            out_specs=VMEM,
            compiler_params=pltpu.CompilerParams(vmem_limit_bytes=4 * MB),
        )(d.reshape(1), sigma2.reshape(16, 128), *owned)


def solution(mesh):
    fine = Mesh(mesh.devices.reshape(2, 4, 8, 2, 2), ("x_lo", "y", "z", "x_hi", "core"))
    dom, grp = ("x_lo", "y", "z"), ("x_hi", "core")
    return jax.shard_map(
        local,
        mesh=fine,
        in_specs=(P(dom + grp, None), P(dom + grp), P(None, dom + grp), P(grp, None, None), P(), P()),
        out_specs=P(grp, dom),
        check_vma=False,
    )
```

```python
import functools

import jax
import jax.numpy as jnp
from jax import lax
from jax.experimental import pallas as pl
from jax.experimental.pallas import tpu as pltpu
from jax.sharding import Mesh, PartitionSpec as P

HALFWIN = 6
BOX = 128
KXW = 32
KYW = 64
TWO_PI = 6.283185307179586
REG_WEIGHT = 0.05

F = 2048
WIDE = 2 * F
ROTS = 30
ROWS = ROTS * 8
NP = 448
PAD = 512
NP2 = 2 * PAD
LANES = NP2 // 128
DIRECT = 1024
QUART = 512
ZBASE = DIRECT + 4 * QUART
UNITS = 15
PART = 8
PROWS = PART * 8

BF = jnp.bfloat16
F32 = jnp.float32
MB = 1024 * 1024


def turn_cos_sin(turns):
    quarter = jnp.floor(4.0 * turns + 0.5)
    x = TWO_PI * (turns - 0.25 * quarter)
    q = quarter - 4.0 * jnp.floor(0.25 * quarter)
    x2 = x * x
    s = x * (1.0 + x2 * (-1.0 / 6 + x2 * (1.0 / 120 + x2 * (-1.0 / 5040 + x2 * (1.0 / 362880)))))
    c = 1.0 + x2 * (-0.5 + x2 * (1.0 / 24 + x2 * (-1.0 / 720 + x2 * (1.0 / 40320))))
    odd = (q == 1.0) | (q == 3.0)
    cos = jnp.where(odd, s, c)
    sin = jnp.where(odd, c, s)
    cos = jnp.where((q == 1.0) | (q == 2.0), -cos, cos)
    sin = jnp.where(q >= 2.0, -sin, sin)
    return cos, sin


SHIFT_ROWS = 64
SHIFT_STEPS = NP // SHIFT_ROWS


def shift_kernel(meta_ref, p_ref, o_ref, held_ref, turned_ref, sems):
    def copy(step):
        rows = pl.ds(step * SHIFT_ROWS, SHIFT_ROWS)
        return pltpu.make_async_copy(p_ref.at[rows, :], held_ref.at[rows, :], sems.at[step])

    for step in range(SHIFT_STEPS):
        copy(step).start()
    turned_ref[...] = jnp.transpose(meta_ref[...])
    lane = lax.broadcasted_iota(jnp.int32, (SHIFT_ROWS, 128), 1)
    kx = (lane & (KXW - 1)).astype(F32)
    ky = ((lane >> 5) - KYW // 2).astype(F32)
    for step in range(SHIFT_STEPS):
        rows = slice(step * SHIFT_ROWS, (step + 1) * SHIFT_ROWS)
        sx = turned_ref[rows, 0:1]
        sy = turned_ref[rows, 1:2]
        c, s = turn_cos_sin((sx * kx + sy * ky) * (1.0 / BOX))
        dc, ds = turn_cos_sin(jnp.broadcast_to(sy * (128 // KXW), (SHIFT_ROWS, 128)) * (1.0 / BOX))
        copy(step).wait()
        for b in range(F // 128):
            re = held_ref[rows, b * 128 : (b + 1) * 128].astype(F32)
            im = held_ref[rows, F + b * 128 : F + (b + 1) * 128].astype(F32)
            o_ref[rows, b * 128 : (b + 1) * 128] = (re * c + im * s).astype(BF)
            o_ref[rows, F + b * 128 : F + (b + 1) * 128] = (im * c - re * s).astype(BF)
            c, s = c * dc - s * ds, s * dc + c * ds


def shift_particles(particles, meta, megabytes):
    return pl.pallas_call(
        shift_kernel,
        out_shape=jax.ShapeDtypeStruct((NP, WIDE), BF),
        in_specs=[VMEM, pl.BlockSpec(memory_space=pl.ANY)],
        out_specs=VMEM,
        scratch_shapes=[
            pltpu.VMEM((NP, WIDE), BF),
            pltpu.VMEM((PAD, 8), F32),
            pltpu.SemaphoreType.DMA((SHIFT_STEPS,)),
        ],
        cost_estimate=cost(5),
        compiler_params=pltpu.CompilerParams(vmem_limit_bytes=megabytes * MB),
    )(meta, particles)


def weigh(own_ref, oth_ref, inv_ref, w_ref):
    width = 512
    for start in range(0, WIDE, width):
        cols = slice(start, start + width)
        inv = inv_ref[:, cols]
        w_ref[0:NP, cols] = (own_ref[:, cols].astype(F32) * inv).astype(BF)
        w_ref[PAD : PAD + NP, cols] = (oth_ref[:, cols].astype(F32) * inv).astype(BF)
        w_ref[NP:PAD, cols] = jnp.zeros((PAD - NP, width), BF)
        w_ref[PAD + NP :, cols] = jnp.zeros((PAD - NP, width), BF)


def correlate(w_ref, inv_ref, pieces, acc_ref, begun=None):
    energy = jnp.zeros((ROWS, 128), F32)
    for piece, base, width in pieces:
        for start in range(0, piece.shape[1], width):
            cols = pl.ds(base + start, width)
            inv = inv_ref[:, cols]
            part = lax.dot_general(
                piece[:, start : start + width],
                w_ref[:, cols],
                (((1,), (1,)), ((), ())),
                preferred_element_type=F32,
            )
            for j in range(LANES):
                block = part[:, j * 128 : (j + 1) * 128]
                acc_ref[j] = block if begun is None else begun[j] + block
            begun = acc_ref
            for lanes in range(0, width, 128):
                v = piece[:, start + lanes : start + lanes + 128].astype(F32)
                energy = energy + v * v * inv[:, lanes : lanes + 128]
    return energy


def offset(bias_ref, energy):
    return bias_ref[...] - 0.5 * jnp.sum(energy, axis=1, keepdims=True)


def exponentiate(acc_ref, bias, metas, out_ref, j):
    half = LANES // 2
    rot = metas[j // half][2:3, (j % half) * 128 : (j % half + 1) * 128]
    low = jnp.full((8, 128), -jnp.inf, F32)
    top = low
    for r in range(ROTS):
        rows = slice(r * 8, r * 8 + 8)
        score = jnp.where(inside_window(r, rot), acc_ref[j, rows, :] + bias[rows, :], low)
        out_ref[j, rows, :] = score
        top = jnp.maximum(top, score)
    top = jnp.max(top, axis=0, keepdims=True)
    mass = jnp.zeros((8, 128), F32)
    for r in range(ROTS):
        rows = slice(r * 8, r * 8 + 8)
        raised = jnp.exp(out_ref[j, rows, :] - top)
        out_ref[j, rows, :] = raised
        mass = mass + raised
    return top, jnp.sum(mass, axis=0, keepdims=True)


def inside_window(rotation, rot):
    return jnp.abs(jnp.abs(float(rotation) - rot) - ROTS / 2) >= ROTS / 2 - HALFWIN


def own_kernel(
    where_ref, own_ref, oth_ref, inv_ref, bias_ref, refs_ref, meta_a, meta_b, q0, z0,
    w_ref, e_ref, stats_ref, begun_ref, energy_ref, acc_ref,
):
    weigh(own_ref, oth_ref, inv_ref, w_ref)
    bias = offset(bias_ref, correlate(w_ref, inv_ref, [(refs_ref, 0, 512)], acc_ref))
    pieces = [(q, pl.multiple_of(where_ref[s], 128), QUART) for s, q in enumerate((q0, z0))]
    energy_ref[...] = correlate(w_ref, inv_ref, pieces, begun_ref)
    row = lax.broadcasted_iota(jnp.int32, (8, 128), 0)
    for j in range(LANES):
        top, mass = exponentiate(acc_ref, bias, (meta_a, meta_b), e_ref, j)
        stats_ref[:, j * 128 : (j + 1) * 128] = jnp.where(row == 0, top, mass)


def other_kernel(
    where_ref, w_ref, inv_ref, bias_ref, meta_a, meta_b, first_ref, begun_ref, energy_ref, d_ref, q1, q2, q3, z1,
    e_ref, stats_ref, acc_ref,
):
    pieces = [(d_ref, 0, 512)]
    for s, q in enumerate((q1, q2, q3, z1)):
        pieces.append((q, pl.multiple_of(where_ref[s], 128), QUART))
    bias = offset(bias_ref, energy_ref[...] + correlate(w_ref, inv_ref, pieces, acc_ref, begun_ref))
    row = lax.broadcasted_iota(jnp.int32, (8, 128), 0)
    for j in range(LANES):
        lanes = slice(j * 128, (j + 1) * 128)
        top_b, mass_b = exponentiate(acc_ref, bias, (meta_a, meta_b), e_ref, j)
        top_a, mass_a = first_ref[0:1, lanes], first_ref[1:2, lanes]
        top = jnp.maximum(top_a, top_b)
        mass = mass_a * jnp.exp(top_a - top) + mass_b * jnp.exp(top_b - top)
        tops = jnp.where(row == 2, top_a, top_b)
        stats_ref[:, lanes] = jnp.where(row == 0, top, jnp.where(row == 1, mass, tops))


def sums_kernel(where_ref, first_ref, second_ref, mine_ref, theirs_ref, own_ref, oth_ref, *refs):
    parts, (p_ref, acc_ref, mass_ref, extra_ref) = refs[:8], refs[8:]
    x_hi, x_lo, y, z = where_ref[0], where_ref[1], where_ref[2], where_ref[3]
    mass_ref[...] = jnp.zeros_like(mass_ref)
    for j in range(LANES):
        lanes = slice(j * 128, (j + 1) * 128)
        facing = (j + LANES // 2) % LANES
        crossed = slice(facing * 128, (facing + 1) * 128)
        top_a, mass_a = mine_ref[0:1, lanes], mine_ref[1:2, lanes]
        top_b, mass_b = theirs_ref[0:1, crossed], theirs_ref[1:2, crossed]
        top = jnp.maximum(top_a, top_b)
        scale = 1.0 / (mass_a * jnp.exp(top_a - top) + mass_b * jnp.exp(top_b - top))
        scale_a = jnp.exp(mine_ref[2:3, lanes] - top) * scale
        scale_b = jnp.exp(mine_ref[3:4, lanes] - top) * scale
        if j % (LANES // 2) == LANES // 2 - 1:
            used = lax.broadcasted_iota(jnp.int32, (1, 128), 1) < 128 - (PAD - NP)
            scale_a = jnp.where(used, scale_a, 0.0)
            scale_b = jnp.where(used, scale_b, 0.0)
        for r in range(ROTS):
            rows = slice(r * 8, r * 8 + 8)
            p = first_ref[j, rows, :] * scale_a
            q = second_ref[j, rows, :] * scale_b
            low = jnp.where(x_hi == 0, p, q)
            high = jnp.where(x_hi == 0, q, p)
            both = jnp.concatenate([low, high], axis=0)
            p_ref[r * 16 : (r + 1) * 16, lanes] = both.astype(BF)
            mass_ref[r * 16 : (r + 1) * 16, :] += both
    lane = lax.broadcasted_iota(jnp.int32, (16, 128), 1)
    totals = jnp.zeros((16, 128), F32)
    for r in range(ROTS):
        row_sum = jnp.sum(mass_ref[r * 16 : (r + 1) * 16, :], axis=1, keepdims=True)
        totals = jnp.where(lane == r, row_sum, totals)
    coarse = totals.astype(BF).astype(F32)
    extra_ref[...] = jnp.where(lane < 32, coarse, pltpu.roll(totals - coarse, 32, 1))
    width = 512
    for cb in range(WIDE // width):
        cols = slice(cb * width, (cb + 1) * width)
        part = jnp.dot(p_ref[:, 0:NP], own_ref[:, cols], preferred_element_type=F32) + jnp.dot(
            p_ref[:, PAD : PAD + NP], oth_ref[:, cols], preferred_element_type=F32
        )
        for j in range(width // 128):
            fb = cb * (width // 128) + j
            for r in range(ROTS):
                for kx in range(2):
                    row = r * 16 + kx * 8
                    acc_ref[kx, 32 * r + fb] = part[row : row + 8, j * 128 : (j + 1) * 128]

    def place(sz, carry):
        dest_z = (z + sz) & 7
        for sx in range(4):
            kx, dest_x = x_hi ^ (sx >> 1), x_lo ^ (sx & 1)
            for sy in range(4):
                base = ((dest_x * 4 + ((y + sy) & 3)) * 8 + dest_z) * UNITS

                def tile(i):
                    if i == UNITS:
                        return extra_ref[pl.ds(pl.multiple_of(kx * 8, 8), 8), :]
                    return acc_ref[kx, base + i]

                for i in range(0, UNITS + 1, 2):
                    both = jnp.concatenate([tile(i), tile(i + 1)], axis=0)
                    number = i // PART
                    hop, rest = (sx, sy) if number % 2 == 0 else (sy, sx)
                    row = (i % PART) * 8
                    part_ref = parts[number * 4 + hop]
                    part_ref[rest, sz, row : row + 16, :] = both.astype(part_ref.dtype)
        return carry

    lax.fori_loop(0, 8, place, 0)


def first_sum_kernel(*refs):
    for half in range(2):
        arrived = refs[half:8:2]
        for rest in range(4):
            for z in range(8):
                total = arrived[0][rest, z].astype(F32)
                for ref in arrived[1:]:
                    total = total + ref[rest, z].astype(F32)
                out_ref = refs[8 + 4 * half + rest]
                out_ref[z] = total.astype(out_ref.dtype)


def second_sum_kernel(*refs):
    for half in range(2):
        arrived = refs[half:8:2]
        for z in range(8):
            total = arrived[0][z]
            for ref in arrived[1:]:
                total = total + ref[z].astype(F32)
            refs[8 + z][half * PROWS : (half + 1) * PROWS, :] = total


def final_kernel(where_ref, sigma_ref, *refs):
    d = where_ref[0]
    out_ref = refs[8]

    def rows_of(i):
        rows = slice(i * 8, i * 8 + 8)
        total = refs[0][rows, :]
        for ref in refs[1:8]:
            total = total + ref[rows, :]
        return total

    mass = rows_of(UNITS)
    mass = mass + pltpu.roll(mass, 128 - 32, 1)
    lane = lax.broadcasted_iota(jnp.int32, (8, 128), 1)
    for i in range(UNITS):
        unit = d * UNITS + i
        rotation = unit >> 5
        here = jnp.sum(jnp.where(lane == rotation, mass, 0.0), axis=1, keepdims=True)
        noise = sigma_ref[pl.ds(unit & 15, 1), :]
        out_ref[:, i * 128 : (i + 1) * 128] = rows_of(i) / (here + REG_WEIGHT * noise)


def cost(micros):
    return pl.CostEstimate(flops=int(micros * 1e9), bytes_accessed=0, transcendentals=0)


SMEM = pl.BlockSpec(memory_space=pltpu.SMEM)
VMEM = pl.BlockSpec(memory_space=pltpu.VMEM)


def ring(size, step):
    return [((i + step) % size, i) for i in range(size)]


X = ("x_lo", "x_hi")
X_SWAP = [(0, 3), (1, 2), (2, 1), (3, 0)]
CORE_SWAP = [(0, 1), (1, 0)]


def from_y(value, step):
    return lax.ppermute(value, "y", ring(4, step))


def to_x(value, flips):
    return lax.ppermute(value, X, [(i, i ^ (flips >> 1) ^ ((flips & 1) << 1)) for i in range(4)])


def to_y(value, step):
    return lax.ppermute(value, "y", ring(4, -step))


def to_z(value, step):
    return lax.ppermute(value, "z", ring(8, -step))


def local(particles, rot_center, shifts, references, class_prior, sigma2):
    x_lo, y, z = lax.axis_index("x_lo"), lax.axis_index("y"), lax.axis_index("z")
    x_hi, core = lax.axis_index("x_hi"), lax.axis_index("core")
    refs = jnp.transpose(references, (1, 0, 2)).reshape(ROWS, WIDE)

    zp = z & 1
    with jax.named_scope("swap"):
        raw = lax.ppermute(particles, "core", CORE_SWAP)
    with jax.named_scope("references"):
        quarter = lax.dynamic_slice_in_dim(refs, DIRECT + y * QUART, QUART, 1)
        half = lax.dynamic_slice_in_dim(refs, ZBASE + zp * QUART, QUART, 1)
        quarter, half, shifts, rot_center = lax.optimization_barrier((quarter, half, shifts, rot_center))
        crossed = lax.ppermute(quarter, X, X_SWAP)
    with jax.named_scope("swap"):
        meta = jnp.concatenate([shifts, rot_center[None]]).astype(F32)
        meta = jnp.pad(meta, ((0, 5), (0, PAD - NP)))
        meta_oth = lax.ppermute(meta, "core", CORE_SWAP)
    with jax.named_scope("references"):
        half, meta, meta_oth = lax.optimization_barrier((half, meta, meta_oth))
        z_crossed = lax.ppermute(half, X, X_SWAP)
        later_refs, meta = lax.optimization_barrier((refs, meta))
        direct, meta_oth = lax.optimization_barrier((later_refs[:, :DIRECT], meta_oth))
        direct = lax.ppermute(direct, X, X_SWAP)
    with jax.named_scope("shift"):
        raw, crossed, meta = lax.optimization_barrier((raw, crossed, meta))
        own = shift_particles(particles, meta, 48)
        oth = shift_particles(raw, meta_oth, 12)
    with jax.named_scope("references"):
        quarters = [from_y(crossed, s) for s in (1, 2, 3)]
        z_crossed, own = lax.optimization_barrier((z_crossed, own))
        z_other = lax.ppermute(z_crossed, "z", [(i, i ^ 1) for i in range(8)])
    inv = (1.0 / jnp.concatenate([sigma2, sigma2])).reshape(1, WIDE)
    log_prior = jnp.log(class_prior).reshape(2, 2, 8)
    own_bias = jnp.tile(log_prior[x_hi, core], ROTS).reshape(ROWS, 1)
    oth_bias = jnp.tile(log_prior[1 - x_hi, core], ROTS).reshape(ROWS, 1)

    raised = jax.ShapeDtypeStruct((LANES, ROWS, 128), F32)
    stats = jax.ShapeDtypeStruct((8, NP2), F32)
    with jax.named_scope("scores"):
        offsets = [DIRECT + ((y + s) & 3) * QUART for s in range(4)]
        z_offsets = [ZBASE + zp * QUART, ZBASE + (1 - zp) * QUART]
        energies = jax.ShapeDtypeStruct((ROWS, 128), F32)
        weighted, first, first_stats, begun, energy = pl.pallas_call(
            own_kernel,
            out_shape=[jax.ShapeDtypeStruct((NP2, WIDE), BF), raised, stats, raised, energies],
            in_specs=[SMEM] + [VMEM] * 9,
            out_specs=[VMEM] * 5,
            scratch_shapes=[pltpu.VMEM((LANES, ROWS, 128), F32)],
            cost_estimate=cost(7),
            compiler_params=pltpu.CompilerParams(vmem_limit_bytes=6 * MB),
        )(jnp.stack([offsets[0], z_offsets[0]]), own, oth, inv, own_bias, refs, meta, meta_oth, crossed, z_crossed)
        second, mine = pl.pallas_call(
            other_kernel,
            out_shape=[raised, stats],
            in_specs=[SMEM] + [VMEM] * 13,
            out_specs=[VMEM] * 2,
            scratch_shapes=[pltpu.VMEM((LANES, ROWS, 128), F32)],
            cost_estimate=cost(5),
            compiler_params=pltpu.CompilerParams(vmem_limit_bytes=6 * MB),
        )(
            jnp.stack(offsets[1:] + z_offsets[1:]), weighted, inv, oth_bias, meta, meta_oth, first_stats,
            begun, energy, direct, *quarters, z_other,
        )
        theirs = lax.ppermute(mine, "core", CORE_SWAP)

    with jax.named_scope("sums"):
        parts = pl.pallas_call(
            sums_kernel,
            out_shape=([jax.ShapeDtypeStruct((4, 8, PROWS, 128), F32)] + [jax.ShapeDtypeStruct((4, 8, PROWS, 128), BF)] * 3) * 2,
            in_specs=[SMEM] + [VMEM] * 6,
            out_specs=[VMEM] * 8,
            scratch_shapes=[
                pltpu.VMEM((ROTS * 16, NP2), BF),
                pltpu.VMEM((2, ROTS * WIDE // 128, 8, 128), F32),
                pltpu.VMEM((ROTS * 16, 128), F32),
                pltpu.VMEM((16, 128), F32),
            ],
            cost_estimate=cost(6),
            compiler_params=pltpu.CompilerParams(vmem_limit_bytes=14 * MB),
        )(jnp.stack([x_hi, x_lo, y, z]), first, second, mine, theirs, own, oth)

    order = (2, 3, 1)
    sends = (to_x, to_y)
    with jax.named_scope("reduce1"):
        arrived = [[parts[0]], [parts[4]]]
        for s in order:
            for n in range(2):
                arrived[n].append(sends[n](parts[4 * n + s], s))
        firsts = pl.pallas_call(
            first_sum_kernel,
            out_shape=([jax.ShapeDtypeStruct((8, PROWS, 128), F32)] + [jax.ShapeDtypeStruct((8, PROWS, 128), BF)] * 3) * 2,
            in_specs=[VMEM] * 8,
            out_specs=[VMEM] * 8,
            compiler_params=pltpu.CompilerParams(vmem_limit_bytes=4 * MB),
        )(*[piece for pair in zip(*arrived) for piece in pair])
    with jax.named_scope("reduce2"):
        pieces = [[firsts[0]], [firsts[4]]]
        for s in order:
            for n in range(2):
                pieces[n].append(sends[1 - n](firsts[4 * n + s], s))
        slots = pl.pallas_call(
            second_sum_kernel,
            out_shape=[jax.ShapeDtypeStruct((2 * PROWS, 128), F32)] * 8,
            in_specs=[VMEM] * 8,
            out_specs=[VMEM] * 8,
            compiler_params=pltpu.CompilerParams(vmem_limit_bytes=4 * MB),
        )(*[piece for pair in zip(*pieces) for piece in pair])
    with jax.named_scope("reduce3"):
        owned = [slots[0]] + [to_z(slots[s], s) for s in (1, 7, 2, 6, 3, 5, 4)]

    with jax.named_scope("means"):
        d = (x_lo * 4 + y) * 8 + z
        return pl.pallas_call(
            final_kernel,
            out_shape=jax.ShapeDtypeStruct((8, 1920), F32),
            in_specs=[SMEM] + [VMEM] * 9,
            out_specs=VMEM,
            compiler_params=pltpu.CompilerParams(vmem_limit_bytes=4 * MB),
        )(d.reshape(1), sigma2.reshape(16, 128), *owned)


def solution(mesh):
    fine = Mesh(mesh.devices.reshape(2, 4, 8, 2, 2), ("x_lo", "y", "z", "x_hi", "core"))
    dom, grp = ("x_lo", "y", "z"), ("x_hi", "core")
    return jax.shard_map(
        local,
        mesh=fine,
        in_specs=(P(dom + grp, None), P(dom + grp), P(None, dom + grp), P(grp, None, None), P(), P()),
        out_specs=P(grp, dom),
        check_vma=False,
    )
```
